512 devices in a mesh: seq: 64 (over y, x, core), head: 8 (over z).
Axes of the slice: x: 4, y: 8, z: 8, core: 2. Of those that a mesh axis runs over, the one named last changes fastest.
Arguments:
- queries: bfloat16 [8192, 4096], P('seq', 'head'), may hold values from -300 to 300
- keyvals: bfloat16 [8192, 8, 128], P('seq', 'head'), may hold values from -6 to 6
- out_proj: bfloat16 [4096, 2880], P('head'), may hold values from -0.09375 to 0.09375
- residual: bfloat16 [8192, 2880], P(('seq', 'head')), may hold values from -60 to 60
- norm_gain: float32 [2880], replicated, may hold values from 0.1 to 1.9
- route_ids: int32 [8192, 4], P('seq'), may hold values from 0 to 31, as said below
- route_weights: bfloat16 [8192, 4], P('seq'), may hold values from 0.049804688 to 0.5
- expert_in: bfloat16 [64, 1440, 3072], P('seq', None, 'head'), may hold values from -0.109375 to 0.109375
- expert_out: bfloat16 [64, 1536, 1440], P('seq', 'head'), may hold values from -0.15625 to 0.15625
Outputs:
- stream: bfloat16 [8192, 2880], P(('seq', 'head'))
- expert_sum: bfloat16 [8192, 2880], P(('seq', 'head'))
The draws below stay inside these ranges and needn't reach their ends.
Inputs may be any that keep to these rules, and one draw needn't show every extreme that they name: `route_ids`: each row names 4 different experts. In each aligned block of 16 rows, one expert, the same in every block, is named by exactly 3 rows, and every other expert by at most 3 rows; the other experts' counts within a block differ by at most one.
All inputs are finite; a program needn't handle non-finite values.
Results may differ from the reference program's by a relative error of at most 0.035.
Values may be sent and summed in bfloat16 or wider, within the bound.
A program may use at most 64 MiB of HBM per device.

```python
import jax
import jax.numpy as jnp
from jax import lax

D = 2880
QUERY_HEADS = 64
KEY_VALUE_HEADS = 8
HEAD_SIZE = 64
HID = 1536
TOP = 4
ATTEND_SPAN = 128
WINDOW_TOKENS = 8192
EXPERTS = 32
HALF = 1440
HID_DEV = 192
ROWS = 16
CAP = 3
N_HEAD = 8


def base_keys(key):
    return jnp.clip(jax.random.normal(jax.random.fold_in(key, 101), (WINDOW_TOKENS, KEY_VALUE_HEADS, HEAD_SIZE), jnp.float32), -6.0, 6.0)


def draw_queries(key, part):
    key = jax.random.fold_in(key, 1)
    value_rows = jnp.clip(jax.random.normal(key, (WINDOW_TOKENS, QUERY_HEADS, HEAD_SIZE), jnp.float32), -6.0, 6.0)
    return value_rows.reshape(WINDOW_TOKENS, QUERY_HEADS * HEAD_SIZE).astype(jnp.bfloat16)


def draw_keyvals(key, part):
    common_expert = base_keys(key)
    key = jax.random.fold_in(key, 2)
    value_rows = jnp.clip(jax.random.normal(key, (WINDOW_TOKENS, KEY_VALUE_HEADS, HEAD_SIZE), jnp.float32), -6.0, 6.0)
    return jnp.concatenate([common_expert, value_rows], axis=-1).astype(jnp.bfloat16)


def draw_residual(key, part):
    key = jax.random.fold_in(key, 3)
    key_base = jax.random.fold_in(key, 0)
    value_rows = jnp.clip(jax.random.normal(key_base, (WINDOW_TOKENS, D), jnp.float32), -6.0, 6.0)
    return value_rows.astype(jnp.bfloat16)


def draw_route_ids(key, part):
    key = jax.random.fold_in(key, 4)
    key_hot, key_perm, key_rows, key_roll = jax.random.split(key, 4)
    tile_block_count = WINDOW_TOKENS // ROWS
    hot_expert = jax.random.randint(key_hot, (), 0, EXPERTS, jnp.int32)

    def permute_others(subkey):
        return jax.random.permutation(subkey, EXPERTS - 1)
    others = (hot_expert + 1 + jax.vmap(permute_others)(jax.random.split(key_perm, tile_block_count))) % EXPERTS
    item = jnp.arange(ROWS * TOP, dtype=jnp.int32)
    row_of = item // TOP
    column_of = item % TOP
    is_hot = (column_of == 0) & (row_of < CAP)
    before = jnp.minimum(CAP, (item + TOP - 1) // TOP)
    order = (item - before) % (EXPERTS - 1)
    chosen = jnp.where(is_hot[None, :], hot_expert, others[:, order]).reshape(tile_block_count, ROWS, TOP)

    def permute_rows(subkey):
        return jax.random.permutation(subkey, ROWS)
    row_order = jax.vmap(permute_rows)(jax.random.split(key_rows, tile_block_count))
    chosen = jnp.take_along_axis(chosen, row_order[:, :, None], axis=1)
    shifts = jax.random.randint(key_roll, (tile_block_count, ROWS, 1), 0, TOP, jnp.int32)
    column_order = (jnp.arange(TOP, dtype=jnp.int32)[None, None, :] + shifts) % TOP
    chosen = jnp.take_along_axis(chosen, column_order, axis=2)
    return chosen.reshape(WINDOW_TOKENS, TOP).astype(jnp.int32)


def level_of(stream_key, extent, shards, least, high):
    loudness = 1.0
    for position, parts in shards:
        heights = jax.random.uniform(jax.random.fold_in(jax.random.fold_in(stream_key, 6), position), (parts,), jnp.float32, least / len(shards), high / len(shards))
        loudness = loudness * jnp.repeat(jnp.exp(heights), extent[position] // parts).reshape((-1,) + (1,) * (len(extent) - 1 - position))
    return loudness


def noise(own_key, shape, deviation, reach, shards=(), kind=jnp.bfloat16):
    entries = jax.random.normal(own_key, shape, jnp.float32) * deviation
    if len(shards) > 0:
        entries = level_of(own_key, shape, shards, -0.22, 0.18) * entries
    return jnp.clip(entries, min=-reach, max=reach).astype(kind)


def setup_inputs(seed: int = 0) -> dict:
    keys = jax.random.split(jax.random.key(seed), 10)
    return {
        "queries": draw_queries(jax.random.fold_in(keys[9], 71), 0),
        "keyvals": draw_keyvals(jax.random.fold_in(keys[9], 71), 0),
        "out_proj": noise(keys[2], (QUERY_HEADS * HEAD_SIZE, D), (QUERY_HEADS * HEAD_SIZE) ** -0.5, 0.09375, ((0, 8),)),
        "residual": draw_residual(jax.random.fold_in(keys[9], 71), 0),
        "norm_gain": jnp.clip(1.0 + 0.18 * jax.random.normal(keys[4], (D,), jnp.float32), 0.1, 1.9),
        "route_ids": draw_route_ids(jax.random.fold_in(keys[9], 71), 0),
        "route_weights": jnp.clip(0.049804688 + 0.4501953 * jax.random.uniform(keys[6], (WINDOW_TOKENS, TOP), jnp.float32) ** level_of(keys[6], (WINDOW_TOKENS, TOP), ((0, 64),), -0.2, 0.2), 0.049804688, 0.5).astype(jnp.bfloat16),
        "expert_in": noise(keys[7], (2 * EXPERTS, HALF, 2 * HID), D ** -0.5, 0.109375, ((0, 64), (2, 8))),
        "expert_out": noise(keys[8], (2 * EXPERTS, HID, HALF), HID ** -0.5, 0.15625, ((0, 64), (1, 8))),
    }


def normalize(hidden, norm_gain):
    mean_square = lax.optimization_barrier(jnp.mean(hidden * hidden, axis=-1, keepdims=True))
    return (hidden * lax.rsqrt(mean_square + 1e-05) * norm_gain).astype(jnp.bfloat16)

def attend(queries, keyvals):
    tile_block_count = WINDOW_TOKENS // ATTEND_SPAN
    query_group = QUERY_HEADS // KEY_VALUE_HEADS
    key_value_pairs = keyvals.astype(jnp.float32)
    preceding_rows = jnp.concatenate([jnp.zeros((ATTEND_SPAN, KEY_VALUE_HEADS, 2 * HEAD_SIZE), jnp.float32), key_value_pairs[:WINDOW_TOKENS - ATTEND_SPAN]], axis=0)
    key_tiles_list = jnp.concatenate([preceding_rows.reshape(tile_block_count, ATTEND_SPAN, KEY_VALUE_HEADS, 2 * HEAD_SIZE), key_value_pairs.reshape(tile_block_count, ATTEND_SPAN, KEY_VALUE_HEADS, 2 * HEAD_SIZE)], axis=1)
    query_tiles_list = queries.astype(jnp.float32).reshape(tile_block_count, ATTEND_SPAN, KEY_VALUE_HEADS, query_group, HEAD_SIZE)
    scores = jnp.einsum('bqkgd,bjkd->bkgqj', query_tiles_list, key_tiles_list[..., :HEAD_SIZE]) * HEAD_SIZE ** (-0.5)
    query_pos = jnp.arange(ATTEND_SPAN, dtype=jnp.int32)[:, None]
    key_pos = jnp.arange(2 * ATTEND_SPAN, dtype=jnp.int32)[None, :]
    first_key = jnp.arange(tile_block_count, dtype=jnp.int32) * ATTEND_SPAN - ATTEND_SPAN
    allowed = (key_pos > query_pos) & (key_pos <= query_pos + ATTEND_SPAN) & (first_key[:, None, None] + key_pos[None] >= 0)
    scores = jnp.where(allowed[:, None, None], scores, -1e+30)
    largest = lax.optimization_barrier(jnp.max(scores, axis=-1, keepdims=True))
    exponent = jnp.exp(scores - largest)
    attention_weights = (exponent / lax.optimization_barrier(jnp.sum(exponent, axis=-1, keepdims=True))).astype(jnp.bfloat16)
    mixed_vals = jnp.einsum('bkgqj,bjkd->bqkgd', attention_weights.astype(jnp.float32), key_tiles_list[..., HEAD_SIZE:])
    return mixed_vals.astype(jnp.bfloat16).reshape(WINDOW_TOKENS, QUERY_HEADS * HEAD_SIZE)

def reference(queries, keyvals, out_proj, residual, norm_gain, route_ids, route_weights, expert_in, expert_out):
    attended = attend(queries, keyvals)
    hidden = residual.astype(jnp.float32) + jnp.dot(attended, out_proj, preferred_element_type=jnp.float32)
    stream = hidden.astype(jnp.bfloat16)
    normed = normalize(hidden, norm_gain)
    tile_block_count = WINDOW_TOKENS // ROWS
    block_ids = route_ids.reshape(tile_block_count, ROWS * TOP)
    one_hot = (block_ids[..., None] == jnp.arange(EXPERTS, dtype=jnp.int32)).astype(jnp.int32)
    earlier = lax.optimization_barrier(jnp.sum((jnp.cumsum(one_hot, axis=1) - one_hot) * one_hot, axis=-1))
    per_expert = tile_block_count * CAP
    slot_flat = (jnp.arange(tile_block_count, dtype=jnp.int32)[:, None] * CAP + earlier).reshape(-1)
    target = route_ids.reshape(-1) * per_expert + slot_flat
    token_of = jnp.arange(WINDOW_TOKENS * TOP, dtype=jnp.int32) // TOP
    pick_rows = jnp.full((EXPERTS * per_expert,), WINDOW_TOKENS, jnp.int32).at[target].set(token_of)
    pick_weights = jnp.zeros((EXPERTS * per_expert,), jnp.float32).at[target].set(route_weights.reshape(-1).astype(jnp.float32))
    padded = jnp.concatenate([normed, jnp.zeros((1, D), jnp.bfloat16)], axis=0)

    def one_expert(totals, expert):
        rows_here = lax.dynamic_slice_in_dim(pick_rows, expert * per_expert, per_expert)
        weights_here = lax.dynamic_slice_in_dim(pick_weights, expert * per_expert, per_expert)
        tokens_in = padded[rows_here]
        w_low = lax.dynamic_index_in_dim(expert_in, 2 * expert, 0, keepdims=False)
        w_high = lax.dynamic_index_in_dim(expert_in, 2 * expert + 1, 0, keepdims=False)
        low_part = jnp.dot(tokens_in[:, :HALF], w_low, preferred_element_type=jnp.float32).astype(jnp.bfloat16)
        high_part = jnp.dot(tokens_in[:, HALF:], w_high, preferred_element_type=jnp.float32).astype(jnp.bfloat16)
        inner_sum = (low_part.astype(jnp.float32) + high_part.astype(jnp.float32)).reshape(per_expert, N_HEAD, 2, HID_DEV)
        gate_in = inner_sum[:, :, 0]
        up_in = inner_sum[:, :, 1]
        active = ((up_in + 1.0) * gate_in * jax.nn.sigmoid(1.702 * gate_in)).astype(jnp.bfloat16)
        pieces = []
        for half_index in range(2):
            down_w = lax.dynamic_index_in_dim(expert_out, 2 * expert + half_index, 0, keepdims=False).reshape(N_HEAD, HID_DEV, HALF)
            block_out = jnp.einsum('mch,chd->mcd', active.astype(jnp.float32), down_w.astype(jnp.float32)).astype(jnp.bfloat16)
            pieces.append(lax.optimization_barrier(jnp.sum(block_out.astype(jnp.float32), axis=1)))
        summed = jnp.concatenate(pieces, axis=1) * weights_here[:, None]
        return (totals.at[rows_here].add(summed), None)
    totals = lax.scan(one_expert, jnp.zeros((WINDOW_TOKENS + 1, D), jnp.float32), jnp.arange(EXPERTS, dtype=jnp.int32))[0]
    return (stream, totals[:WINDOW_TOKENS].astype(jnp.bfloat16))
```

```python
import jax
import jax.numpy as jnp
from jax import lax
from jax.experimental import pallas as pl
from jax.experimental.pallas import tpu as pltpu
from jax.sharding import PartitionSpec as P

MESH = pl.DeviceIdType.MESH
BF = jnp.bfloat16
F32 = jnp.float32
I32 = jnp.int32

NS, NZ = 64, 8
NC = NS // 2
TOK, OWN, TOP = 128, 16, 4
D, HALF, CH = 2880, 1440, 12
R = 6
CAP = R // 2
MSG = 80
GS, GR = 8, 48
NR = NC * R
H = 4
SB = NR // H
GH = SB // GR
FAR = 7


def idiv(v, n):
    if n & (n - 1) == 0:
        return lax.shift_right_logical(v, jnp.full_like(v, n.bit_length() - 1))
    return ((v.astype(F32) + 0.5) * (1.0 / n)).astype(I32)


def imod(v, n):
    return v - idiv(v, n) * n


def iota(shape, dim):
    return lax.broadcasted_iota(I32, shape, dim)


def dot(a, b):
    return jnp.dot(a, b, preferred_element_type=F32)


def dot_nt(a, b):
    return lax.dot_general(a, b, (((1,), (1,)), ((), ())), preferred_element_type=F32)


def ones(cond):
    return jnp.where(cond, 1.0, 0.0).astype(BF)


def kernel(
    q_hbm, kv_hbm, wo_hbm, res_hbm, gain_hbm, info_hbm, win_hbm, wout_hbm,
    stream_ref, esum_ref,
    q_v, kv2, wo_v, res_v, gain_v, info2, win_v, wout_v,
    att_v, own_f, ps, rs, stage, xbuf, dm, cm, pm, pt,
    sb1, rb1, slots, low_own, low_oth, qs, racc, sb2, rb2, fin, fsend,
    load_sem, kv_ss, kv_rs, info_ss, info_rs, rs_ss, rs_rs, st_ss, st_rs,
    a1_ss, a1_rs, ag_ss, ag_rs, lo_ss, lo_rs, q_ss, q_rs, a2_ss, a2_rs, f_ss, f_rs,
):
    s = lax.axis_index("seq")
    z = lax.axis_index("head")
    p = lax.rem(s, 2)
    chip = lax.div(s, 2)
    other = s + 1 - 2 * p
    nxt = lax.rem(s + 1, NS)
    prv = lax.rem(s + NS - 1, NS)
    up = lax.rem(z + 1, NZ)
    dn = lax.rem(z + NZ - 1, NZ)

    loads = [
        pltpu.make_async_copy(src, dst, load_sem.at[i])
        for i, (src, dst) in enumerate(
            [
                (kv_hbm, kv2.at[1]),
                (q_hbm, q_v),
                (info_hbm.at[pl.ds(pl.multiple_of(z * OWN, OWN), OWN)], info2.at[p]),
                (wo_hbm, wo_v),
                (res_hbm, res_v),
                (gain_hbm, gain_v),
                (win_hbm.at[0], win_v),
                (wout_hbm.at[0], wout_v),
            ]
        )
    ]
    for c in loads:
        c.start()

    barrier = pltpu.get_barrier_semaphore()

    def greet(seq, head):
        pl.semaphore_signal(barrier, inc=1, device_id=(seq, head), device_id_type=MESH)

    greet(other, z)
    greet(prv, z)

    @pl.loop(1, NZ)
    def _(d):
        greet(s, lax.rem(z + d, NZ))

    @pl.loop(1, NC)
    def _(d):
        greet(lax.rem(chip + d, NC) * 2 + p, z)

    pl.semaphore_wait(barrier, 1 + 1 + (NZ - 1) + (NC - 1))

    def remote(src, dst, ss, rs_, seq, head):
        return pltpu.make_async_remote_copy(
            src_ref=src, dst_ref=dst, send_sem=ss, recv_sem=rs_,
            device_id=(seq, head), device_id_type=MESH,
        )

    loads[0].wait()
    kv_copy = remote(kv2.at[1], kv2.at[0], kv_ss, kv_rs, nxt, z)
    kv_copy.start()
    loads[2].wait()
    info_copy = remote(info2.at[p], info2.at[p], info_ss, info_rs, other, z)
    info_copy.start()
    loads[1].wait()
    kv_copy.wait_recv()

    kvf = kv2[...].reshape(2 * TOK, 128).astype(F32)
    lane = iota((2 * TOK, 128), 1)
    turned = pltpu.roll(kvf, 64, 1)
    k_even = jnp.where(lane < 64, kvf, 0.0).astype(BF)
    k_odd = jnp.where(lane >= 64, turned, 0.0).astype(BF)
    v_even = jnp.where(lane < 64, turned, 0.0).astype(BF)
    v_odd = jnp.where(lane >= 64, kvf, 0.0).astype(BF)
    qpos = iota((TOK, 2 * TOK), 0)
    kpos = iota((TOK, 2 * TOK), 1)
    allowed = (kpos > qpos) & (kpos <= qpos + TOK) & (s * TOK - TOK + kpos >= 0)
    for pair in range(4):
        qp = q_v[:, 128 * pair:128 * (pair + 1)]
        acc = None
        for kk, vv in ((k_even, v_even), (k_odd, v_odd)):
            sc = jnp.where(allowed, dot_nt(qp, kk) * 0.125, -1e30)
            ex = jnp.exp(sc - jnp.max(sc, axis=-1, keepdims=True))
            w = (ex / jnp.sum(ex, axis=-1, keepdims=True)).astype(BF)
            part = dot(w, vv)
            acc = part if acc is None else acc + part
        att_v[:, 128 * pair:128 * (pair + 1)] = acc.astype(BF)

    loads[3].wait()
    for n0 in range(0, D, 512):
        n1 = min(D, n0 + 512)
        part = dot(att_v[...], wo_v[:, n0:n1]).reshape(NZ, OWN, n1 - n0)
        own_f[:, :, n0:n1] = part
        ps[:, :, n0:n1] = part.astype(BF)

    def rs_copy(d):
        to = lax.rem(z + d, NZ)
        return remote(ps.at[to], rs.at[d - 1], rs_ss.at[d - 1], rs_rs.at[d - 1], s, to)

    for d in (4, 3, 5, 2, 6, 1, 7):
        rs_copy(d).start()

    info_copy.wait_recv()
    inf = info2[...].reshape(2 * OWN, 128)
    lanes = iota((2 * OWN, 128), 1).astype(F32)
    named = jnp.zeros((2 * OWN, 128), F32)
    weight = jnp.zeros((2 * OWN, 128), F32)
    for k in range(TOP):
        hit = inf[:, k:k + 1] == lanes
        named = named + jnp.where(hit, 1.0, 0.0)
        weight = weight + jnp.where(hit, inf[:, TOP + k:TOP + k + 1], 0.0)
    named, weight = named.astype(BF), weight.astype(BF)
    ta, tb = iota((2 * OWN, 2 * OWN), 0), iota((2 * OWN, 2 * OWN), 1)
    before = ones((tb < ta) & (idiv(tb, OWN) == idiv(ta, OWN)))
    slot = dot(before, named).astype(BF)
    ra = iota((NC * R, 128), 0)
    expand = ones(idiv(ra, R) == iota((NC * R, 128), 1))
    r_i = imod(iota((NC * R, 2 * OWN), 0), R)
    t_i = iota((NC * R, 2 * OWN), 1)
    want = r_i - idiv(r_i, CAP) * CAP
    picked = (
        (dot_nt(expand, named) > 0.5)
        & (dot_nt(expand, slot) == want.astype(F32))
        & (idiv(t_i, OWN) == idiv(r_i, CAP))
    )
    spread = ones(iota((2 * OWN, CH * 2 * OWN), 0) == imod(iota((2 * OWN, CH * 2 * OWN), 1), 2 * OWN))
    wide = dot(ones(picked), spread).astype(BF)
    m_i = iota((NC * MSG, NC * R), 0)
    rest = imod(m_i, MSG)
    rows_of = ones(
        (idiv(m_i, MSG) * R + imod(rest, R) == iota((NC * MSG, NC * R), 1)) & (rest < CH * R)
    )
    mm = iota((MSG, CH * 2 * OWN), 0)
    chunk_ok = jnp.where(idiv(mm, R) == idiv(iota((MSG, CH * 2 * OWN), 1), 2 * OWN), 1.0, 0.0)
    full = dot(rows_of, wide).reshape(NC, MSG, CH * 2 * OWN) * chunk_ok[None]
    dm[...] = full.reshape(NC * MSG, CH * 2 * OWN).astype(BF)

    def perm(shape, a_dim):
        i, j = iota(shape, a_dim), iota(shape, 1 - a_dim)
        inner = imod(j, MSG)
        return ones(
            (idiv(i, GR) == idiv(inner, R))
            & (idiv(imod(i, GR), R) == idiv(j, MSG))
            & (imod(i, R) == imod(inner, R))
            & (inner < CH * R)
        )

    pm[...] = perm((CH * GR, GS * MSG), 0)
    pt[...] = perm((GS * MSG, CH * GR), 1)

    loads[4].wait()
    loads[5].wait()
    total = res_v[...].astype(F32) + own_f[z]
    for d in (1, 7, 2, 6, 3, 5, 4):
        rs_copy(d).wait_recv()
        total = total + rs[d - 1].astype(F32)
    stream_ref[...] = total.astype(BF)
    mean_square = jnp.mean(total * total, axis=-1, keepdims=True)
    normed = (total * lax.rsqrt(mean_square + 1e-5) * gain_v[...]).astype(BF)
    for h in range(2):
        for c in range(CH):
            lo = h * HALF + c * 128
            hi = min(lo + 128, (h + 1) * HALF)
            piece = normed[:, lo:hi]
            if hi - lo < 128:
                piece = jnp.concatenate([piece, jnp.zeros((OWN, 128 - hi + lo), BF)], axis=1)
            stage[h, c] = piece
    mine = pl.ds(pl.multiple_of(p * OWN, OWN), OWN)
    st_copy = remote(stage.at[1 - p], xbuf.at[:, mine, :], st_ss, st_rs, other, z)
    st_copy.start()
    xbuf[:, mine, :] = stage[p]
    st_copy.wait_recv()

    msgs = dot(dm[...], xbuf[...].reshape(CH * 2 * OWN, 128)).astype(BF)
    sb1[...] = msgs.reshape(NC, MSG, 128)

    def a1_copy(d):
        to = lax.rem(chip + d, NC)
        return remote(sb1.at[to], rb1.at[chip], a1_ss.at[to], a1_rs.at[chip], to * 2 + p, z)

    @pl.loop(1, NC)
    def _(d):
        a1_copy(d).start()

    rb1[chip] = sb1[chip]

    def a1_wait(src):
        @pl.when(src != chip)
        def _():
            remote(sb1.at[src], rb1.at[src], a1_ss.at[src], a1_rs.at[src], src * 2 + p, z).wait_recv()

    far_from = 3 + 3 * p
    far_to = lax.rem(z + 1 + (NZ - 2) * p, NZ)
    far_back = lax.rem(z + NZ - 1 + 2 * p, NZ)

    def rows(h):
        return pl.ds(h * SB, SB)

    def ag_copy(src, dst, h, head):
        return remote(
            slots.at[src, rows(h)], slots.at[dst, rows(h)],
            ag_ss.at[dst, h], ag_rs.at[dst, h], s, head,
        )

    def lo_copy(slot_at, h):
        return remote(
            low_own.at[slot_at, rows(h)], low_oth.at[slot_at, rows(h)],
            lo_ss.at[slot_at, h], lo_rs.at[slot_at, h], other, z,
        )

    def low(slot_at, h):
        low_own[slot_at, rows(h)] = dot(slots[slot_at, rows(h)], win_v[...]).astype(BF)
        lo_copy(slot_at, h).start()

    for h in range(H):
        for g in range(h * GH, (h + 1) * GH):
            for i in range(GS):
                a1_wait(g * GS + i)
            got = dot(pm[...], rb1[GS * g:GS * (g + 1)].reshape(GS * MSG, 128)).astype(BF)
            for c in range(CH):
                width = min(128, HALF - 128 * c)
                slots[0, GR * g:GR * (g + 1), 128 * c:128 * c + width] = got[GR * c:GR * (c + 1), :width]
        ag_copy(0, 1, h, up).start()
        ag_copy(0, 4, h, dn).start()
    loads[6].wait()
    for h in range(H):
        low(0, h)

    e_l = iota((2 * OWN, NC * R), 1)
    r_l = imod(e_l, R)
    back = ones(iota((128, NC * R), 0) == idiv(iota((128, NC * R), 1), R))
    take = (dot(slot, back) == (r_l - idiv(r_l, CAP) * CAP).astype(F32)) & (
        idiv(iota((2 * OWN, NC * R), 0), OWN) == idiv(r_l, CAP)
    )
    w_t = jnp.where(take, dot(weight, back), 0.0).astype(BF)
    spread_t = ones(iota((CH * 2 * OWN, 2 * OWN), 1) == imod(iota((CH * 2 * OWN, 2 * OWN), 0), 2 * OWN))
    tall = dot(spread_t, w_t).astype(BF)
    m_l = iota((NC * R, NC * MSG), 1)
    rest_l = imod(m_l, MSG)
    cols_of = ones(
        (idiv(m_l, MSG) * R + imod(rest_l, R) == iota((NC * R, NC * MSG), 0)) & (rest_l < CH * R)
    )
    full_t = dot(tall, cols_of)
    c_l = idiv(imod(iota((CH * 2 * OWN, NC * MSG), 1), MSG), R)
    cm[...] = jnp.where(c_l == idiv(iota((CH * 2 * OWN, NC * MSG), 0), 2 * OWN), full_t, 0.0).astype(BF)

    for k in (1, 2, 3):
        for h in range(H):
            ag_copy(0, k, h, up).wait_recv()
            if k < 3:
                ag_copy(k, k + 1, h, up).start()
            ag_copy(0, k + 3, h, dn).wait_recv()
            if k < 3:
                ag_copy(k + 3, k + 4, h, dn).start()
            else:
                ag_copy(far_from, FAR, h, far_to).start()
            low(k, h)
            low(k + 3, h)
    loads[7].wait()
    for h in range(H):
        ag_copy(far_from, FAR, h, far_to).wait_recv()
        low(FAR, h)

    def expert(slot_at, h):
        lo_copy(slot_at, h).wait_recv()
        inner = low_own[slot_at, rows(h)].astype(F32) + low_oth[slot_at, rows(h)].astype(F32)
        gate, upv = inner[:, :192], inner[:, 192:]
        active = ((upv + 1.0) * gate * jax.nn.sigmoid(1.702 * gate)).astype(BF)
        return dot(active, wout_v[...])

    def q_copy(slot_at, dst, h, head):
        return remote(
            qs.at[slot_at, rows(h)], racc.at[dst, rows(h)],
            q_ss.at[slot_at, h], q_rs.at[dst, h], s, head,
        )

    for h in range(H):
        qs[FAR, rows(h)] = expert(FAR, h).astype(BF)
        q_copy(FAR, FAR, h, far_back).start()
    for h in range(H):
        below, above = expert(3, h), expert(6, h)
        q_copy(FAR, FAR, h, far_back).wait_recv()
        got = racc[FAR, rows(h)].astype(F32)
        qs[3, rows(h)] = (below + jnp.where(p == 0, got, 0.0)).astype(BF)
        q_copy(3, 2, h, dn).start()
        qs[6, rows(h)] = (above + jnp.where(p == 0, 0.0, got)).astype(BF)
        q_copy(6, 5, h, up).start()
    for k in (2, 1):
        for h in range(H):
            below, above = expert(k, h), expert(k + 3, h)
            q_copy(k, k, h, dn).wait_recv()
            qs[k, rows(h)] = (below + racc[k, rows(h)].astype(F32)).astype(BF)
            q_copy(k, k - 1, h, dn).start()
            q_copy(k + 3, k + 3, h, up).wait_recv()
            qs[k + 3, rows(h)] = (above + racc[k + 3, rows(h)].astype(F32)).astype(BF)
            q_copy(k + 3, k + 2, h, up).start()

    def a2_copy(to):
        return remote(sb2.at[to], rb2.at[chip], a2_ss.at[to], a2_rs.at[chip], to * 2 + p, z)

    for h in range(H):
        value = expert(0, h)
        q_copy(0, 0, h, dn).wait_recv()
        q_copy(0, 3, h, up).wait_recv()
        value = (value + racc[0, rows(h)].astype(F32) + racc[3, rows(h)].astype(F32)).astype(BF)
        for i in range(GH):
            g = h * GH + i
            part = value[GR * i:GR * (i + 1)]
            pieces = [part[:, 128 * c:128 * (c + 1)] for c in range(CH - 1)]
            last = part[:, 128 * (CH - 1):]
            pieces.append(jnp.concatenate([last, jnp.zeros((GR, 128 * CH - HALF), BF)], axis=1))
            out = dot(pt[...], jnp.concatenate(pieces, axis=0)).astype(BF)
            sb2[GS * g:GS * (g + 1)] = out.reshape(GS, MSG, 128)

            @pl.loop(0, GS)
            def _(j):
                to = g * GS + j

                @pl.when(to != chip)
                def _():
                    a2_copy(to).start()

    rb2[chip] = sb2[chip]

    @pl.loop(0, NC)
    def _(src):
        @pl.when(src != chip)
        def _():
            remote(sb2.at[src], rb2.at[src], a2_ss.at[src], a2_rs.at[src], src * 2 + p, z).wait_recv()

    out = dot(cm[...], rb2[...].reshape(NC * MSG, 128)).astype(BF).reshape(CH, 2 * OWN, 128)
    cm_out = xbuf
    cm_out[...] = out
    theirs = pl.ds(pl.multiple_of((1 - p) * OWN, OWN), OWN)
    fsend[...] = cm_out[:, theirs, :]
    f_copy = remote(fsend, fin.at[p], f_ss, f_rs, other, z)
    f_copy.start()
    fin[p] = cm_out[:, mine, :]
    f_copy.wait_recv()
    esum_ref[...] = jnp.concatenate(
        [fin[h, c][:, :min(128, HALF - 128 * c)] for h in range(2) for c in range(CH)], axis=1
    )

    kv_copy.wait_send()
    info_copy.wait_send()
    st_copy.wait_send()
    f_copy.wait_send()
    for d in range(1, NZ):
        rs_copy(d).wait_send()

    @pl.loop(1, NC)
    def _(d):
        a1_copy(d).wait_send()
        a2_copy(lax.rem(chip + d, NC)).wait_send()

    for slot_at in range(8):
        for h in range(H):
            lo_copy(slot_at, h).wait_send()
            if slot_at:
                ag_copy(0, slot_at, h, up).wait_send()
                q_copy(slot_at, slot_at, h, up).wait_send()


def per_device(q, kv, wo, res, gain, ids, weights, w_in, w_out):
    info = jnp.concatenate([ids.astype(F32), weights.astype(F32), jnp.zeros((TOK, 128 - 2 * TOP), F32)], axis=1)
    vm = pltpu.VMEM
    dma = pltpu.SemaphoreType.DMA
    scratch = [
        vm((TOK, 512), BF), vm((2, TOK, 128), BF), vm((512, D), BF), vm((OWN, D), BF), vm((1, D), F32),
        vm((2, OWN, 128), F32), vm((HALF, 384), BF), vm((192, HALF), BF),
        vm((TOK, 512), BF), vm((NZ, OWN, D), F32), vm((NZ, OWN, D), BF), vm((NZ - 1, OWN, D), BF),
        vm((2, CH, OWN, 128), BF), vm((CH, 2 * OWN, 128), BF),
        vm((NC * MSG, CH * 2 * OWN), BF), vm((CH * 2 * OWN, NC * MSG), BF),
        vm((CH * GR, GS * MSG), BF), vm((GS * MSG, CH * GR), BF),
        vm((NC, MSG, 128), BF), vm((NC, MSG, 128), BF),
        vm((8, NR, HALF), BF), vm((8, NR, 384), BF), vm((8, NR, 384), BF),
        vm((8, NR, HALF), BF), vm((8, NR, HALF), BF),
        vm((NC, MSG, 128), BF), vm((NC, MSG, 128), BF),
        vm((2, CH, OWN, 128), BF), vm((CH, OWN, 128), BF),
        dma((8,)), dma, dma, dma, dma, dma((NZ - 1,)), dma((NZ - 1,)), dma, dma,
        dma((NC,)), dma((NC,)), dma((8, H)), dma((8, H)), dma((8, H)), dma((8, H)),
        dma((8, H)), dma((8, H)), dma((NC,)), dma((NC,)), dma, dma,
    ]
    return pl.pallas_call(
        kernel,
        out_shape=(jax.ShapeDtypeStruct((OWN, D), BF), jax.ShapeDtypeStruct((OWN, D), BF)),
        in_specs=[pl.BlockSpec(memory_space=pl.ANY)] * 8,
        out_specs=(pl.BlockSpec(memory_space=vm), pl.BlockSpec(memory_space=vm)),
        scratch_shapes=scratch,
        compiler_params=pltpu.CompilerParams(
            collective_id=0, has_side_effects=True, vmem_limit_bytes=58 * 1024 * 1024
        ),
        cost_estimate=pl.CostEstimate(flops=4_000_000_000, bytes_accessed=8_000_000, transcendentals=300_000),
    )(q, kv.reshape(TOK, 128), wo, res, gain.reshape(1, D), info, w_in, w_out)


def solution(mesh):
    placed = (
        P("seq", "head"), P("seq", "head", None), P("head", None), P(("seq", "head"), None), P(),
        P("seq", None), P("seq", None), P("seq", None, "head"), P("seq", "head", None),
    )
    return jax.shard_map(
        per_device, mesh=mesh, in_specs=placed,
        out_specs=(P(("seq", "head"), None), P(("seq", "head"), None)), check_vma=False,
    )
```

```python
import jax
import jax.numpy as jnp
from jax import lax
from jax.experimental import pallas as pl
from jax.experimental.pallas import tpu as pltpu
from jax.sharding import PartitionSpec as P

MESH = pl.DeviceIdType.MESH
BF = jnp.bfloat16
F32 = jnp.float32
I32 = jnp.int32

NS, NZ = 64, 8
NC = NS // 2
TOK, OWN, TOP = 128, 16, 4
D, HALF, CH = 2880, 1440, 12
NX, NY = 4, 8
R = 4
CAP = R // 2
MSG = 48
GS, GR = 4, 16
NR = NC * R
H = 2
SB = NR // H
GH = SB // GR
FAR = 7
OV = 8
OM = 32
OB = CH * OWN


def idiv(v, n):
    if n & (n - 1) == 0:
        return lax.shift_right_logical(v, jnp.full_like(v, n.bit_length() - 1))
    return ((v.astype(F32) + 0.5) * (1.0 / n)).astype(I32)


def imod(v, n):
    return v - idiv(v, n) * n


def iota(shape, dim):
    return lax.broadcasted_iota(I32, shape, dim)


def dot(a, b):
    return jnp.dot(a, b, preferred_element_type=F32)


def dot_nt(a, b):
    return lax.dot_general(a, b, (((1,), (1,)), ((), ())), preferred_element_type=F32)


def ones(cond):
    return jnp.where(cond, 1.0, 0.0).astype(BF)


def kernel(
    q_hbm, kv_hbm, wo_hbm, res_hbm, gain_hbm, ids_hbm, rw_hbm, win_hbm, wout_hbm,
    stream_ref, esum_ref,
    q_v, kv2, wo_v, res_v, gain_v, ids_v, rw_v, both, info2, win_v, wout_v,
    att_v, own_f, ps, rs, stage, xbuf, dm, cm, pm, pt,
    sb1, rb1, slots, low_own, low_oth, qs, racc, sb2, rb2, fin, fsend,
    om, co, p2, p2t, osend, oz, ox, obuf, oret, osel, oyr, ozs, ozr,
    load_sem, kv_ss, kv_rs, info_ss, info_rs, rs_ss, rs_rs, st_ss, st_rs,
    a1_ss, a1_rs, ag_ss, ag_rs, lo_ss, lo_rs, q_ss, q_rs, a2_ss, a2_rs, f_ss, f_rs,
    oz_ss, oz_rs, oy_ss, oy_rs, ox_ss, ox_rs, or_ss, or_rs, oyr_ss, oyr_rs, ozr_ss, ozr_rs,
):
    s = lax.axis_index("seq")
    z = lax.axis_index("head")
    p = lax.rem(s, 2)
    chip = lax.div(s, 2)
    x = lax.rem(chip, NX)
    y = lax.div(chip, NX)
    other = s + 1 - 2 * p
    nxt = lax.rem(s + 1, NS)
    prv = lax.rem(s + NS - 1, NS)
    up = lax.rem(z + 1, NZ)
    dn = lax.rem(z + NZ - 1, NZ)

    loads = [
        pltpu.make_async_copy(src, dst, load_sem.at[i])
        for i, (src, dst) in enumerate(
            [
                (kv_hbm, kv2.at[1]),
                (q_hbm, q_v),
                (ids_hbm, ids_v),
                (wo_hbm, wo_v),
                (res_hbm, res_v),
                (gain_hbm, gain_v),
                (win_hbm.at[0], win_v),
                (wout_hbm.at[0], wout_v),
                (rw_hbm, rw_v),
            ]
        )
    ]
    for c in loads:
        c.start()

    barrier = pltpu.get_barrier_semaphore()

    def greet(seq, head):
        pl.semaphore_signal(barrier, inc=1, device_id=(seq, head), device_id_type=MESH)

    greet(other, z)
    greet(prv, z)

    @pl.loop(1, NZ)
    def _(d):
        greet(s, lax.rem(z + d, NZ))

    @pl.loop(1, NC)
    def _(d):
        greet(lax.rem(chip + d, NC) * 2 + p, z)

    pl.semaphore_wait(barrier, 1 + 1 + (NZ - 1) + (NC - 1))

    def remote(src, dst, ss, rs_, seq, head):
        return pltpu.make_async_remote_copy(
            src_ref=src, dst_ref=dst, send_sem=ss, recv_sem=rs_,
            device_id=(seq, head), device_id_type=MESH,
        )

    loads[0].wait()
    kv_copy = remote(kv2.at[1], kv2.at[0], kv_ss, kv_rs, nxt, z)
    kv_copy.start()
    loads[2].wait()
    loads[8].wait()
    both[0:TOP] = ids_v[...].astype(F32)
    both[TOP:] = rw_v[...].astype(F32)
    chosen = ones(iota((OWN, TOK), 1) == iota((OWN, TOK), 0) + z * OWN)
    info2[p, :, 0:2 * TOP] = dot_nt(chosen, both[...].astype(BF))
    info_copy = remote(info2.at[p], info2.at[p], info_ss, info_rs, other, z)
    info_copy.start()
    loads[1].wait()
    kv_copy.wait_recv()

    kvf = kv2[...].reshape(2 * TOK, 128).astype(F32)
    lane = iota((2 * TOK, 128), 1)
    turned = pltpu.roll(kvf, 64, 1)
    k_even = jnp.where(lane < 64, kvf, 0.0).astype(BF)
    k_odd = jnp.where(lane >= 64, turned, 0.0).astype(BF)
    v_even = jnp.where(lane < 64, turned, 0.0).astype(BF)
    v_odd = jnp.where(lane >= 64, kvf, 0.0).astype(BF)
    qpos = iota((TOK, 2 * TOK), 0)
    kpos = iota((TOK, 2 * TOK), 1)
    allowed = (kpos > qpos) & (kpos <= qpos + TOK) & (s * TOK - TOK + kpos >= 0)
    for pair in range(4):
        qp = q_v[:, 128 * pair:128 * (pair + 1)]
        acc = None
        for kk, vv in ((k_even, v_even), (k_odd, v_odd)):
            sc = jnp.where(allowed, dot_nt(qp, kk) * 0.125, -1e30)
            ex = jnp.exp(sc - jnp.max(sc, axis=-1, keepdims=True))
            w = (ex / jnp.sum(ex, axis=-1, keepdims=True)).astype(BF)
            part = dot(w, vv)
            acc = part if acc is None else acc + part
        att_v[:, 128 * pair:128 * (pair + 1)] = acc.astype(BF)

    loads[3].wait()
    for n0 in range(0, D, 512):
        n1 = min(D, n0 + 512)
        part = dot_nt(att_v[...], wo_v[n0:n1]).reshape(NZ, OWN, n1 - n0)
        own_f[:, :, n0:n1] = part
        ps[:, :, n0:n1] = part.astype(BF)

    def rs_copy(d):
        to = lax.rem(z + d, NZ)
        return remote(ps.at[to], rs.at[d - 1], rs_ss.at[d - 1], rs_rs.at[d - 1], s, to)

    for d in (4, 3, 5, 2, 6, 1, 7):
        rs_copy(d).start()

    info_copy.wait_recv()
    inf = info2[...].reshape(2 * OWN, 128)
    lanes = iota((2 * OWN, 128), 1).astype(F32)
    named = jnp.zeros((2 * OWN, 128), F32)
    weight = jnp.zeros((2 * OWN, 128), F32)
    for k in range(TOP):
        hit = inf[:, k:k + 1] == lanes
        named = named + jnp.where(hit, 1.0, 0.0)
        weight = weight + jnp.where(hit, inf[:, TOP + k:TOP + k + 1], 0.0)
    named, weight = named.astype(BF), weight.astype(BF)
    ta, tb = iota((2 * OWN, 2 * OWN), 0), iota((2 * OWN, 2 * OWN), 1)
    before = ones((tb < ta) & (idiv(tb, OWN) == idiv(ta, OWN)))
    slot = dot(before, named).astype(BF)
    ra = iota((NC * R, 128), 0)
    expand = ones(idiv(ra, R) == iota((NC * R, 128), 1))
    r_i = imod(iota((NC * R, 2 * OWN), 0), R)
    t_i = iota((NC * R, 2 * OWN), 1)
    want = r_i - idiv(r_i, CAP) * CAP
    picked = (
        (dot_nt(expand, named) > 0.5)
        & (dot_nt(expand, slot) == want.astype(F32))
        & (idiv(t_i, OWN) == idiv(r_i, CAP))
    )
    spread = ones(iota((2 * OWN, CH * 2 * OWN), 0) == imod(iota((2 * OWN, CH * 2 * OWN), 1), 2 * OWN))
    wide = dot(ones(picked), spread).astype(BF)
    m_i = iota((NC * MSG, NC * R), 0)
    rest = imod(m_i, MSG)
    rows_of = ones(
        (idiv(m_i, MSG) * R + imod(rest, R) == iota((NC * MSG, NC * R), 1)) & (rest < CH * R)
    )
    mm = iota((MSG, CH * 2 * OWN), 0)
    chunk_ok = jnp.where(idiv(mm, R) == idiv(iota((MSG, CH * 2 * OWN), 1), 2 * OWN), 1.0, 0.0)
    full = dot(rows_of, wide).reshape(NC, MSG, CH * 2 * OWN) * chunk_ok[None]
    dm[...] = full.reshape(NC * MSG, CH * 2 * OWN).astype(BF)

    third = jnp.where((named > 0.5) & (slot > 1.5), 1.0, 0.0)
    third_row = dot_nt(jnp.ones((8, 128), BF), third.astype(BF))[0:1]
    third_wide = dot(jnp.broadcast_to(third_row, (8, 2 * OWN)).astype(BF), spread)[0:1]
    o_m, o_q = iota((OM, CH * 2 * OWN), 0), iota((OM, CH * 2 * OWN), 1)
    o_ok = (idiv(o_m, 2) == idiv(o_q, 2 * OWN)) & (imod(o_m, 2) == imod(idiv(o_q, OWN), 2))
    om[...] = jnp.where(o_ok, third_wide, 0.0).astype(BF)
    hot = jnp.max(third, axis=0, keepdims=True)
    e_row = iota((1, 128), 1)
    hot_x = jnp.sum(hot * imod(e_row, NX).astype(F32), axis=1, keepdims=True)
    hot_y = jnp.sum(hot * idiv(e_row, NX).astype(F32), axis=1, keepdims=True)

    def perm2(shape, a_dim):
        i, j = iota(shape, a_dim), iota(shape, 1 - a_dim)
        inner = imod(j, OM)
        return ones(
            (idiv(i, OWN) == idiv(inner, 2))
            & (idiv(imod(i, OWN), 2) == idiv(j, OM))
            & (imod(i, 2) == imod(inner, 2))
        )

    p2[...] = perm2((OB, NZ * OM), 0)
    p2t[...] = perm2((NZ * OM, OB), 1)

    def perm(shape, a_dim):
        i, j = iota(shape, a_dim), iota(shape, 1 - a_dim)
        inner = imod(j, MSG)
        return ones(
            (idiv(i, GR) == idiv(inner, R))
            & (idiv(imod(i, GR), R) == idiv(j, MSG))
            & (imod(i, R) == imod(inner, R))
            & (inner < CH * R)
        )

    pm[...] = perm((CH * GR, GS * MSG), 0)
    pt[...] = perm((GS * MSG, CH * GR), 1)

    loads[4].wait()
    loads[5].wait()
    total = res_v[...].astype(F32) + own_f[z]
    for d in (1, 7, 2, 6, 3, 5, 4):
        rs_copy(d).wait_recv()
        total = total + rs[d - 1].astype(F32)
    stream_ref[...] = total.astype(BF)
    mean_square = jnp.mean(total * total, axis=-1, keepdims=True)
    normed = (total * lax.rsqrt(mean_square + 1e-5) * gain_v[...].reshape(1, D)).astype(BF)
    for h in range(2):
        for c in range(CH):
            lo = h * HALF + c * 128
            hi = min(lo + 128, (h + 1) * HALF)
            piece = normed[:, lo:hi]
            if hi - lo < 128:
                piece = jnp.concatenate([piece, jnp.zeros((OWN, 128 - hi + lo), BF)], axis=1)
            stage[h, c] = piece
    mine = pl.ds(pl.multiple_of(p * OWN, OWN), OWN)
    st_copy = remote(stage.at[1 - p], xbuf.at[:, mine, :], st_ss, st_rs, other, z)
    st_copy.start()
    xbuf[:, mine, :] = stage[p]
    st_copy.wait_recv()

    osend[...] = dot(om[...], xbuf[...].reshape(CH * 2 * OWN, 128)).astype(BF)

    def oz_copy(d):
        return remote(osend, oz.at[z], oz_ss.at[d - 1], oz_rs.at[z], s, lax.rem(z + d, NZ))

    for d in range(1, NZ):
        oz_copy(d).start()
    oz[z] = osend[...]

    def at(y_, x_):
        return (y_ * NX + x_) * 2 + p

    msgs = dot(dm[...], xbuf[...].reshape(CH * 2 * OWN, 128)).astype(BF)
    sb1[...] = msgs.reshape(NC, MSG, 128)

    def a1_copy(d):
        to = lax.rem(chip + d, NC)
        return remote(sb1.at[to], rb1.at[chip], a1_ss.at[to], a1_rs.at[chip], to * 2 + p, z)

    @pl.loop(1, NC)
    def _(d):
        a1_copy(d).start()

    rb1[chip] = sb1[chip]

    def a1_wait(src):
        @pl.when(src != chip)
        def _():
            remote(sb1.at[src], rb1.at[src], a1_ss.at[src], a1_rs.at[src], src * 2 + p, z).wait_recv()

    far_from = 3 + 3 * p
    far_to = lax.rem(z + 1 + (NZ - 2) * p, NZ)
    far_back = lax.rem(z + NZ - 1 + 2 * p, NZ)

    def rows(h):
        return pl.ds(h * SB, SB)

    def ag_copy(src, dst, h, head):
        return remote(
            slots.at[src, rows(h)], slots.at[dst, rows(h)],
            ag_ss.at[dst, h], ag_rs.at[dst, h], s, head,
        )

    def lo_copy(slot_at, h):
        return remote(
            low_own.at[slot_at, rows(h)], low_oth.at[slot_at, rows(h)],
            lo_ss.at[slot_at, h], lo_rs.at[slot_at, h], other, z,
        )

    def low(slot_at, h):
        low_own[slot_at, rows(h)] = dot(slots[slot_at, rows(h)], win_v[...]).astype(BF)
        lo_copy(slot_at, h).start()

    for h in range(H):
        for g in range(h * GH, (h + 1) * GH):
            for i in range(GS):
                a1_wait(g * GS + i)
            got = dot(pm[...], rb1[GS * g:GS * (g + 1)].reshape(GS * MSG, 128)).astype(BF)
            for c in range(CH):
                width = min(128, HALF - 128 * c)
                slots[0, GR * g:GR * (g + 1), 128 * c:128 * c + width] = got[GR * c:GR * (c + 1), :width]
        ag_copy(0, 1, h, up).start()
        ag_copy(0, 4, h, dn).start()
    for d in range(1, NZ):
        from_z = lax.rem(z + d, NZ)
        remote(osend, oz.at[from_z], oz_ss.at[d - 1], oz_rs.at[from_z], s, from_z).wait_recv()
    ox[x, y] = dot(p2[...], oz[...].reshape(NZ * OM, 128)).astype(BF)

    def oy_copy(d):
        to = lax.rem(y + d, NY)
        return remote(ox.at[x, y], ox.at[x, y], oy_ss.at[d - 1], oy_rs.at[y], at(to, x), z)

    for d in range(1, NY):
        oy_copy(d).start()

    loads[6].wait()
    for h in range(H):
        low(0, h)

    e_l = iota((2 * OWN, NC * R), 1)
    r_l = imod(e_l, R)
    back = ones(iota((128, NC * R), 0) == idiv(iota((128, NC * R), 1), R))
    take = (dot(slot, back) == (r_l - idiv(r_l, CAP) * CAP).astype(F32)) & (
        idiv(iota((2 * OWN, NC * R), 0), OWN) == idiv(r_l, CAP)
    )
    w_t = jnp.where(take, dot(weight, back), 0.0).astype(BF)
    spread_t = ones(iota((CH * 2 * OWN, 2 * OWN), 1) == imod(iota((CH * 2 * OWN, 2 * OWN), 0), 2 * OWN))
    tall = dot(spread_t, w_t).astype(BF)
    m_l = iota((NC * R, NC * MSG), 1)
    rest_l = imod(m_l, MSG)
    cols_of = ones(
        (idiv(m_l, MSG) * R + imod(rest_l, R) == iota((NC * R, NC * MSG), 0)) & (rest_l < CH * R)
    )
    full_t = dot(tall, cols_of)
    c_l = idiv(imod(iota((CH * 2 * OWN, NC * MSG), 1), MSG), R)
    w_third = jnp.sum(third * weight.astype(F32), axis=1, keepdims=True)
    w_tall = dot(spread_t, jnp.broadcast_to(w_third, (2 * OWN, 128)).astype(BF))[:, :OM]
    o_q, o_m = iota((CH * 2 * OWN, OM), 0), iota((CH * 2 * OWN, OM), 1)
    o_ok = (idiv(o_m, 2) == idiv(o_q, 2 * OWN)) & (imod(o_m, 2) == imod(idiv(o_q, OWN), 2))
    co[...] = jnp.where(o_ok, w_tall, 0.0).astype(BF)
    cm[...] = jnp.where(c_l == idiv(iota((CH * 2 * OWN, NC * MSG), 0), 2 * OWN), full_t, 0.0).astype(BF)

    def ox_copy(d, from_y):
        return remote(
            ox.at[x, from_y], ox.at[x, from_y], ox_ss.at[d - 1, from_y], ox_rs.at[x, from_y],
            at(y, lax.rem(x + d, NX)), z,
        )

    def ox_send():
        @pl.loop(0, NY)
        def _(dy):
            from_y = lax.rem(y + dy, NY)

            @pl.when(dy > 0)
            def _():
                remote(
                    ox.at[x, from_y], ox.at[x, from_y], ox_ss.at[0, from_y], oy_rs.at[from_y], at(from_y, x), z
                ).wait_recv()

            for d in range(1, NX):
                ox_copy(d, from_y).start()

    def ox_take():
        for d in range(NX):
            from_x = lax.rem(x + d, NX)
            if d:
                @pl.loop(0, NY)
                def _(from_y):
                    remote(
                        ox.at[from_x, from_y], ox.at[from_x, from_y], ox_ss.at[d - 1, from_y],
                        ox_rs.at[from_x, from_y], at(y, from_x), z,
                    ).wait_recv()
            for c in range(CH):
                width = min(128, HALF - 128 * c)
                piece = ox[from_x, :, OWN * c:OWN * (c + 1), :].reshape(NR, 128)
                slots[OV + d, :, 128 * c:128 * c + width] = piece[:, :width]
            for h in range(H):
                low(OV + d, h)

    for k in (1, 2, 3):
        for h in range(H):
            ag_copy(0, k, h, up).wait_recv()
            if k < 3:
                ag_copy(k, k + 1, h, up).start()
            ag_copy(0, k + 3, h, dn).wait_recv()
            if k < 3:
                ag_copy(k + 3, k + 4, h, dn).start()
            else:
                ag_copy(far_from, FAR, h, far_to).start()
            low(k, h)
            low(k + 3, h)
        if k == 1:
            ox_send()
    loads[7].wait()
    for h in range(H):
        ag_copy(far_from, FAR, h, far_to).wait_recv()
        low(FAR, h)
    ox_take()

    def expert(slot_at, h):
        lo_copy(slot_at, h).wait_recv()
        inner = low_own[slot_at, rows(h)].astype(F32) + low_oth[slot_at, rows(h)].astype(F32)
        gate, upv = inner[:, :192], inner[:, 192:]
        active = ((upv + 1.0) * gate * jax.nn.sigmoid(1.702 * gate)).astype(BF)
        return dot(active, wout_v[...])

    def q_copy(slot_at, dst, h, head):
        return remote(
            qs.at[slot_at, rows(h)], racc.at[dst, rows(h)],
            q_ss.at[slot_at, h], q_rs.at[dst, h], s, head,
        )

    for h in range(H):
        qs[FAR, rows(h)] = expert(FAR, h).astype(BF)
        q_copy(FAR, FAR, h, far_back).start()
    for h in range(H):
        below, above = expert(3, h), expert(6, h)
        q_copy(FAR, FAR, h, far_back).wait_recv()
        got = racc[FAR, rows(h)].astype(F32)
        qs[3, rows(h)] = (below + jnp.where(p == 0, got, 0.0)).astype(BF)
        q_copy(3, 2, h, dn).start()
        qs[6, rows(h)] = (above + jnp.where(p == 0, 0.0, got)).astype(BF)
        q_copy(6, 5, h, up).start()

    def or_copy(d):
        return remote(
            obuf.at[d], oret.at[x], or_ss.at[d - 1], or_rs.at[x], at(y, lax.rem(x + d, NX)), z
        )

    def oyr_copy(d):
        to = lax.rem(y + d, NY)
        return remote(osel.at[to], oyr.at[y], oyr_ss.at[d - 1], oyr_rs.at[y], at(to, x), z)

    def ozr_copy(d):
        to = lax.rem(z + d, NZ)
        return remote(ozs.at[to], ozr.at[z], ozr_ss.at[d - 1], ozr_rs.at[z], s, to)

    def ov_expert():
        for d in (2, 1, 3, 0):
            for h in range(H):
                value = expert(OV + d, h).astype(BF)
                n = SB // OWN
                for c in range(CH):
                    piece = value[:, 128 * c:128 * (c + 1)]
                    if piece.shape[1] < 128:
                        piece = jnp.concatenate([piece, jnp.zeros((SB, 128 * CH - HALF), BF)], axis=1)
                    obuf[d, n * h:n * (h + 1), OWN * c:OWN * (c + 1), :] = piece.reshape(n, OWN, 128)
            if d:
                or_copy(d).start()

    def ov_back_y():
        for d in range(1, NX):
            from_x = lax.rem(x + d, NX)
            remote(obuf.at[d], oret.at[from_x], or_ss.at[d - 1], or_rs.at[from_x], at(y, from_x), z).wait_recv()

        @pl.loop(0, NY)
        def _(to_y):
            acc = jnp.where(hot_x == x.astype(F32), obuf[0, to_y].astype(F32), 0.0)
            for d in range(1, NX):
                from_x = lax.rem(x + d, NX)
                acc = jnp.where(hot_x == from_x.astype(F32), oret[from_x, to_y].astype(F32), acc)
            osel[to_y] = acc.astype(BF)

        for d in range(1, NY):
            oyr_copy(d).start()

    def ov_back_z():
        acc = jnp.where(hot_y == y.astype(F32), osel[y].astype(F32), 0.0)
        for d in range(1, NY):
            from_y = lax.rem(y + d, NY)
            remote(osel.at[from_y], oyr.at[from_y], oyr_ss.at[d - 1], oyr_rs.at[from_y], at(from_y, x), z).wait_recv()
            acc = jnp.where(hot_y == from_y.astype(F32), oyr[from_y].astype(F32), acc)
        ozs[...] = dot(p2t[...], acc.astype(BF)).astype(BF).reshape(NZ, OM, 128)
        for d in range(1, NZ):
            ozr_copy(d).start()
        ozr[z] = ozs[z]

    ov_expert()
    for k in (2, 1):
        for h in range(H):
            below, above = expert(k, h), expert(k + 3, h)
            q_copy(k, k, h, dn).wait_recv()
            qs[k, rows(h)] = (below + racc[k, rows(h)].astype(F32)).astype(BF)
            q_copy(k, k - 1, h, dn).start()
            q_copy(k + 3, k + 3, h, up).wait_recv()
            qs[k + 3, rows(h)] = (above + racc[k + 3, rows(h)].astype(F32)).astype(BF)
            q_copy(k + 3, k + 2, h, up).start()
        if k == 2:
            ov_back_y()

    def a2_copy(to):
        return remote(sb2.at[to], rb2.at[chip], a2_ss.at[to], a2_rs.at[chip], to * 2 + p, z)

    for h in range(H):
        value = expert(0, h)
        q_copy(0, 0, h, dn).wait_recv()
        q_copy(0, 3, h, up).wait_recv()
        value = (value + racc[0, rows(h)].astype(F32) + racc[3, rows(h)].astype(F32)).astype(BF)
        for i in range(GH):
            g = h * GH + i
            part = value[GR * i:GR * (i + 1)]
            pieces = [part[:, 128 * c:128 * (c + 1)] for c in range(CH - 1)]
            last = part[:, 128 * (CH - 1):]
            pieces.append(jnp.concatenate([last, jnp.zeros((GR, 128 * CH - HALF), BF)], axis=1))
            out = dot(pt[...], jnp.concatenate(pieces, axis=0)).astype(BF)
            sb2[GS * g:GS * (g + 1)] = out.reshape(GS, MSG, 128)

            @pl.loop(0, GS)
            def _(j):
                to = g * GS + j

                @pl.when(to != chip)
                def _():
                    a2_copy(to).start()

    ov_back_z()
    rb2[chip] = sb2[chip]
    for d in range(1, NZ):
        from_z = lax.rem(z + d, NZ)
        remote(ozs.at[from_z], ozr.at[from_z], ozr_ss.at[d - 1], ozr_rs.at[from_z], s, from_z).wait_recv()
    third_sum = jnp.sum(ozr[...].astype(F32), axis=0).astype(BF)

    @pl.loop(0, NC)
    def _(src):
        @pl.when(src != chip)
        def _():
            remote(sb2.at[src], rb2.at[src], a2_ss.at[src], a2_rs.at[src], src * 2 + p, z).wait_recv()

    out = dot(cm[...], rb2[...].reshape(NC * MSG, 128)) + dot(co[...], third_sum)
    out = out.astype(BF).reshape(CH, 2 * OWN, 128)
    cm_out = xbuf
    cm_out[...] = out
    theirs = pl.ds(pl.multiple_of((1 - p) * OWN, OWN), OWN)
    fsend[...] = cm_out[:, theirs, :]
    f_copy = remote(fsend, fin.at[p], f_ss, f_rs, other, z)
    f_copy.start()
    fin[p] = cm_out[:, mine, :]
    f_copy.wait_recv()
    esum_ref[...] = jnp.concatenate(
        [fin[h, c][:, :min(128, HALF - 128 * c)] for h in range(2) for c in range(CH)], axis=1
    )

    kv_copy.wait_send()
    info_copy.wait_send()
    st_copy.wait_send()
    f_copy.wait_send()
    for d in range(1, NZ):
        rs_copy(d).wait_send()
        oz_copy(d).wait_send()
        oy_copy(d).wait_send()
        oyr_copy(d).wait_send()
        ozr_copy(d).wait_send()
    for d in range(1, NX):
        or_copy(d).wait_send()

        @pl.loop(0, NY)
        def _(from_y):
            ox_copy(d, from_y).wait_send()

    @pl.loop(1, NC)
    def _(d):
        a1_copy(d).wait_send()
        a2_copy(lax.rem(chip + d, NC)).wait_send()

    for slot_at in range(OV + NX):
        for h in range(H):
            lo_copy(slot_at, h).wait_send()
            if 0 < slot_at < OV:
                ag_copy(0, slot_at, h, up).wait_send()
                q_copy(slot_at, slot_at, h, up).wait_send()


def per_device(q, kv, wo, res, gain, ids, weights, w_in, w_out):
    vm = pltpu.VMEM
    dma = pltpu.SemaphoreType.DMA
    scratch = [
        vm((TOK, 512), BF), vm((2, TOK, 128), BF), vm((D, 512), BF), vm((OWN, D), BF), vm((D,), F32),
        vm((TOP, TOK), I32), vm((TOP, TOK), BF), vm((2 * TOP, TOK), F32), vm((2, OWN, 128), F32), vm((HALF, 384), BF), vm((192, HALF), BF),
        vm((TOK, 512), BF), vm((NZ, OWN, D), F32), vm((NZ, OWN, D), BF), vm((NZ - 1, OWN, D), BF),
        vm((2, CH, OWN, 128), BF), vm((CH, 2 * OWN, 128), BF),
        vm((NC * MSG, CH * 2 * OWN), BF), vm((CH * 2 * OWN, NC * MSG), BF),
        vm((CH * GR, GS * MSG), BF), vm((GS * MSG, CH * GR), BF),
        vm((NC, MSG, 128), BF), vm((NC, MSG, 128), BF),
        vm((OV + NX, NR, HALF), BF), vm((OV + NX, NR, 384), BF), vm((OV + NX, NR, 384), BF),
        vm((8, NR, HALF), BF), vm((8, NR, HALF), BF),
        vm((NC, MSG, 128), BF), vm((NC, MSG, 128), BF),
        vm((2, CH, OWN, 128), BF), vm((CH, OWN, 128), BF),
        vm((OM, CH * 2 * OWN), BF), vm((CH * 2 * OWN, OM), BF), vm((OB, NZ * OM), BF), vm((NZ * OM, OB), BF),
        vm((OM, 128), BF), vm((NZ, OM, 128), BF), vm((NX, NY, OB, 128), BF), vm((NX, NY, OB, 128), BF),
        vm((NX, NY, OB, 128), BF), vm((NY, OB, 128), BF), vm((NY, OB, 128), BF),
        vm((NZ, OM, 128), BF), vm((NZ, OM, 128), BF),
        dma((9,)), dma, dma, dma, dma, dma((NZ - 1,)), dma((NZ - 1,)), dma, dma,
        dma((NC,)), dma((NC,)), dma((8, H)), dma((8, H)), dma((OV + NX, H)), dma((OV + NX, H)),
        dma((8, H)), dma((8, H)), dma((NC,)), dma((NC,)), dma, dma,
        dma((NZ,)), dma((NZ,)), dma((NY,)), dma((NY,)), dma((NX, NY)), dma((NX, NY)), dma((NX,)), dma((NX,)),
        dma((NY,)), dma((NY,)), dma((NZ,)), dma((NZ,)),
    ]
    return pl.pallas_call(
        kernel,
        out_shape=(jax.ShapeDtypeStruct((OWN, D), BF), jax.ShapeDtypeStruct((OWN, D), BF)),
        in_specs=[pl.BlockSpec(memory_space=pl.ANY)] * 9,
        out_specs=(pl.BlockSpec(memory_space=vm), pl.BlockSpec(memory_space=vm)),
        scratch_shapes=scratch,
        compiler_params=pltpu.CompilerParams(
            collective_id=0, has_side_effects=True, vmem_limit_bytes=58 * 1024 * 1024
        ),
        cost_estimate=pl.CostEstimate(flops=4_000_000_000, bytes_accessed=8_000_000, transcendentals=300_000),
    )(q, kv.reshape(TOK, 128), wo.T, res, gain, ids.T, weights.T, w_in, w_out)


def solution(mesh):
    placed = (
        P("seq", "head"), P("seq", "head", None), P("head", None), P(("seq", "head"), None), P(),
        P("seq", None), P("seq", None), P("seq", None, "head"), P("seq", "head", None),
    )
    return jax.shard_map(
        per_device, mesh=mesh, in_specs=placed,
        out_specs=(P(("seq", "head"), None), P(("seq", "head"), None)), check_vma=False,
    )
```

```python
import jax
import jax.numpy as jnp
from jax import lax
from jax.experimental import pallas as pl
from jax.experimental.pallas import tpu as pltpu
from jax.sharding import PartitionSpec as P

MESH = pl.DeviceIdType.MESH
BF = jnp.bfloat16
F32 = jnp.float32
I32 = jnp.int32

NS, NZ = 64, 8
NC = NS // 2
TOK, OWN, TOP = 128, 16, 4
D, HALF, CH = 2880, 1440, 12
NX, NY = 4, 8
R = 4
CAP = R // 2
MSG = 48
GS, GR = 4, 16
NR = NC * R
H = 2
SB = NR // H
GH = SB // GR
FAR = 7
OV = 8
OM = 32
PIECES = ((0, 1536), (1536, D))
OB = CH * OWN

NEAR = sorted(
    [(dy, dx) for dy in range(-3, 5) for dx in range(-1, 3)], key=lambda o: (abs(o[0]) + abs(o[1]), o)
)
SEEN = [NEAR.index(((3 - dy) % NY - 3, (1 - dx) % NX - 1)) for dy, dx in NEAR]


def idiv(v, n):
    if n & (n - 1) == 0:
        return lax.shift_right_logical(v, jnp.full_like(v, n.bit_length() - 1))
    return ((v.astype(F32) + 0.5) * (1.0 / n)).astype(I32)


def imod(v, n):
    return v - idiv(v, n) * n


def iota(shape, dim):
    return lax.broadcasted_iota(I32, shape, dim)


def dot(a, b):
    return jnp.dot(a, b, preferred_element_type=F32)


def dot_nt(a, b):
    return lax.dot_general(a, b, (((1,), (1,)), ((), ())), preferred_element_type=F32)


def ones(cond):
    return jnp.where(cond, 1.0, 0.0).astype(BF)


def kernel(
    q_hbm, kv_hbm, wo_hbm, res_hbm, gain_hbm, ids_hbm, rw_hbm, win_hbm, wout_hbm,
    stream_ref, esum_ref,
    q_v, kv2, wo_v, res_v, gain_v, ids_v, rw_v, both, info2, win_v, wout_v,
    att_v, own_f, ps, rs, stage, xbuf, dm, cm, pm, pt,
    sb1, rb1, slots, low_own, low_oth, qs, racc, sb2, rb2, fin, fsend,
    om, co, p2, p2t, osend, oz, ox, obuf, ofar, oret, osel, oyr, ozs, ozr,
    load_sem, kv_ss, kv_rs, info_ss, info_rs, rs_ss, rs_rs, st_ss, st_rs,
    a1_ss, a1_rs, ag_ss, ag_rs, lo_ss, lo_rs, q_ss, q_rs, a2_ss, a2_rs, f_ss, f_rs,
    oz_ss, oz_rs, oy_ss, oy_rs, ox_ss, ox_rs, or_ss, or_rs, oyr_ss, oyr_rs, ozr_ss, ozr_rs,
):
    s = lax.axis_index("seq")
    z = lax.axis_index("head")
    p = lax.rem(s, 2)
    chip = lax.div(s, 2)
    x = lax.rem(chip, NX)
    y = lax.div(chip, NX)
    other = s + 1 - 2 * p
    nxt = lax.rem(s + 1, NS)
    prv = lax.rem(s + NS - 1, NS)
    up = lax.rem(z + 1, NZ)
    dn = lax.rem(z + NZ - 1, NZ)

    loads = [
        pltpu.make_async_copy(src, dst, load_sem.at[i])
        for i, (src, dst) in enumerate(
            [
                (kv_hbm, kv2.at[1]),
                (q_hbm, q_v),
                (ids_hbm, ids_v),
                (wo_hbm, wo_v),
                (res_hbm, res_v),
                (gain_hbm, gain_v),
                (win_hbm.at[0], win_v),
                (wout_hbm.at[0], wout_v),
                (rw_hbm, rw_v),
            ]
        )
    ]
    for c in loads:
        c.start()

    barrier = pltpu.get_barrier_semaphore()

    def greet(seq, head):
        pl.semaphore_signal(barrier, inc=1, device_id=(seq, head), device_id_type=MESH)

    greet(other, z)
    greet(prv, z)

    @pl.loop(1, NZ)
    def _(d):
        greet(s, lax.rem(z + d, NZ))

    @pl.loop(1, NC)
    def _(d):
        greet(lax.rem(chip + d, NC) * 2 + p, z)

    pl.semaphore_wait(barrier, 1 + 1 + (NZ - 1) + (NC - 1))

    def remote(src, dst, ss, rs_, seq, head):
        return pltpu.make_async_remote_copy(
            src_ref=src, dst_ref=dst, send_sem=ss, recv_sem=rs_,
            device_id=(seq, head), device_id_type=MESH,
        )

    loads[0].wait()
    kv_copy = remote(kv2.at[1], kv2.at[0], kv_ss, kv_rs, nxt, z)
    kv_copy.start()
    loads[2].wait()
    loads[8].wait()
    both[0:TOP] = ids_v[...].astype(F32)
    both[TOP:] = rw_v[...].astype(F32)
    chosen = ones(iota((OWN, TOK), 1) == iota((OWN, TOK), 0) + z * OWN)
    info2[p, :, 0:2 * TOP] = dot_nt(chosen, both[...].astype(BF))
    info_copy = remote(info2.at[p], info2.at[p], info_ss, info_rs, other, z)
    info_copy.start()
    def perm2(shape, a_dim):
        i, j = iota(shape, a_dim), iota(shape, 1 - a_dim)
        inner = imod(j, OM)
        return ones(
            (idiv(i, OWN) == idiv(inner, 2))
            & (idiv(imod(i, OWN), 2) == idiv(j, OM))
            & (imod(i, 2) == imod(inner, 2))
        )

    p2[...] = perm2((OB, NZ * OM), 0)
    p2t[...] = perm2((NZ * OM, OB), 1)

    def perm(shape, a_dim):
        i, j = iota(shape, a_dim), iota(shape, 1 - a_dim)
        inner = imod(j, MSG)
        return ones(
            (idiv(i, GR) == idiv(inner, R))
            & (idiv(imod(i, GR), R) == idiv(j, MSG))
            & (imod(i, R) == imod(inner, R))
            & (inner < CH * R)
        )

    pm[...] = perm((CH * GR, GS * MSG), 0)
    pt[...] = perm((GS * MSG, CH * GR), 1)
    loads[1].wait()
    kv_copy.wait_recv()

    kvf = kv2[...].reshape(2 * TOK, 128).astype(F32)
    lane = iota((2 * TOK, 128), 1)
    turned = pltpu.roll(kvf, 64, 1)
    k_even = jnp.where(lane < 64, kvf, 0.0).astype(BF)
    k_odd = jnp.where(lane >= 64, turned, 0.0).astype(BF)
    v_even = jnp.where(lane < 64, turned, 0.0).astype(BF)
    v_odd = jnp.where(lane >= 64, kvf, 0.0).astype(BF)
    qpos = iota((TOK, 2 * TOK), 0)
    kpos = iota((TOK, 2 * TOK), 1)
    allowed = (kpos > qpos) & (kpos <= qpos + TOK) & (s * TOK - TOK + kpos >= 0)
    for pair in range(4):
        qp = q_v[:, 128 * pair:128 * (pair + 1)]
        acc = None
        for kk, vv in ((k_even, v_even), (k_odd, v_odd)):
            sc = jnp.where(allowed, dot_nt(qp, kk) * 0.125, -1e30)
            ex = jnp.exp(sc - jnp.max(sc, axis=-1, keepdims=True))
            w = (ex / jnp.sum(ex, axis=-1, keepdims=True)).astype(BF)
            part = dot(w, vv)
            acc = part if acc is None else acc + part
        att_v[:, 128 * pair:128 * (pair + 1)] = acc.astype(BF)

    far_from = 3 + 3 * p
    far_to = lax.rem(z + 1 + (NZ - 2) * p, NZ)
    far_back = lax.rem(z + NZ - 1 + 2 * p, NZ)

    def h_copy(slot_at, dst, c, head):
        lo, hi = PIECES[c]
        return remote(
            ps.at[slot_at, :, lo:hi], rs.at[dst, :, lo:hi], rs_ss.at[slot_at, c], rs_rs.at[dst, c], s, head
        )

    def block(d, c):
        lo, hi = PIECES[c]
        return own_f[lax.rem(z + d + NZ, NZ), :, lo:hi]

    def got_h(dst, c):
        lo, hi = PIECES[c]
        h_copy(FAR, dst, c, up).wait_recv()
        return rs[dst, :, lo:hi].astype(F32)

    def send_h(slot_at, dst, c, head, value):
        lo, hi = PIECES[c]
        ps[slot_at, :, lo:hi] = value.astype(BF)
        h_copy(slot_at, dst, c, head).start()

    loads[3].wait()
    for c, (lo, hi) in enumerate(PIECES):
        for n0 in range(lo, hi, 512):
            n1 = min(hi, n0 + 512)
            own_f[:, :, n0:n1] = dot_nt(att_v[...], wo_v[n0:n1]).reshape(NZ, OWN, n1 - n0)
        send_h(FAR, FAR, c, far_back, block(4, c))

    info_copy.wait_recv()
    inf = info2[...].reshape(2 * OWN, 128)
    lanes = iota((2 * OWN, 128), 1).astype(F32)
    named = jnp.zeros((2 * OWN, 128), F32)
    weight = jnp.zeros((2 * OWN, 128), F32)
    for k in range(TOP):
        hit = inf[:, k:k + 1] == lanes
        named = named + jnp.where(hit, 1.0, 0.0)
        weight = weight + jnp.where(hit, inf[:, TOP + k:TOP + k + 1], 0.0)
    named, weight = named.astype(BF), weight.astype(BF)
    ta, tb = iota((2 * OWN, 2 * OWN), 0), iota((2 * OWN, 2 * OWN), 1)
    before = ones((tb < ta) & (idiv(tb, OWN) == idiv(ta, OWN)))
    slot = dot(before, named).astype(BF)
    ra = iota((NC * R, 128), 0)
    expand = ones(idiv(ra, R) == iota((NC * R, 128), 1))

    for c in range(2):
        got = got_h(FAR, c)
        send_h(3, 2, c, dn, block(-3, c) + jnp.where(p == 0, got, 0.0))
        send_h(6, 5, c, up, block(3, c) + jnp.where(p == 0, 0.0, got))

    r_i = imod(iota((NC * R, 2 * OWN), 0), R)
    t_i = iota((NC * R, 2 * OWN), 1)
    want = r_i - idiv(r_i, CAP) * CAP
    picked = (
        (dot_nt(expand, named) > 0.5)
        & (dot_nt(expand, slot) == want.astype(F32))
        & (idiv(t_i, OWN) == idiv(r_i, CAP))
    )
    spread = ones(iota((2 * OWN, CH * 2 * OWN), 0) == imod(iota((2 * OWN, CH * 2 * OWN), 1), 2 * OWN))
    wide = dot(ones(picked), spread).astype(BF)
    m_i = iota((NC * MSG, NC * R), 0)
    rest = imod(m_i, MSG)
    rows_of = ones(
        (idiv(m_i, MSG) * R + imod(rest, R) == iota((NC * MSG, NC * R), 1)) & (rest < CH * R)
    )
    mm = iota((MSG, CH * 2 * OWN), 0)
    chunk_ok = jnp.where(idiv(mm, R) == idiv(iota((MSG, CH * 2 * OWN), 1), 2 * OWN), 1.0, 0.0)
    full = dot(rows_of, wide).reshape(NC, MSG, CH * 2 * OWN) * chunk_ok[None]
    dm[...] = full.reshape(NC * MSG, CH * 2 * OWN).astype(BF)


    for c in range(2):
        send_h(2, 1, c, dn, block(-2, c) + got_h(2, c))
        send_h(5, 4, c, up, block(2, c) + got_h(5, c))

    third = jnp.where((named > 0.5) & (slot > 1.5), 1.0, 0.0)
    third_row = dot_nt(jnp.ones((8, 128), BF), third.astype(BF))[0:1]
    third_wide = dot(jnp.broadcast_to(third_row, (8, 2 * OWN)).astype(BF), spread)[0:1]
    o_m, o_q = iota((OM, CH * 2 * OWN), 0), iota((OM, CH * 2 * OWN), 1)
    o_ok = (idiv(o_m, 2) == idiv(o_q, 2 * OWN)) & (imod(o_m, 2) == imod(idiv(o_q, OWN), 2))
    om[...] = jnp.where(o_ok, third_wide, 0.0).astype(BF)
    hot = jnp.max(third, axis=0, keepdims=True)
    e_row = iota((1, 128), 1)
    hot_x = jnp.sum(hot * imod(e_row, NX).astype(F32), axis=1, keepdims=True)
    hot_y = jnp.sum(hot * idiv(e_row, NX).astype(F32), axis=1, keepdims=True)


    for c in range(2):
        send_h(1, 0, c, dn, block(-1, c) + got_h(1, c))
        send_h(4, 3, c, up, block(1, c) + got_h(4, c))

    loads[4].wait()
    loads[5].wait()
    total = jnp.concatenate([block(0, c) + (got_h(0, c) + got_h(3, c)) for c in range(2)], axis=1)
    total = total + res_v[...].astype(F32)
    stream_ref[...] = total.astype(BF)
    mean_square = jnp.mean(total * total, axis=-1, keepdims=True)
    normed = (total * lax.rsqrt(mean_square + 1e-5) * gain_v[...].reshape(1, D)).astype(BF)
    for h in range(2):
        for c in range(CH):
            lo = h * HALF + c * 128
            hi = min(lo + 128, (h + 1) * HALF)
            piece = normed[:, lo:hi]
            if hi - lo < 128:
                piece = jnp.concatenate([piece, jnp.zeros((OWN, 128 - hi + lo), BF)], axis=1)
            stage[h, c] = piece
    mine = pl.ds(pl.multiple_of(p * OWN, OWN), OWN)
    st_copy = remote(stage.at[1 - p], xbuf.at[:, mine, :], st_ss, st_rs, other, z)
    st_copy.start()
    xbuf[:, mine, :] = stage[p]
    st_copy.wait_recv()

    osend[...] = dot(om[...], xbuf[...].reshape(CH * 2 * OWN, 128)).astype(BF)

    def oz_copy(d):
        return remote(osend, oz.at[z], oz_ss.at[d - 1], oz_rs.at[z], s, lax.rem(z + d, NZ))

    for d in range(1, NZ):
        oz_copy(d).start()
    oz[z] = osend[...]

    def at(y_, x_):
        return (y_ * NX + x_) * 2 + p

    msgs = dot(dm[...], xbuf[...].reshape(CH * 2 * OWN, 128)).astype(BF)
    sb1[...] = msgs.reshape(NC, MSG, 128)

    def near(r):
        dy, dx = NEAR[r]
        return lax.rem(y + dy + NY, NY) * NX + lax.rem(x + dx + NX, NX)

    def a1_copy(r):
        to = near(r)
        return remote(sb1.at[to], rb1.at[SEEN[r]], a1_ss.at[r], a1_rs.at[SEEN[r]], to * 2 + p, z)

    for r in range(1, NC):
        a1_copy(r).start()
    rb1[0] = sb1[chip]

    e_l = iota((2 * OWN, NC * R), 1)
    r_l = imod(e_l, R)
    back = ones(iota((128, NC * R), 0) == idiv(iota((128, NC * R), 1), R))
    take = (dot(slot, back) == (r_l - idiv(r_l, CAP) * CAP).astype(F32)) & (
        idiv(iota((2 * OWN, NC * R), 0), OWN) == idiv(r_l, CAP)
    )
    w_t = jnp.where(take, dot(weight, back), 0.0).astype(BF)
    spread_t = ones(iota((CH * 2 * OWN, 2 * OWN), 1) == imod(iota((CH * 2 * OWN, 2 * OWN), 0), 2 * OWN))
    tall = dot(spread_t, w_t).astype(BF)
    m_l = iota((NC * R, NC * MSG), 1)
    rest_l = imod(m_l, MSG)
    cols_of = ones(
        (idiv(m_l, MSG) * R + imod(rest_l, R) == iota((NC * R, NC * MSG), 0)) & (rest_l < CH * R)
    )
    full_t = dot(tall, cols_of)
    c_l = idiv(imod(iota((CH * 2 * OWN, NC * MSG), 1), MSG), R)
    w_third = jnp.sum(third * weight.astype(F32), axis=1, keepdims=True)
    w_tall = dot(spread_t, jnp.broadcast_to(w_third, (2 * OWN, 128)).astype(BF))[:, :OM]
    o_q, o_m = iota((CH * 2 * OWN, OM), 0), iota((CH * 2 * OWN, OM), 1)
    o_ok = (idiv(o_m, 2) == idiv(o_q, 2 * OWN)) & (imod(o_m, 2) == imod(idiv(o_q, OWN), 2))
    co[...] = jnp.where(o_ok, w_tall, 0.0).astype(BF)
    cm[...] = jnp.where(c_l == idiv(iota((CH * 2 * OWN, NC * MSG), 0), 2 * OWN), full_t, 0.0).astype(BF)

    def a1_wait(r):
        if r:
            a1_copy(SEEN[r]).wait_recv()

    def rows(h):
        return pl.ds(h * SB, SB)

    def ag_copy(src, dst, h, head):
        return remote(
            slots.at[src, rows(h)], slots.at[dst, rows(h)],
            ag_ss.at[dst, h], ag_rs.at[dst, h], s, head,
        )

    def lo_copy(slot_at, h):
        return remote(
            low_own.at[slot_at, rows(h)], low_oth.at[slot_at, rows(h)],
            lo_ss.at[slot_at, h], lo_rs.at[slot_at, h], other, z,
        )

    def low(slot_at, h):
        low_own[slot_at, rows(h)] = dot(slots[slot_at, rows(h)], win_v[...]).astype(BF)
        lo_copy(slot_at, h).start()

    for h in range(H):
        for g in range(h * GH, (h + 1) * GH):
            for i in range(GS):
                a1_wait(g * GS + i)
            got = dot(pm[...], rb1[GS * g:GS * (g + 1)].reshape(GS * MSG, 128)).astype(BF)
            for c in range(CH):
                width = min(128, HALF - 128 * c)
                slots[0, GR * g:GR * (g + 1), 128 * c:128 * c + width] = got[GR * c:GR * (c + 1), :width]
        ag_copy(0, 1, h, up).start()
        ag_copy(0, 4, h, dn).start()
    for d in range(1, NZ):
        from_z = lax.rem(z + d, NZ)
        remote(osend, oz.at[from_z], oz_ss.at[d - 1], oz_rs.at[from_z], s, from_z).wait_recv()
    ox[x, y] = dot(p2[...], oz[...].reshape(NZ * OM, 128)).astype(BF)

    def oy_copy(d):
        to = lax.rem(y + d, NY)
        return remote(ox.at[x, y], ox.at[x, y], oy_ss.at[d - 1], oy_rs.at[y], at(to, x), z)

    for d in range(1, NY):
        oy_copy(d).start()

    loads[6].wait()
    for h in range(H):
        low(0, h)

    right, left = lax.rem(x + 1, NX), lax.rem(x + NX - 1, NX)

    def ox_copy(way, from_x, from_y):
        return remote(
            ox.at[from_x, from_y], ox.at[from_x, from_y], ox_ss.at[way, from_y], ox_rs.at[from_x, from_y],
            at(y, right if way in (0, 2) else left), z,
        )

    def ox_send(dy):
        from_y = lax.rem(y + dy, NY)
        if dy:
            remote(
                ox.at[x, from_y], ox.at[x, from_y], ox_ss.at[0, from_y], oy_rs.at[from_y], at(from_y, x), z
            ).wait_recv()
        ox_copy(0, x, from_y).start()
        ox_copy(1, x, from_y).start()

    def ox_take(d):
        from_x = lax.rem(x + d, NX)
        if d:
            for from_y in range(NY):
                ox_copy(0, from_x, from_y).wait_recv()
                if d == 3 and from_y < 4:
                    ox_copy(2, left, from_y).start()
                if d == 1 and from_y >= 4:
                    ox_copy(3, right, from_y).start()
        for c in range(CH):
            width = min(128, HALF - 128 * c)
            piece = ox[from_x, :, OWN * c:OWN * (c + 1), :].reshape(NR, 128)
            slots[OV + d, :, 128 * c:128 * c + width] = piece[:, :width]
        for h in range(H):
            low(OV + d, h)

    ox_send(0)
    aside = {
        (1, 0): (lambda: (ox_send(1), ox_send(7))),
        (1, 1): (lambda: (ox_send(2), ox_send(6))),
        (2, 0): (lambda: (ox_send(3), ox_send(5), ox_send(4))),
        (2, 1): (lambda: ox_take(0)),
        (3, 0): (lambda: ox_take(3)),
        (3, 1): (lambda: ox_take(1)),
    }
    for k in (1, 2, 3):
        for h in range(H):
            ag_copy(0, k, h, up).wait_recv()
            if k < 3:
                ag_copy(k, k + 1, h, up).start()
            ag_copy(0, k + 3, h, dn).wait_recv()
            if k < 3:
                ag_copy(k + 3, k + 4, h, dn).start()
            else:
                ag_copy(far_from, FAR, h, far_to).start()
            low(k, h)
            low(k + 3, h)
            aside[k, h]()
    loads[7].wait()
    for h in range(H):
        ag_copy(far_from, FAR, h, far_to).wait_recv()
        low(FAR, h)

    def expert(slot_at, h):
        lo_copy(slot_at, h).wait_recv()
        inner = low_own[slot_at, rows(h)].astype(F32) + low_oth[slot_at, rows(h)].astype(F32)
        gate, upv = inner[:, :192], inner[:, 192:]
        active = ((upv + 1.0) * gate * jax.nn.sigmoid(1.702 * gate)).astype(BF)
        return dot(active, wout_v[...])

    def q_copy(slot_at, dst, h, head):
        return remote(
            qs.at[slot_at, rows(h)], racc.at[dst, rows(h)],
            q_ss.at[slot_at, h], q_rs.at[dst, h], s, head,
        )

    for h in range(H):
        qs[FAR, rows(h)] = expert(FAR, h).astype(BF)
        q_copy(FAR, FAR, h, far_back).start()
    ox_take(2)
    for h in range(H):
        below, above = expert(3, h), expert(6, h)
        q_copy(FAR, FAR, h, far_back).wait_recv()
        got = racc[FAR, rows(h)].astype(F32)
        qs[3, rows(h)] = (below + jnp.where(p == 0, got, 0.0)).astype(BF)
        q_copy(3, 2, h, dn).start()
        qs[6, rows(h)] = (above + jnp.where(p == 0, 0.0, got)).astype(BF)
        q_copy(6, 5, h, up).start()

    def of_copy(way):
        part = slice(0, 4) if way == 0 else slice(4, 8)
        return remote(
            obuf.at[2, part], ofar.at[part], or_ss.at[way], or_rs.at[way], at(y, left if way == 0 else right), z
        )

    def or_copy(way):
        return remote(
            obuf.at[3 - 2 * way], oret.at[way], or_ss.at[2 + way], or_rs.at[2 + way],
            at(y, left if way == 0 else right), z,
        )

    def oyr_copy(d):
        to = lax.rem(y + d, NY)
        return remote(osel.at[to], oyr.at[y], oyr_ss.at[d - 1], oyr_rs.at[y], at(to, x), z)

    def ozr_copy(d):
        to = lax.rem(z + d, NZ)
        return remote(ozs.at[to], ozr.at[z], ozr_ss.at[d - 1], ozr_rs.at[z], s, to)

    here = hot_x == x.astype(F32)

    def ov_expert(d):
        for h in range(H):
            value = expert(OV + d, h).astype(BF)
            n = SB // OWN
            for c in range(CH):
                piece = value[:, 128 * c:128 * (c + 1)]
                if piece.shape[1] < 128:
                    piece = jnp.concatenate([piece, jnp.zeros((SB, 128 * CH - HALF), BF)], axis=1)
                obuf[d, n * h:n * (h + 1), OWN * c:OWN * (c + 1), :] = piece.reshape(n, OWN, 128)

    def ov_far():
        ov_expert(2)
        for way in range(2):
            of_copy(way).start()

    def ov_near():
        for way in range(2):
            ov_expert(3 - 2 * way)
        for way in range(2):
            of_copy(way).wait_recv()
            for to_y in range(4 * way, 4 * way + 4):
                mixed = jnp.where(here, obuf[3 - 2 * way, to_y].astype(F32), ofar[to_y].astype(F32))
                obuf[3 - 2 * way, to_y] = mixed.astype(BF)
            or_copy(way).start()
        ov_expert(0)

    def ov_back_y():
        for way in range(2):
            or_copy(way).wait_recv()
        for to_y in range(NY):
            pass_by = 0 if to_y < 4 else 1
            acc = oret[pass_by, to_y].astype(F32)
            neighbour = left if to_y < 4 else right
            acc = jnp.where(hot_x == neighbour.astype(F32), oret[1 - pass_by, to_y].astype(F32), acc)
            osel[to_y] = jnp.where(here, obuf[0, to_y].astype(F32), acc).astype(BF)
        for d in range(1, NY):
            oyr_copy(d).start()

    def ov_back_z():
        acc = jnp.where(hot_y == y.astype(F32), osel[y].astype(F32), 0.0)
        for d in range(1, NY):
            from_y = lax.rem(y + d, NY)
            remote(osel.at[from_y], oyr.at[from_y], oyr_ss.at[d - 1], oyr_rs.at[from_y], at(from_y, x), z).wait_recv()
            acc = jnp.where(hot_y == from_y.astype(F32), oyr[from_y].astype(F32), acc)
        ozs[...] = dot(p2t[...], acc.astype(BF)).astype(BF).reshape(NZ, OM, 128)
        for d in range(1, NZ):
            ozr_copy(d).start()
        ozr[z] = ozs[z]

    ov_far()
    for k in (2, 1):
        for h in range(H):
            below, above = expert(k, h), expert(k + 3, h)
            q_copy(k, k, h, dn).wait_recv()
            qs[k, rows(h)] = (below + racc[k, rows(h)].astype(F32)).astype(BF)
            q_copy(k, k - 1, h, dn).start()
            q_copy(k + 3, k + 3, h, up).wait_recv()
            qs[k + 3, rows(h)] = (above + racc[k + 3, rows(h)].astype(F32)).astype(BF)
            q_copy(k + 3, k + 2, h, up).start()
        if k == 2:
            ov_near()
        else:
            ov_back_y()

    def a2_copy(r):
        to = near(r)
        return remote(sb2.at[r], rb2.at[chip], a2_ss.at[r], a2_rs.at[chip], to * 2 + p, z)

    for h in range(H):
        value = expert(0, h)
        q_copy(0, 0, h, dn).wait_recv()
        q_copy(0, 3, h, up).wait_recv()
        value = (value + racc[0, rows(h)].astype(F32) + racc[3, rows(h)].astype(F32)).astype(BF)
        for i in range(GH):
            g = h * GH + i
            part = value[GR * i:GR * (i + 1)]
            pieces = [part[:, 128 * c:128 * (c + 1)] for c in range(CH - 1)]
            last = part[:, 128 * (CH - 1):]
            pieces.append(jnp.concatenate([last, jnp.zeros((GR, 128 * CH - HALF), BF)], axis=1))
            out = dot(pt[...], jnp.concatenate(pieces, axis=0)).astype(BF)
            sb2[GS * g:GS * (g + 1)] = out.reshape(GS, MSG, 128)
            for r in range(GS * g, GS * (g + 1)):
                if r:
                    a2_copy(r).start()

    ov_back_z()
    rb2[chip] = sb2[0]
    for d in range(1, NZ):
        from_z = lax.rem(z + d, NZ)
        remote(ozs.at[from_z], ozr.at[from_z], ozr_ss.at[d - 1], ozr_rs.at[from_z], s, from_z).wait_recv()
    third_sum = jnp.sum(ozr[...].astype(F32), axis=0).astype(BF)

    @pl.loop(0, NC)
    def _(src):
        @pl.when(src != chip)
        def _():
            remote(sb2.at[src], rb2.at[src], a2_ss.at[0], a2_rs.at[src], src * 2 + p, z).wait_recv()

    out = dot(cm[...], rb2[...].reshape(NC * MSG, 128)) + dot(co[...], third_sum)
    out = out.astype(BF).reshape(CH, 2 * OWN, 128)
    cm_out = xbuf
    cm_out[...] = out
    theirs = pl.ds(pl.multiple_of((1 - p) * OWN, OWN), OWN)
    fsend[...] = cm_out[:, theirs, :]
    f_copy = remote(fsend, fin.at[p], f_ss, f_rs, other, z)
    f_copy.start()
    fin[p] = cm_out[:, mine, :]
    f_copy.wait_recv()
    esum_ref[...] = jnp.concatenate(
        [fin[h, c][:, :min(128, HALF - 128 * c)] for h in range(2) for c in range(CH)], axis=1
    )

    kv_copy.wait_send()
    info_copy.wait_send()
    st_copy.wait_send()
    f_copy.wait_send()
    for d in range(1, NZ):
        oz_copy(d).wait_send()
        oy_copy(d).wait_send()
        oyr_copy(d).wait_send()
        ozr_copy(d).wait_send()
        for c in range(2):
            h_copy(d, d, c, up).wait_send()
    for way in range(2):
        of_copy(way).wait_send()
        or_copy(way).wait_send()
    for from_y in range(NY):
        ox_copy(0, x, from_y).wait_send()
        ox_copy(1, x, from_y).wait_send()
        ox_copy(2 if from_y < 4 else 3, x, from_y).wait_send()
    for r in range(1, NC):
        a1_copy(r).wait_send()
        a2_copy(r).wait_send()

    for slot_at in range(OV + NX):
        for h in range(H):
            lo_copy(slot_at, h).wait_send()
            if 0 < slot_at < OV:
                ag_copy(0, slot_at, h, up).wait_send()
                q_copy(slot_at, slot_at, h, up).wait_send()


def per_device(q, kv, wo, res, gain, ids, weights, w_in, w_out):
    vm = pltpu.VMEM
    dma = pltpu.SemaphoreType.DMA
    scratch = [
        vm((TOK, 512), BF), vm((2, TOK, 128), BF), vm((D, 512), BF), vm((OWN, D), BF), vm((D,), F32),
        vm((TOP, TOK), I32), vm((TOP, TOK), BF), vm((2 * TOP, TOK), F32), vm((2, OWN, 128), F32), vm((HALF, 384), BF), vm((192, HALF), BF),
        vm((TOK, 512), BF), vm((NZ, OWN, D), F32), vm((NZ, OWN, D), BF), vm((NZ, OWN, D), BF),
        vm((2, CH, OWN, 128), BF), vm((CH, 2 * OWN, 128), BF),
        vm((NC * MSG, CH * 2 * OWN), BF), vm((CH * 2 * OWN, NC * MSG), BF),
        vm((CH * GR, GS * MSG), BF), vm((GS * MSG, CH * GR), BF),
        vm((NC, MSG, 128), BF), vm((NC, MSG, 128), BF),
        vm((OV + NX, NR, HALF), BF), vm((OV + NX, NR, 384), BF), vm((OV + NX, NR, 384), BF),
        vm((8, NR, HALF), BF), vm((8, NR, HALF), BF),
        vm((NC, MSG, 128), BF), vm((NC, MSG, 128), BF),
        vm((2, CH, OWN, 128), BF), vm((CH, OWN, 128), BF),
        vm((OM, CH * 2 * OWN), BF), vm((CH * 2 * OWN, OM), BF), vm((OB, NZ * OM), BF), vm((NZ * OM, OB), BF),
        vm((OM, 128), BF), vm((NZ, OM, 128), BF), vm((NX, NY, OB, 128), BF), vm((NX, NY, OB, 128), BF),
        vm((NY, OB, 128), BF), vm((2, NY, OB, 128), BF), vm((NY, OB, 128), BF), vm((NY, OB, 128), BF),
        vm((NZ, OM, 128), BF), vm((NZ, OM, 128), BF),
        dma((9,)), dma, dma, dma, dma, dma((NZ, 2)), dma((NZ, 2)), dma, dma,
        dma((NC,)), dma((NC,)), dma((8, H)), dma((8, H)), dma((OV + NX, H)), dma((OV + NX, H)),
        dma((8, H)), dma((8, H)), dma((NC,)), dma((NC,)), dma, dma,
        dma((NZ,)), dma((NZ,)), dma((NY,)), dma((NY,)), dma((NX, NY)), dma((NX, NY)), dma((NX,)), dma((NX,)),
        dma((NY,)), dma((NY,)), dma((NZ,)), dma((NZ,)),
    ]
    return pl.pallas_call(
        kernel,
        out_shape=(jax.ShapeDtypeStruct((OWN, D), BF), jax.ShapeDtypeStruct((OWN, D), BF)),
        in_specs=[pl.BlockSpec(memory_space=pl.ANY)] * 9,
        out_specs=(pl.BlockSpec(memory_space=vm), pl.BlockSpec(memory_space=vm)),
        scratch_shapes=scratch,
        compiler_params=pltpu.CompilerParams(
            collective_id=0, has_side_effects=True, vmem_limit_bytes=58 * 1024 * 1024
        ),
        cost_estimate=pl.CostEstimate(flops=4_000_000_000, bytes_accessed=8_000_000, transcendentals=300_000),
    )(q, kv.reshape(TOK, 128), wo.T, res, gain, ids.T, weights.T, w_in, w_out)


def solution(mesh):
    placed = (
        P("seq", "head"), P("seq", "head", None), P("head", None), P(("seq", "head"), None), P(),
        P("seq", None), P("seq", None), P("seq", None, "head"), P("seq", "head", None),
    )
    return jax.shard_map(
        per_device, mesh=mesh, in_specs=placed,
        out_specs=(P(("seq", "head"), None), P(("seq", "head"), None)), check_vma=False,
    )
```

```python
import jax
import jax.numpy as jnp
from jax import lax
from jax.experimental import pallas as pl
from jax.experimental.pallas import tpu as pltpu
from jax.sharding import PartitionSpec as P

MESH = pl.DeviceIdType.MESH
BF = jnp.bfloat16
F32 = jnp.float32
I32 = jnp.int32

NS, NZ = 64, 8
NC = NS // 2
TOK, OWN, TOP = 128, 16, 4
D, HALF, CH = 2880, 1440, 12
NX, NY = 4, 8
R = 4
CAP = R // 2
MSG = 48
GS, GR = 4, 16
NR = NC * R
H = 4
SB = NR // H
GH = SB // GR
FAR = 7
OV = 8
OM = 32
PIECES = ((0, 1536), (1536, D))
OB = CH * OWN

NEAR = sorted(
    [(dy, dx) for dy in range(-3, 5) for dx in range(-1, 3)], key=lambda o: (abs(o[0]) + abs(o[1]), o)
)
SEEN = [NEAR.index(((3 - dy) % NY - 3, (1 - dx) % NX - 1)) for dy, dx in NEAR]


def idiv(v, n):
    if n & (n - 1) == 0:
        return lax.shift_right_logical(v, jnp.full_like(v, n.bit_length() - 1))
    return ((v.astype(F32) + 0.5) * (1.0 / n)).astype(I32)


def imod(v, n):
    return v - idiv(v, n) * n


def iota(shape, dim):
    return lax.broadcasted_iota(I32, shape, dim)


def dot(a, b):
    return jnp.dot(a, b, preferred_element_type=F32)


def dot_nt(a, b):
    return lax.dot_general(a, b, (((1,), (1,)), ((), ())), preferred_element_type=F32)


def ones(cond):
    return jnp.where(cond, 1.0, 0.0).astype(BF)


def kernel(
    q_hbm, kv_hbm, wo_hbm, res_hbm, gain_hbm, ids_hbm, rw_hbm, win_hbm, wout_hbm,
    stream_ref, esum_ref,
    q_v, kv2, wo_v, res_v, gain_v, ids_v, rw_v, both, info2, win_v, wout_v,
    att_v, own_f, ps, rs, stage, xbuf, dm, cm, pm, pt,
    sb1, rb1, slots, low_own, low_oth, qs, racc, sb2, rb2, fin, fsend,
    om, co, p2, p2t, osend, oz, ox, obuf, ofar, oret, osel, oyr, ozs, ozr,
    load_sem, kv_ss, kv_rs, info_ss, info_rs, rs_ss, rs_rs, st_ss, st_rs,
    a1_ss, a1_rs, ag_ss, ag_rs, lo_ss, lo_rs, q_ss, q_rs, a2_ss, a2_rs, f_ss, f_rs,
    oz_ss, oz_rs, oy_ss, oy_rs, ox_ss, ox_rs, or_ss, or_rs, oyr_ss, oyr_rs, ozr_ss, ozr_rs,
):
    s = lax.axis_index("seq")
    z = lax.axis_index("head")
    p = lax.rem(s, 2)
    chip = lax.div(s, 2)
    x = lax.rem(chip, NX)
    y = lax.div(chip, NX)
    other = s + 1 - 2 * p
    nxt = lax.rem(s + 1, NS)
    prv = lax.rem(s + NS - 1, NS)
    up = lax.rem(z + 1, NZ)
    dn = lax.rem(z + NZ - 1, NZ)

    loads = [
        pltpu.make_async_copy(src, dst, load_sem.at[i])
        for i, (src, dst) in enumerate(
            [
                (kv_hbm, kv2.at[1]),
                (q_hbm, q_v),
                (ids_hbm, ids_v),
                (wo_hbm, wo_v),
                (res_hbm, res_v),
                (gain_hbm, gain_v),
                (win_hbm.at[0], win_v),
                (wout_hbm.at[0], wout_v),
                (rw_hbm, rw_v),
            ]
        )
    ]
    for c in loads:
        c.start()

    barrier = pltpu.get_barrier_semaphore()

    def greet(seq, head):
        pl.semaphore_signal(barrier, inc=1, device_id=(seq, head), device_id_type=MESH)

    greet(other, z)
    greet(prv, z)

    @pl.loop(1, NZ)
    def _(d):
        greet(s, lax.rem(z + d, NZ))

    @pl.loop(1, NC)
    def _(d):
        greet(lax.rem(chip + d, NC) * 2 + p, z)

    pl.semaphore_wait(barrier, 1 + 1 + (NZ - 1) + (NC - 1))

    def remote(src, dst, ss, rs_, seq, head):
        return pltpu.make_async_remote_copy(
            src_ref=src, dst_ref=dst, send_sem=ss, recv_sem=rs_,
            device_id=(seq, head), device_id_type=MESH,
        )

    loads[0].wait()
    kv_copy = remote(kv2.at[1], kv2.at[0], kv_ss, kv_rs, nxt, z)
    kv_copy.start()
    loads[2].wait()
    loads[8].wait()
    both[0:TOP] = ids_v[...].astype(F32)
    both[TOP:] = rw_v[...].astype(F32)
    chosen = ones(iota((OWN, TOK), 1) == iota((OWN, TOK), 0) + z * OWN)
    info2[p, :, 0:2 * TOP] = dot_nt(chosen, both[...].astype(BF))
    info_copy = remote(info2.at[p], info2.at[p], info_ss, info_rs, other, z)
    info_copy.start()
    def perm2(shape, a_dim):
        i, j = iota(shape, a_dim), iota(shape, 1 - a_dim)
        inner = imod(j, OM)
        return ones(
            (idiv(i, OWN) == idiv(inner, 2))
            & (idiv(imod(i, OWN), 2) == idiv(j, OM))
            & (imod(i, 2) == imod(inner, 2))
        )

    p2[...] = perm2((OB, NZ * OM), 0)
    p2t[...] = perm2((NZ * OM, OB), 1)

    def perm(shape, a_dim):
        i, j = iota(shape, a_dim), iota(shape, 1 - a_dim)
        inner = imod(j, MSG)
        return ones(
            (idiv(i, GR) == idiv(inner, R))
            & (idiv(imod(i, GR), R) == idiv(j, MSG))
            & (imod(i, R) == imod(inner, R))
            & (inner < CH * R)
        )

    pm[...] = perm((CH * GR, GS * MSG), 0)
    pt[...] = perm((GS * MSG, CH * GR), 1)
    loads[1].wait()
    kv_copy.wait_recv()

    kvf = kv2[...].reshape(2 * TOK, 128).astype(F32)
    lane = iota((2 * TOK, 128), 1)
    turned = pltpu.roll(kvf, 64, 1)
    k_even = jnp.where(lane < 64, kvf, 0.0).astype(BF)
    k_odd = jnp.where(lane >= 64, turned, 0.0).astype(BF)
    v_even = jnp.where(lane < 64, turned, 0.0).astype(BF)
    v_odd = jnp.where(lane >= 64, kvf, 0.0).astype(BF)
    qpos = iota((TOK, 2 * TOK), 0)
    kpos = iota((TOK, 2 * TOK), 1)
    allowed = (kpos > qpos) & (kpos <= qpos + TOK) & (s * TOK - TOK + kpos >= 0)
    for pair in range(4):
        qp = q_v[:, 128 * pair:128 * (pair + 1)]
        acc = None
        for kk, vv in ((k_even, v_even), (k_odd, v_odd)):
            sc = jnp.where(allowed, dot_nt(qp, kk) * 0.125, -1e30)
            ex = jnp.exp(sc - jnp.max(sc, axis=-1, keepdims=True))
            w = (ex / jnp.sum(ex, axis=-1, keepdims=True)).astype(BF)
            part = dot(w, vv)
            acc = part if acc is None else acc + part
        att_v[:, 128 * pair:128 * (pair + 1)] = acc.astype(BF)

    far_from = 3 + 3 * p
    far_to = lax.rem(z + 1 + (NZ - 2) * p, NZ)
    far_back = lax.rem(z + NZ - 1 + 2 * p, NZ)

    def h_copy(slot_at, dst, c, head):
        lo, hi = PIECES[c]
        return remote(
            ps.at[slot_at, :, lo:hi], rs.at[dst, :, lo:hi], rs_ss.at[slot_at, c], rs_rs.at[dst, c], s, head
        )

    def block(d, c):
        lo, hi = PIECES[c]
        return own_f[lax.rem(z + d + NZ, NZ), :, lo:hi]

    def got_h(dst, c):
        lo, hi = PIECES[c]
        h_copy(FAR, dst, c, up).wait_recv()
        return rs[dst, :, lo:hi].astype(F32)

    def send_h(slot_at, dst, c, head, value):
        lo, hi = PIECES[c]
        ps[slot_at, :, lo:hi] = value.astype(BF)
        h_copy(slot_at, dst, c, head).start()

    loads[3].wait()
    for c, (lo, hi) in enumerate(PIECES):
        for n0 in range(lo, hi, 512):
            n1 = min(hi, n0 + 512)
            own_f[:, :, n0:n1] = dot_nt(att_v[...], wo_v[n0:n1]).reshape(NZ, OWN, n1 - n0)
        send_h(FAR, FAR, c, far_back, block(4, c))

    info_copy.wait_recv()
    inf = info2[...].reshape(2 * OWN, 128)
    lanes = iota((2 * OWN, 128), 1).astype(F32)
    named = jnp.zeros((2 * OWN, 128), F32)
    weight = jnp.zeros((2 * OWN, 128), F32)
    for k in range(TOP):
        hit = inf[:, k:k + 1] == lanes
        named = named + jnp.where(hit, 1.0, 0.0)
        weight = weight + jnp.where(hit, inf[:, TOP + k:TOP + k + 1], 0.0)
    named, weight = named.astype(BF), weight.astype(BF)
    ta, tb = iota((2 * OWN, 2 * OWN), 0), iota((2 * OWN, 2 * OWN), 1)
    before = ones((tb < ta) & (idiv(tb, OWN) == idiv(ta, OWN)))
    slot = dot(before, named).astype(BF)
    ra = iota((NC * R, 128), 0)
    expand = ones(idiv(ra, R) == iota((NC * R, 128), 1))

    for c in range(2):
        got = got_h(FAR, c)
        send_h(3, 2, c, dn, block(-3, c) + jnp.where(p == 0, got, 0.0))
        send_h(6, 5, c, up, block(3, c) + jnp.where(p == 0, 0.0, got))

    r_i = imod(iota((NC * R, 2 * OWN), 0), R)
    t_i = iota((NC * R, 2 * OWN), 1)
    want = r_i - idiv(r_i, CAP) * CAP
    picked = (
        (dot_nt(expand, named) > 0.5)
        & (dot_nt(expand, slot) == want.astype(F32))
        & (idiv(t_i, OWN) == idiv(r_i, CAP))
    )
    spread = ones(iota((2 * OWN, CH * 2 * OWN), 0) == imod(iota((2 * OWN, CH * 2 * OWN), 1), 2 * OWN))
    wide = dot(ones(picked), spread).astype(BF)
    m_i = iota((NC * MSG, NC * R), 0)
    rest = imod(m_i, MSG)
    rows_of = ones(
        (idiv(m_i, MSG) * R + imod(rest, R) == iota((NC * MSG, NC * R), 1)) & (rest < CH * R)
    )
    mm = iota((MSG, CH * 2 * OWN), 0)
    chunk_ok = jnp.where(idiv(mm, R) == idiv(iota((MSG, CH * 2 * OWN), 1), 2 * OWN), 1.0, 0.0)
    full = dot(rows_of, wide).reshape(NC, MSG, CH * 2 * OWN) * chunk_ok[None]
    dm[...] = full.reshape(NC * MSG, CH * 2 * OWN).astype(BF)


    for c in range(2):
        send_h(2, 1, c, dn, block(-2, c) + got_h(2, c))
        send_h(5, 4, c, up, block(2, c) + got_h(5, c))

    third = jnp.where((named > 0.5) & (slot > 1.5), 1.0, 0.0)
    third_row = dot_nt(jnp.ones((8, 128), BF), third.astype(BF))[0:1]
    third_wide = dot(jnp.broadcast_to(third_row, (8, 2 * OWN)).astype(BF), spread)[0:1]
    o_m, o_q = iota((OM, CH * 2 * OWN), 0), iota((OM, CH * 2 * OWN), 1)
    o_ok = (idiv(o_m, 2) == idiv(o_q, 2 * OWN)) & (imod(o_m, 2) == imod(idiv(o_q, OWN), 2))
    om[...] = jnp.where(o_ok, third_wide, 0.0).astype(BF)
    hot = jnp.max(third, axis=0, keepdims=True)
    e_row = iota((1, 128), 1)
    hot_x = jnp.sum(hot * imod(e_row, NX).astype(F32), axis=1, keepdims=True)
    hot_y = jnp.sum(hot * idiv(e_row, NX).astype(F32), axis=1, keepdims=True)


    for c in range(2):
        send_h(1, 0, c, dn, block(-1, c) + got_h(1, c))
        send_h(4, 3, c, up, block(1, c) + got_h(4, c))

    loads[4].wait()
    loads[5].wait()
    total = jnp.concatenate([block(0, c) + (got_h(0, c) + got_h(3, c)) for c in range(2)], axis=1)
    total = total + res_v[...].astype(F32)
    stream_ref[...] = total.astype(BF)
    mean_square = jnp.mean(total * total, axis=-1, keepdims=True)
    normed = (total * lax.rsqrt(mean_square + 1e-5) * gain_v[...].reshape(1, D)).astype(BF)
    for h in range(2):
        for c in range(CH):
            lo = h * HALF + c * 128
            hi = min(lo + 128, (h + 1) * HALF)
            piece = normed[:, lo:hi]
            if hi - lo < 128:
                piece = jnp.concatenate([piece, jnp.zeros((OWN, 128 - hi + lo), BF)], axis=1)
            stage[h, c] = piece
    mine = pl.ds(pl.multiple_of(p * OWN, OWN), OWN)
    st_copy = remote(stage.at[1 - p], xbuf.at[:, mine, :], st_ss, st_rs, other, z)
    st_copy.start()
    xbuf[:, mine, :] = stage[p]
    st_copy.wait_recv()

    osend[...] = dot(om[...], xbuf[...].reshape(CH * 2 * OWN, 128)).astype(BF)

    def oz_copy(d):
        return remote(osend, oz.at[z], oz_ss.at[d - 1], oz_rs.at[z], s, lax.rem(z + d, NZ))

    for d in range(1, NZ):
        oz_copy(d).start()
    oz[z] = osend[...]

    def at(y_, x_):
        return (y_ * NX + x_) * 2 + p

    msgs = dot(dm[...], xbuf[...].reshape(CH * 2 * OWN, 128)).astype(BF)
    sb1[...] = msgs.reshape(NC, MSG, 128)

    def near(r):
        dy, dx = NEAR[r]
        return lax.rem(y + dy + NY, NY) * NX + lax.rem(x + dx + NX, NX)

    def a1_copy(r):
        to = near(r)
        return remote(sb1.at[to], rb1.at[SEEN[r]], a1_ss.at[r], a1_rs.at[SEEN[r]], to * 2 + p, z)

    for r in range(1, NC):
        a1_copy(r).start()
    rb1[0] = sb1[chip]

    e_l = iota((2 * OWN, NC * R), 1)
    r_l = imod(e_l, R)
    back = ones(iota((128, NC * R), 0) == idiv(iota((128, NC * R), 1), R))
    take = (dot(slot, back) == (r_l - idiv(r_l, CAP) * CAP).astype(F32)) & (
        idiv(iota((2 * OWN, NC * R), 0), OWN) == idiv(r_l, CAP)
    )
    w_t = jnp.where(take, dot(weight, back), 0.0).astype(BF)
    spread_t = ones(iota((CH * 2 * OWN, 2 * OWN), 1) == imod(iota((CH * 2 * OWN, 2 * OWN), 0), 2 * OWN))
    tall = dot(spread_t, w_t).astype(BF)
    m_l = iota((NC * R, NC * MSG), 1)
    rest_l = imod(m_l, MSG)
    cols_of = ones(
        (idiv(m_l, MSG) * R + imod(rest_l, R) == iota((NC * R, NC * MSG), 0)) & (rest_l < CH * R)
    )
    full_t = dot(tall, cols_of)
    c_l = idiv(imod(iota((CH * 2 * OWN, NC * MSG), 1), MSG), R)
    w_third = jnp.sum(third * weight.astype(F32), axis=1, keepdims=True)
    w_tall = dot(spread_t, jnp.broadcast_to(w_third, (2 * OWN, 128)).astype(BF))[:, :OM]
    o_q, o_m = iota((CH * 2 * OWN, OM), 0), iota((CH * 2 * OWN, OM), 1)
    o_ok = (idiv(o_m, 2) == idiv(o_q, 2 * OWN)) & (imod(o_m, 2) == imod(idiv(o_q, OWN), 2))
    co[...] = jnp.where(o_ok, w_tall, 0.0).astype(BF)
    cm[...] = jnp.where(c_l == idiv(iota((CH * 2 * OWN, NC * MSG), 0), 2 * OWN), full_t, 0.0).astype(BF)

    def a1_wait(r):
        if r:
            a1_copy(SEEN[r]).wait_recv()

    def rows(h):
        return pl.ds(h * SB, SB)

    def ag_copy(src, dst, h, head):
        return remote(
            slots.at[src, rows(h)], slots.at[dst, rows(h)],
            ag_ss.at[dst, h], ag_rs.at[dst, h], s, head,
        )

    def lo_copy(slot_at, h):
        return remote(
            low_own.at[slot_at, rows(h)], low_oth.at[slot_at, rows(h)],
            lo_ss.at[slot_at, h], lo_rs.at[slot_at, h], other, z,
        )

    def low(slot_at, h):
        low_own[slot_at, rows(h)] = dot(slots[slot_at, rows(h)], win_v[...]).astype(BF)
        lo_copy(slot_at, h).start()

    for h in range(H):
        for g in range(h * GH, (h + 1) * GH):
            for i in range(GS):
                a1_wait(g * GS + i)
            got = dot(pm[...], rb1[GS * g:GS * (g + 1)].reshape(GS * MSG, 128)).astype(BF)
            for c in range(CH):
                width = min(128, HALF - 128 * c)
                slots[0, GR * g:GR * (g + 1), 128 * c:128 * c + width] = got[GR * c:GR * (c + 1), :width]
        ag_copy(0, 1, h, up).start()
        ag_copy(0, 4, h, dn).start()
    for d in range(1, NZ):
        from_z = lax.rem(z + d, NZ)
        remote(osend, oz.at[from_z], oz_ss.at[d - 1], oz_rs.at[from_z], s, from_z).wait_recv()
    ox[x, y] = dot(p2[...], oz[...].reshape(NZ * OM, 128)).astype(BF)

    def oy_copy(d):
        to = lax.rem(y + d, NY)
        return remote(ox.at[x, y], ox.at[x, y], oy_ss.at[d - 1], oy_rs.at[y], at(to, x), z)

    for d in range(1, NY):
        oy_copy(d).start()

    loads[6].wait()
    for h in range(H):
        low(0, h)

    right, left = lax.rem(x + 1, NX), lax.rem(x + NX - 1, NX)

    def ox_copy(way, from_x, from_y):
        return remote(
            ox.at[from_x, from_y], ox.at[from_x, from_y], ox_ss.at[way, from_y], ox_rs.at[from_x, from_y],
            at(y, right if way in (0, 2) else left), z,
        )

    def ox_send(dy):
        from_y = lax.rem(y + dy, NY)
        if dy:
            remote(
                ox.at[x, from_y], ox.at[x, from_y], ox_ss.at[0, from_y], oy_rs.at[from_y], at(from_y, x), z
            ).wait_recv()
        ox_copy(0, x, from_y).start()
        ox_copy(1, x, from_y).start()

    def ox_take(d):
        from_x = lax.rem(x + d, NX)
        if d:
            for from_y in range(NY):
                ox_copy(0, from_x, from_y).wait_recv()
                if d == 3 and from_y < 4:
                    ox_copy(2, left, from_y).start()
                if d == 1 and from_y >= 4:
                    ox_copy(3, right, from_y).start()
        for c in range(CH):
            width = min(128, HALF - 128 * c)
            piece = ox[from_x, :, OWN * c:OWN * (c + 1), :].reshape(NR, 128)
            slots[OV + d, :, 128 * c:128 * c + width] = piece[:, :width]
        for h in range(H):
            low(OV + d, h)

    ox_send(0)
    aside = {
        (1, 1): (lambda: (ox_send(1), ox_send(7))),
        (1, 3): (lambda: (ox_send(2), ox_send(6))),
        (2, 1): (lambda: (ox_send(3), ox_send(5), ox_send(4))),
        (2, 3): (lambda: ox_take(0)),
        (3, 1): (lambda: ox_take(3)),
        (3, 3): (lambda: ox_take(1)),
    }
    for k in (1, 2, 3):
        for h in range(H):
            ag_copy(0, k, h, up).wait_recv()
            if k < 3:
                ag_copy(k, k + 1, h, up).start()
            ag_copy(0, k + 3, h, dn).wait_recv()
            if k < 3:
                ag_copy(k + 3, k + 4, h, dn).start()
            else:
                ag_copy(far_from, FAR, h, far_to).start()
            low(k, h)
            low(k + 3, h)
            if (k, h) in aside:
                aside[k, h]()
    def expert(slot_at, h):
        lo_copy(slot_at, h).wait_recv()
        inner = low_own[slot_at, rows(h)].astype(F32) + low_oth[slot_at, rows(h)].astype(F32)
        gate, upv = inner[:, :192], inner[:, 192:]
        active = ((upv + 1.0) * gate * jax.nn.sigmoid(1.702 * gate)).astype(BF)
        return dot(active, wout_v[...])

    def q_copy(slot_at, dst, h, head):
        return remote(
            qs.at[slot_at, rows(h)], racc.at[dst, rows(h)],
            q_ss.at[slot_at, h], q_rs.at[dst, h], s, head,
        )

    back = tuple(reversed(range(H)))
    first = 6 - 3 * p
    first_to = lax.rem(z + 1 + (NZ - 2) * p, NZ)
    loads[7].wait()
    for h in back:
        qs[first, rows(h)] = expert(first, h).astype(BF)
        q_copy(first, first - 1, h, first_to).start()
    for h in range(H):
        ag_copy(far_from, FAR, h, far_to).wait_recv()
        low(FAR, h)

    for h in back:
        qs[FAR, rows(h)] = expert(FAR, h).astype(BF)
        q_copy(FAR, FAR, h, far_back).start()
    ox_take(2)
    for h in back:
        value = expert(far_from, h)
        q_copy(FAR, FAR, h, far_back).wait_recv()
        qs[far_from, rows(h)] = (value + racc[FAR, rows(h)].astype(F32)).astype(BF)
        q_copy(far_from, far_from - 1, h, far_back).start()

    def of_copy(way):
        part = slice(0, 4) if way == 0 else slice(4, 8)
        return remote(
            obuf.at[2, part], ofar.at[part], or_ss.at[way], or_rs.at[way], at(y, left if way == 0 else right), z
        )

    def or_copy(way):
        return remote(
            obuf.at[3 - 2 * way], oret.at[way], or_ss.at[2 + way], or_rs.at[2 + way],
            at(y, left if way == 0 else right), z,
        )

    def oyr_copy(d):
        to = lax.rem(y + d, NY)
        return remote(osel.at[to], oyr.at[y], oyr_ss.at[d - 1], oyr_rs.at[y], at(to, x), z)

    def ozr_copy(d):
        to = lax.rem(z + d, NZ)
        return remote(ozs.at[to], ozr.at[z], ozr_ss.at[d - 1], ozr_rs.at[z], s, to)

    here = hot_x == x.astype(F32)

    def ov_expert(d):
        for h in range(H):
            value = expert(OV + d, h).astype(BF)
            n = SB // OWN
            for c in range(CH):
                piece = value[:, 128 * c:128 * (c + 1)]
                if piece.shape[1] < 128:
                    piece = jnp.concatenate([piece, jnp.zeros((SB, 128 * CH - HALF), BF)], axis=1)
                obuf[d, n * h:n * (h + 1), OWN * c:OWN * (c + 1), :] = piece.reshape(n, OWN, 128)

    def ov_far():
        ov_expert(2)
        for way in range(2):
            of_copy(way).start()

    def ov_near():
        for way in range(2):
            ov_expert(3 - 2 * way)
        for way in range(2):
            of_copy(way).wait_recv()
            for to_y in range(4 * way, 4 * way + 4):
                mixed = jnp.where(here, obuf[3 - 2 * way, to_y].astype(F32), ofar[to_y].astype(F32))
                obuf[3 - 2 * way, to_y] = mixed.astype(BF)
            or_copy(way).start()
        ov_expert(0)

    def ov_back_y():
        for way in range(2):
            or_copy(way).wait_recv()
        for to_y in range(NY):
            pass_by = 0 if to_y < 4 else 1
            acc = oret[pass_by, to_y].astype(F32)
            neighbour = left if to_y < 4 else right
            acc = jnp.where(hot_x == neighbour.astype(F32), oret[1 - pass_by, to_y].astype(F32), acc)
            osel[to_y] = jnp.where(here, obuf[0, to_y].astype(F32), acc).astype(BF)
        for d in range(1, NY):
            oyr_copy(d).start()

    def ov_back_z():
        acc = jnp.where(hot_y == y.astype(F32), osel[y].astype(F32), 0.0)
        for d in range(1, NY):
            from_y = lax.rem(y + d, NY)
            remote(osel.at[from_y], oyr.at[from_y], oyr_ss.at[d - 1], oyr_rs.at[from_y], at(from_y, x), z).wait_recv()
            acc = jnp.where(hot_y == from_y.astype(F32), oyr[from_y].astype(F32), acc)
        ozs[...] = dot(p2t[...], acc.astype(BF)).astype(BF).reshape(NZ, OM, 128)
        for d in range(1, NZ):
            ozr_copy(d).start()
        ozr[z] = ozs[z]

    ov_far()
    for k in (2, 1):
        for h in back:
            below, above = expert(k, h), expert(k + 3, h)
            q_copy(k, k, h, dn).wait_recv()
            qs[k, rows(h)] = (below + racc[k, rows(h)].astype(F32)).astype(BF)
            q_copy(k, k - 1, h, dn).start()
            q_copy(k + 3, k + 3, h, up).wait_recv()
            qs[k + 3, rows(h)] = (above + racc[k + 3, rows(h)].astype(F32)).astype(BF)
            q_copy(k + 3, k + 2, h, up).start()
        if k == 2:
            ov_near()
        else:
            ov_back_y()

    def a2_copy(r):
        to = near(r)
        return remote(sb2.at[r], rb2.at[chip], a2_ss.at[r], a2_rs.at[chip], to * 2 + p, z)

    for h in back:
        value = expert(0, h)
        q_copy(0, 0, h, dn).wait_recv()
        q_copy(0, 3, h, up).wait_recv()
        value = (value + racc[0, rows(h)].astype(F32) + racc[3, rows(h)].astype(F32)).astype(BF)
        for i in range(GH):
            g = h * GH + i
            part = value[GR * i:GR * (i + 1)]
            pieces = [part[:, 128 * c:128 * (c + 1)] for c in range(CH - 1)]
            last = part[:, 128 * (CH - 1):]
            pieces.append(jnp.concatenate([last, jnp.zeros((GR, 128 * CH - HALF), BF)], axis=1))
            out = dot(pt[...], jnp.concatenate(pieces, axis=0)).astype(BF)
            sb2[GS * g:GS * (g + 1)] = out.reshape(GS, MSG, 128)
            for r in range(GS * g, GS * (g + 1)):
                if r:
                    a2_copy(r).start()

    ov_back_z()
    rb2[chip] = sb2[0]
    for d in range(1, NZ):
        from_z = lax.rem(z + d, NZ)
        remote(ozs.at[from_z], ozr.at[from_z], ozr_ss.at[d - 1], ozr_rs.at[from_z], s, from_z).wait_recv()
    third_sum = jnp.sum(ozr[...].astype(F32), axis=0).astype(BF)

    @pl.loop(0, NC)
    def _(src):
        @pl.when(src != chip)
        def _():
            remote(sb2.at[src], rb2.at[src], a2_ss.at[0], a2_rs.at[src], src * 2 + p, z).wait_recv()

    out = dot(cm[...], rb2[...].reshape(NC * MSG, 128)) + dot(co[...], third_sum)
    out = out.astype(BF).reshape(CH, 2 * OWN, 128)
    cm_out = xbuf
    cm_out[...] = out
    theirs = pl.ds(pl.multiple_of((1 - p) * OWN, OWN), OWN)
    fsend[...] = cm_out[:, theirs, :]
    f_copy = remote(fsend, fin.at[p], f_ss, f_rs, other, z)
    f_copy.start()
    fin[p] = cm_out[:, mine, :]
    f_copy.wait_recv()
    esum_ref[...] = jnp.concatenate(
        [fin[h, c][:, :min(128, HALF - 128 * c)] for h in range(2) for c in range(CH)], axis=1
    )

    kv_copy.wait_send()
    info_copy.wait_send()
    st_copy.wait_send()
    f_copy.wait_send()
    for d in range(1, NZ):
        oz_copy(d).wait_send()
        oy_copy(d).wait_send()
        oyr_copy(d).wait_send()
        ozr_copy(d).wait_send()
        for c in range(2):
            h_copy(d, d, c, up).wait_send()
    for way in range(2):
        of_copy(way).wait_send()
        or_copy(way).wait_send()
    for from_y in range(NY):
        ox_copy(0, x, from_y).wait_send()
        ox_copy(1, x, from_y).wait_send()
        ox_copy(2 if from_y < 4 else 3, x, from_y).wait_send()
    for r in range(1, NC):
        a1_copy(r).wait_send()
        a2_copy(r).wait_send()

    for slot_at in range(OV + NX):
        for h in range(H):
            lo_copy(slot_at, h).wait_send()
            if 0 < slot_at < OV:
                ag_copy(0, slot_at, h, up).wait_send()
                q_copy(slot_at, slot_at, h, up).wait_send()


def deliver(stream_in, esum_in, stream_out, esum_out, sem):
    copies = [
        pltpu.make_async_copy(stream_in, stream_out, sem.at[0]),
        pltpu.make_async_copy(esum_in, esum_out, sem.at[1]),
    ]
    for c in copies:
        c.start()
    for c in copies:
        c.wait()


def per_device(q, kv, wo, res, gain, ids, weights, w_in, w_out):
    vm = pltpu.VMEM
    dma = pltpu.SemaphoreType.DMA
    scratch = [
        vm((TOK, 512), BF), vm((2, TOK, 128), BF), vm((D, 512), BF), vm((OWN, D), BF), vm((D,), F32),
        vm((TOP, TOK), I32), vm((TOP, TOK), BF), vm((2 * TOP, TOK), F32), vm((2, OWN, 128), F32), vm((HALF, 384), BF), vm((192, HALF), BF),
        vm((TOK, 512), BF), vm((NZ, OWN, D), F32), vm((NZ, OWN, D), BF), vm((NZ, OWN, D), BF),
        vm((2, CH, OWN, 128), BF), vm((CH, 2 * OWN, 128), BF),
        vm((NC * MSG, CH * 2 * OWN), BF), vm((CH * 2 * OWN, NC * MSG), BF),
        vm((CH * GR, GS * MSG), BF), vm((GS * MSG, CH * GR), BF),
        vm((NC, MSG, 128), BF), vm((NC, MSG, 128), BF),
        vm((OV + NX, NR, HALF), BF), vm((OV + NX, NR, 384), BF), vm((OV + NX, NR, 384), BF),
        vm((8, NR, HALF), BF), vm((8, NR, HALF), BF),
        vm((NC, MSG, 128), BF), vm((NC, MSG, 128), BF),
        vm((2, CH, OWN, 128), BF), vm((CH, OWN, 128), BF),
        vm((OM, CH * 2 * OWN), BF), vm((CH * 2 * OWN, OM), BF), vm((OB, NZ * OM), BF), vm((NZ * OM, OB), BF),
        vm((OM, 128), BF), vm((NZ, OM, 128), BF), vm((NX, NY, OB, 128), BF), vm((NX, NY, OB, 128), BF),
        vm((NY, OB, 128), BF), vm((2, NY, OB, 128), BF), vm((NY, OB, 128), BF), vm((NY, OB, 128), BF),
        vm((NZ, OM, 128), BF), vm((NZ, OM, 128), BF),
        dma((9,)), dma, dma, dma, dma, dma((NZ, 2)), dma((NZ, 2)), dma, dma,
        dma((NC,)), dma((NC,)), dma((8, H)), dma((8, H)), dma((OV + NX, H)), dma((OV + NX, H)),
        dma((8, H)), dma((8, H)), dma((NC,)), dma((NC,)), dma, dma,
        dma((NZ,)), dma((NZ,)), dma((NY,)), dma((NY,)), dma((NX, NY)), dma((NX, NY)), dma((NX,)), dma((NX,)),
        dma((NY,)), dma((NY,)), dma((NZ,)), dma((NZ,)),
    ]
    made = pl.pallas_call(
        kernel,
        out_shape=(jax.ShapeDtypeStruct((OWN, D), BF), jax.ShapeDtypeStruct((OWN, D), BF)),
        in_specs=[pl.BlockSpec(memory_space=pl.ANY)] * 9,
        out_specs=(pl.BlockSpec(memory_space=vm), pl.BlockSpec(memory_space=vm)),
        scratch_shapes=scratch,
        compiler_params=pltpu.CompilerParams(
            collective_id=0, has_side_effects=True, vmem_limit_bytes=58 * 1024 * 1024
        ),
        cost_estimate=pl.CostEstimate(flops=4_000_000_000, bytes_accessed=8_000_000, transcendentals=300_000),
    )(q, kv.reshape(TOK, 128), wo.T, res, gain, ids.T, weights.T, w_in, w_out)
    return pl.pallas_call(
        deliver,
        out_shape=(jax.ShapeDtypeStruct((OWN, D), BF), jax.ShapeDtypeStruct((OWN, D), BF)),
        in_specs=[pl.BlockSpec(memory_space=pl.ANY)] * 2,
        out_specs=(pl.BlockSpec(memory_space=pl.ANY), pl.BlockSpec(memory_space=pl.ANY)),
        scratch_shapes=[dma((2,))],
    )(*made)


def solution(mesh):
    placed = (
        P("seq", "head"), P("seq", "head", None), P("head", None), P(("seq", "head"), None), P(),
        P("seq", None), P("seq", None), P("seq", None, "head"), P("seq", "head", None),
    )
    return jax.shard_map(
        per_device, mesh=mesh, in_specs=placed,
        out_specs=(P(("seq", "head"), None), P(("seq", "head"), None)), check_vma=False,
    )
```

```python
import jax
import jax.numpy as jnp
from jax import lax
from jax.experimental import pallas as pl
from jax.experimental.pallas import tpu as pltpu
from jax.sharding import PartitionSpec as P

MESH = pl.DeviceIdType.MESH
BF = jnp.bfloat16
F32 = jnp.float32
I32 = jnp.int32

NS, NZ = 64, 8
NC = NS // 2
TOK, OWN, TOP = 128, 16, 4
D, HALF, CH = 2880, 1440, 12
NX, NY = 4, 8
R = 4
CAP = R // 2
MSG = 48
GS, GR = 4, 16
NR = NC * R
H = 2
SB = NR // H
GH = SB // GR
FAR = 7
OV = 8
OM = 32
PIECES = ((0, 1024), (1024, 2048), (2048, D))
NP = len(PIECES)
OB = CH * OWN

NEAR = sorted(
    [(dy, dx) for dy in range(-3, 5) for dx in range(-1, 3)], key=lambda o: (abs(o[0]) + abs(o[1]), o)
)
SEEN = [NEAR.index(((3 - dy) % NY - 3, (1 - dx) % NX - 1)) for dy, dx in NEAR]


def idiv(v, n):
    if n & (n - 1) == 0:
        return lax.shift_right_logical(v, jnp.full_like(v, n.bit_length() - 1))
    return ((v.astype(F32) + 0.5) * (1.0 / n)).astype(I32)


def imod(v, n):
    return v - idiv(v, n) * n


def iota(shape, dim):
    return lax.broadcasted_iota(I32, shape, dim)


def dot(a, b):
    return jnp.dot(a, b, preferred_element_type=F32)


def dot_nt(a, b):
    return lax.dot_general(a, b, (((1,), (1,)), ((), ())), preferred_element_type=F32)


def ones(cond):
    return jnp.where(cond, 1.0, 0.0).astype(BF)


def kernel(
    q_hbm, kv_hbm, wo_hbm, res_hbm, gain_hbm, ids_hbm, rw_hbm, win_hbm, wout_hbm,
    stream_ref, esum_ref,
    q_v, kv2, wo_v, res_v, gain_v, ids_v, rw_v, both, info2, win_v, wout_v,
    att_v, own_f, ps, rs, stage, xbuf, dm, cm, pm, pt,
    sb1, rb1, slots, low_own, low_oth, qs, racc, sb2, rb2, fin, fsend,
    om, co, p2, p2t, osend, oz, ox, obuf, ofar, oret, osel, oyr, ozs, ozr,
    load_sem, kv_ss, kv_rs, info_ss, info_rs, rs_ss, rs_rs, st_ss, st_rs,
    a1_ss, a1_rs, ag_ss, ag_rs, lo_ss, lo_rs, q_ss, q_rs, a2_ss, a2_rs, f_ss, f_rs,
    oz_ss, oz_rs, oy_ss, oy_rs, ox_ss, ox_rs, or_ss, or_rs, oyr_ss, oyr_rs, ozr_ss, ozr_rs,
):
    s = lax.axis_index("seq")
    z = lax.axis_index("head")
    p = lax.rem(s, 2)
    chip = lax.div(s, 2)
    x = lax.rem(chip, NX)
    y = lax.div(chip, NX)
    other = s + 1 - 2 * p
    nxt = lax.rem(s + 1, NS)
    prv = lax.rem(s + NS - 1, NS)
    up = lax.rem(z + 1, NZ)
    dn = lax.rem(z + NZ - 1, NZ)

    loads = [
        pltpu.make_async_copy(src, dst, load_sem.at[i])
        for i, (src, dst) in enumerate(
            [
                (kv_hbm, kv2.at[1]),
                (q_hbm, q_v),
                (ids_hbm, ids_v),
                (wo_hbm, wo_v),
                (res_hbm, res_v),
                (gain_hbm, gain_v),
                (win_hbm.at[0], win_v),
                (wout_hbm.at[0], wout_v),
                (rw_hbm, rw_v),
            ]
        )
    ]
    for c in loads:
        c.start()

    barrier = pltpu.get_barrier_semaphore()

    def greet(seq, head):
        pl.semaphore_signal(barrier, inc=1, device_id=(seq, head), device_id_type=MESH)

    greet(other, z)
    greet(prv, z)

    @pl.loop(1, NZ)
    def _(d):
        greet(s, lax.rem(z + d, NZ))

    @pl.loop(1, NC)
    def _(d):
        greet(lax.rem(chip + d, NC) * 2 + p, z)

    pl.semaphore_wait(barrier, 1 + 1 + (NZ - 1) + (NC - 1))

    def remote(src, dst, ss, rs_, seq, head):
        return pltpu.make_async_remote_copy(
            src_ref=src, dst_ref=dst, send_sem=ss, recv_sem=rs_,
            device_id=(seq, head), device_id_type=MESH,
        )

    loads[0].wait()
    kv_copy = remote(kv2.at[1], kv2.at[0], kv_ss, kv_rs, nxt, z)
    kv_copy.start()
    loads[2].wait()
    loads[8].wait()
    both[0:TOP] = ids_v[...].astype(F32)
    both[TOP:] = rw_v[...].astype(F32)
    chosen = ones(iota((OWN, TOK), 1) == iota((OWN, TOK), 0) + z * OWN)
    info2[p, :, 0:2 * TOP] = dot_nt(chosen, both[...].astype(BF))
    info_copy = remote(info2.at[p], info2.at[p], info_ss, info_rs, other, z)
    info_copy.start()
    def perm2(shape, a_dim):
        i, j = iota(shape, a_dim), iota(shape, 1 - a_dim)
        inner = imod(j, OM)
        return ones(
            (idiv(i, OWN) == idiv(inner, 2))
            & (idiv(imod(i, OWN), 2) == idiv(j, OM))
            & (imod(i, 2) == imod(inner, 2))
        )

    p2[...] = perm2((OB, NZ * OM), 0)
    p2t[...] = perm2((NZ * OM, OB), 1)

    def perm(shape, a_dim):
        i, j = iota(shape, a_dim), iota(shape, 1 - a_dim)
        inner = imod(j, MSG)
        return ones(
            (idiv(i, GR) == idiv(inner, R))
            & (idiv(imod(i, GR), R) == idiv(j, MSG))
            & (imod(i, R) == imod(inner, R))
            & (inner < CH * R)
        )

    pm[...] = perm((CH * GR, GS * MSG), 0)
    pt[...] = perm((GS * MSG, CH * GR), 1)
    loads[1].wait()
    kv_copy.wait_recv()

    kvf = kv2[...].reshape(2 * TOK, 128).astype(F32)
    lane = iota((2 * TOK, 128), 1)
    turned = pltpu.roll(kvf, 64, 1)
    k_even = jnp.where(lane < 64, kvf, 0.0).astype(BF)
    k_odd = jnp.where(lane >= 64, turned, 0.0).astype(BF)
    v_even = jnp.where(lane < 64, turned, 0.0).astype(BF)
    v_odd = jnp.where(lane >= 64, kvf, 0.0).astype(BF)
    qpos = iota((TOK, 2 * TOK), 0)
    kpos = iota((TOK, 2 * TOK), 1)
    allowed = (kpos > qpos) & (kpos <= qpos + TOK) & (s * TOK - TOK + kpos >= 0)
    for pair in range(4):
        qp = q_v[:, 128 * pair:128 * (pair + 1)]
        acc = None
        for kk, vv in ((k_even, v_even), (k_odd, v_odd)):
            sc = jnp.where(allowed, dot_nt(qp, kk) * 0.125, -1e30)
            ex = jnp.exp(sc - jnp.max(sc, axis=-1, keepdims=True))
            w = (ex / jnp.sum(ex, axis=-1, keepdims=True)).astype(BF)
            part = dot(w, vv)
            acc = part if acc is None else acc + part
        att_v[:, 128 * pair:128 * (pair + 1)] = acc.astype(BF)

    far_from = 3 + 3 * p
    far_to = lax.rem(z + 1 + (NZ - 2) * p, NZ)
    far_back = lax.rem(z + NZ - 1 + 2 * p, NZ)

    def h_copy(slot_at, dst, c, head):
        lo, hi = PIECES[c]
        return remote(
            ps.at[slot_at, :, lo:hi], rs.at[dst, :, lo:hi], rs_ss.at[slot_at, c], rs_rs.at[dst, c], s, head
        )

    def block(d, c):
        lo, hi = PIECES[c]
        return own_f[lax.rem(z + d + NZ, NZ), :, lo:hi]

    def got_h(dst, c):
        lo, hi = PIECES[c]
        h_copy(FAR, dst, c, up).wait_recv()
        return rs[dst, :, lo:hi].astype(F32)

    def send_h(slot_at, dst, c, head, value):
        lo, hi = PIECES[c]
        ps[slot_at, :, lo:hi] = value.astype(BF)
        h_copy(slot_at, dst, c, head).start()

    loads[3].wait()
    for c, (lo, hi) in enumerate(PIECES):
        for n0 in range(lo, hi, 512):
            n1 = min(hi, n0 + 512)
            own_f[:, :, n0:n1] = dot_nt(att_v[...], wo_v[n0:n1]).reshape(NZ, OWN, n1 - n0)
        send_h(FAR, FAR, c, far_back, block(4, c))

    info_copy.wait_recv()
    inf = info2[...].reshape(2 * OWN, 128)
    lanes = iota((2 * OWN, 128), 1).astype(F32)
    named = jnp.zeros((2 * OWN, 128), F32)
    weight = jnp.zeros((2 * OWN, 128), F32)
    for k in range(TOP):
        hit = inf[:, k:k + 1] == lanes
        named = named + jnp.where(hit, 1.0, 0.0)
        weight = weight + jnp.where(hit, inf[:, TOP + k:TOP + k + 1], 0.0)
    named, weight = named.astype(BF), weight.astype(BF)
    ta, tb = iota((2 * OWN, 2 * OWN), 0), iota((2 * OWN, 2 * OWN), 1)
    before = ones((tb < ta) & (idiv(tb, OWN) == idiv(ta, OWN)))
    slot = dot(before, named).astype(BF)
    ra = iota((NC * R, 128), 0)
    expand = ones(idiv(ra, R) == iota((NC * R, 128), 1))

    for c in range(NP):
        got = got_h(FAR, c)
        send_h(3, 2, c, dn, block(-3, c) + jnp.where(p == 0, got, 0.0))
        send_h(6, 5, c, up, block(3, c) + jnp.where(p == 0, 0.0, got))

    r_i = imod(iota((NC * R, 2 * OWN), 0), R)
    t_i = iota((NC * R, 2 * OWN), 1)
    want = r_i - idiv(r_i, CAP) * CAP
    picked = (
        (dot_nt(expand, named) > 0.5)
        & (dot_nt(expand, slot) == want.astype(F32))
        & (idiv(t_i, OWN) == idiv(r_i, CAP))
    )
    spread = ones(iota((2 * OWN, CH * 2 * OWN), 0) == imod(iota((2 * OWN, CH * 2 * OWN), 1), 2 * OWN))
    wide = dot(ones(picked), spread).astype(BF)
    m_i = iota((NC * MSG, NC * R), 0)
    rest = imod(m_i, MSG)
    rows_of = ones(
        (idiv(m_i, MSG) * R + imod(rest, R) == iota((NC * MSG, NC * R), 1)) & (rest < CH * R)
    )
    mm = iota((MSG, CH * 2 * OWN), 0)
    chunk_ok = jnp.where(idiv(mm, R) == idiv(iota((MSG, CH * 2 * OWN), 1), 2 * OWN), 1.0, 0.0)
    full = dot(rows_of, wide).reshape(NC, MSG, CH * 2 * OWN) * chunk_ok[None]
    dm[...] = full.reshape(NC * MSG, CH * 2 * OWN).astype(BF)


    for c in range(NP):
        send_h(2, 1, c, dn, block(-2, c) + got_h(2, c))
        send_h(5, 4, c, up, block(2, c) + got_h(5, c))

    third = jnp.where((named > 0.5) & (slot > 1.5), 1.0, 0.0)
    third_row = dot_nt(jnp.ones((8, 128), BF), third.astype(BF))[0:1]
    third_wide = dot(jnp.broadcast_to(third_row, (8, 2 * OWN)).astype(BF), spread)[0:1]
    o_m, o_q = iota((OM, CH * 2 * OWN), 0), iota((OM, CH * 2 * OWN), 1)
    o_ok = (idiv(o_m, 2) == idiv(o_q, 2 * OWN)) & (imod(o_m, 2) == imod(idiv(o_q, OWN), 2))
    om[...] = jnp.where(o_ok, third_wide, 0.0).astype(BF)
    hot = jnp.max(third, axis=0, keepdims=True)
    e_row = iota((1, 128), 1)
    hot_x = jnp.sum(hot * imod(e_row, NX).astype(F32), axis=1, keepdims=True)
    hot_y = jnp.sum(hot * idiv(e_row, NX).astype(F32), axis=1, keepdims=True)


    for c in range(NP):
        send_h(1, 0, c, dn, block(-1, c) + got_h(1, c))
        send_h(4, 3, c, up, block(1, c) + got_h(4, c))

    loads[4].wait()
    loads[5].wait()
    total = jnp.concatenate([block(0, c) + (got_h(0, c) + got_h(3, c)) for c in range(NP)], axis=1)
    total = total + res_v[...].astype(F32)
    stream_ref[...] = total.astype(BF)
    mean_square = jnp.mean(total * total, axis=-1, keepdims=True)
    normed = (total * lax.rsqrt(mean_square + 1e-5) * gain_v[...].reshape(1, D)).astype(BF)
    for h in range(2):
        for c in range(CH):
            lo = h * HALF + c * 128
            hi = min(lo + 128, (h + 1) * HALF)
            piece = normed[:, lo:hi]
            if hi - lo < 128:
                piece = jnp.concatenate([piece, jnp.zeros((OWN, 128 - hi + lo), BF)], axis=1)
            stage[h, c] = piece
    mine = pl.ds(pl.multiple_of(p * OWN, OWN), OWN)
    st_copy = remote(stage.at[1 - p], xbuf.at[:, mine, :], st_ss, st_rs, other, z)
    st_copy.start()
    xbuf[:, mine, :] = stage[p]
    st_copy.wait_recv()

    osend[...] = dot(om[...], xbuf[...].reshape(CH * 2 * OWN, 128)).astype(BF)

    def oz_copy(d):
        return remote(osend, oz.at[z], oz_ss.at[d - 1], oz_rs.at[z], s, lax.rem(z + d, NZ))

    for d in range(1, NZ):
        oz_copy(d).start()
    oz[z] = osend[...]

    def at(y_, x_):
        return (y_ * NX + x_) * 2 + p

    msgs = dot(dm[...], xbuf[...].reshape(CH * 2 * OWN, 128)).astype(BF)
    sb1[...] = msgs.reshape(NC, MSG, 128)

    def near(r):
        dy, dx = NEAR[r]
        return lax.rem(y + dy + NY, NY) * NX + lax.rem(x + dx + NX, NX)

    def a1_copy(r):
        to = near(r)
        return remote(sb1.at[to], rb1.at[SEEN[r]], a1_ss.at[r], a1_rs.at[SEEN[r]], to * 2 + p, z)

    for r in range(1, NC):
        a1_copy(r).start()
    rb1[0] = sb1[chip]

    e_l = iota((2 * OWN, NC * R), 1)
    r_l = imod(e_l, R)
    back = ones(iota((128, NC * R), 0) == idiv(iota((128, NC * R), 1), R))
    take = (dot(slot, back) == (r_l - idiv(r_l, CAP) * CAP).astype(F32)) & (
        idiv(iota((2 * OWN, NC * R), 0), OWN) == idiv(r_l, CAP)
    )
    w_t = jnp.where(take, dot(weight, back), 0.0).astype(BF)
    spread_t = ones(iota((CH * 2 * OWN, 2 * OWN), 1) == imod(iota((CH * 2 * OWN, 2 * OWN), 0), 2 * OWN))
    tall = dot(spread_t, w_t).astype(BF)
    m_l = iota((NC * R, NC * MSG), 1)
    rest_l = imod(m_l, MSG)
    cols_of = ones(
        (idiv(m_l, MSG) * R + imod(rest_l, R) == iota((NC * R, NC * MSG), 0)) & (rest_l < CH * R)
    )
    full_t = dot(tall, cols_of)
    c_l = idiv(imod(iota((CH * 2 * OWN, NC * MSG), 1), MSG), R)
    w_third = jnp.sum(third * weight.astype(F32), axis=1, keepdims=True)
    w_tall = dot(spread_t, jnp.broadcast_to(w_third, (2 * OWN, 128)).astype(BF))[:, :OM]
    o_q, o_m = iota((CH * 2 * OWN, OM), 0), iota((CH * 2 * OWN, OM), 1)
    o_ok = (idiv(o_m, 2) == idiv(o_q, 2 * OWN)) & (imod(o_m, 2) == imod(idiv(o_q, OWN), 2))
    co[...] = jnp.where(o_ok, w_tall, 0.0).astype(BF)
    cm[...] = jnp.where(c_l == idiv(iota((CH * 2 * OWN, NC * MSG), 0), 2 * OWN), full_t, 0.0).astype(BF)

    def a1_wait(r):
        if r:
            a1_copy(SEEN[r]).wait_recv()

    def rows(h):
        return pl.ds(h * SB, SB)

    def ag_copy(src, dst, h, head):
        return remote(
            slots.at[src, rows(h)], slots.at[dst, rows(h)],
            ag_ss.at[dst, h], ag_rs.at[dst, h], s, head,
        )

    def lo_copy(slot_at, h):
        return remote(
            low_own.at[slot_at, rows(h)], low_oth.at[slot_at, rows(h)],
            lo_ss.at[slot_at, h], lo_rs.at[slot_at, h], other, z,
        )

    def low(slot_at, h):
        low_own[slot_at, rows(h)] = dot(slots[slot_at, rows(h)], win_v[...]).astype(BF)
        lo_copy(slot_at, h).start()

    for h in range(H):
        for g in range(h * GH, (h + 1) * GH):
            for i in range(GS):
                a1_wait(g * GS + i)
            got = dot(pm[...], rb1[GS * g:GS * (g + 1)].reshape(GS * MSG, 128)).astype(BF)
            for c in range(CH):
                width = min(128, HALF - 128 * c)
                slots[0, GR * g:GR * (g + 1), 128 * c:128 * c + width] = got[GR * c:GR * (c + 1), :width]
        ag_copy(0, 1, h, up).start()
        ag_copy(0, 4, h, dn).start()
    for d in range(1, NZ):
        from_z = lax.rem(z + d, NZ)
        remote(osend, oz.at[from_z], oz_ss.at[d - 1], oz_rs.at[from_z], s, from_z).wait_recv()
    ox[x, y] = dot(p2[...], oz[...].reshape(NZ * OM, 128)).astype(BF)

    def oy_copy(d):
        to = lax.rem(y + d, NY)
        return remote(ox.at[x, y], ox.at[x, y], oy_ss.at[d - 1], oy_rs.at[y], at(to, x), z)

    for d in range(1, NY):
        oy_copy(d).start()

    loads[6].wait()
    for h in range(H):
        low(0, h)

    right, left = lax.rem(x + 1, NX), lax.rem(x + NX - 1, NX)

    def ox_copy(way, from_x, from_y):
        return remote(
            ox.at[from_x, from_y], ox.at[from_x, from_y], ox_ss.at[way, from_y], ox_rs.at[from_x, from_y],
            at(y, right if way in (0, 2) else left), z,
        )

    def ox_send(dy):
        from_y = lax.rem(y + dy, NY)
        if dy:
            remote(
                ox.at[x, from_y], ox.at[x, from_y], ox_ss.at[0, from_y], oy_rs.at[from_y], at(from_y, x), z
            ).wait_recv()
        ox_copy(0, x, from_y).start()
        ox_copy(1, x, from_y).start()

    def ox_take(d):
        from_x = lax.rem(x + d, NX)
        if d:
            for from_y in range(NY):
                ox_copy(0, from_x, from_y).wait_recv()
                if d == 3 and from_y < 4:
                    ox_copy(2, left, from_y).start()
                if d == 1 and from_y >= 4:
                    ox_copy(3, right, from_y).start()
        for c in range(CH):
            width = min(128, HALF - 128 * c)
            piece = ox[from_x, :, OWN * c:OWN * (c + 1), :].reshape(NR, 128)
            slots[OV + d, :, 128 * c:128 * c + width] = piece[:, :width]
        for h in range(H):
            low(OV + d, h)

    ox_send(0)
    aside = {
        (1, 0): (lambda: (ox_send(1), ox_send(7))),
        (1, 1): (lambda: (ox_send(2), ox_send(6))),
        (2, 0): (lambda: (ox_send(3), ox_send(5), ox_send(4))),
        (2, 1): (lambda: ox_take(0)),
        (3, 0): (lambda: ox_take(3)),
        (3, 1): (lambda: ox_take(1)),
    }
    for k in (1, 2, 3):
        for h in range(H):
            ag_copy(0, k, h, up).wait_recv()
            if k < 3:
                ag_copy(k, k + 1, h, up).start()
            ag_copy(0, k + 3, h, dn).wait_recv()
            if k < 3:
                ag_copy(k + 3, k + 4, h, dn).start()
            else:
                ag_copy(far_from, FAR, h, far_to).start()
            low(k, h)
            low(k + 3, h)
            aside[k, h]()
    loads[7].wait()
    for h in range(H):
        ag_copy(far_from, FAR, h, far_to).wait_recv()
        low(FAR, h)

    def expert(slot_at, h):
        lo_copy(slot_at, h).wait_recv()
        inner = low_own[slot_at, rows(h)].astype(F32) + low_oth[slot_at, rows(h)].astype(F32)
        gate, upv = inner[:, :192], inner[:, 192:]
        active = ((upv + 1.0) * gate * jax.nn.sigmoid(1.702 * gate)).astype(BF)
        return dot(active, wout_v[...])

    def q_copy(slot_at, dst, h, head):
        return remote(
            qs.at[slot_at, rows(h)], racc.at[dst, rows(h)],
            q_ss.at[slot_at, h], q_rs.at[dst, h], s, head,
        )

    for h in range(H):
        qs[FAR, rows(h)] = expert(FAR, h).astype(BF)
        q_copy(FAR, FAR, h, far_back).start()
    ox_take(2)
    for h in range(H):
        below, above = expert(3, h), expert(6, h)
        q_copy(FAR, FAR, h, far_back).wait_recv()
        got = racc[FAR, rows(h)].astype(F32)
        qs[3, rows(h)] = (below + jnp.where(p == 0, got, 0.0)).astype(BF)
        q_copy(3, 2, h, dn).start()
        qs[6, rows(h)] = (above + jnp.where(p == 0, 0.0, got)).astype(BF)
        q_copy(6, 5, h, up).start()

    def of_copy(way):
        part = slice(0, 4) if way == 0 else slice(4, 8)
        return remote(
            obuf.at[2, part], ofar.at[part], or_ss.at[way], or_rs.at[way], at(y, left if way == 0 else right), z
        )

    def or_copy(way):
        return remote(
            obuf.at[3 - 2 * way], oret.at[way], or_ss.at[2 + way], or_rs.at[2 + way],
            at(y, left if way == 0 else right), z,
        )

    def oyr_copy(d):
        to = lax.rem(y + d, NY)
        return remote(osel.at[to], oyr.at[y], oyr_ss.at[d - 1], oyr_rs.at[y], at(to, x), z)

    def ozr_copy(d):
        to = lax.rem(z + d, NZ)
        return remote(ozs.at[to], ozr.at[z], ozr_ss.at[d - 1], ozr_rs.at[z], s, to)

    here = hot_x == x.astype(F32)

    def ov_expert(d):
        for h in range(H):
            value = expert(OV + d, h).astype(BF)
            n = SB // OWN
            for c in range(CH):
                piece = value[:, 128 * c:128 * (c + 1)]
                if piece.shape[1] < 128:
                    piece = jnp.concatenate([piece, jnp.zeros((SB, 128 * CH - HALF), BF)], axis=1)
                obuf[d, n * h:n * (h + 1), OWN * c:OWN * (c + 1), :] = piece.reshape(n, OWN, 128)

    def ov_far():
        ov_expert(2)
        for way in range(2):
            of_copy(way).start()

    def ov_near():
        for way in range(2):
            ov_expert(3 - 2 * way)
        for way in range(2):
            of_copy(way).wait_recv()
            for to_y in range(4 * way, 4 * way + 4):
                mixed = jnp.where(here, obuf[3 - 2 * way, to_y].astype(F32), ofar[to_y].astype(F32))
                obuf[3 - 2 * way, to_y] = mixed.astype(BF)
            or_copy(way).start()
        ov_expert(0)

    def ov_back_y():
        for way in range(2):
            or_copy(way).wait_recv()
        for to_y in range(NY):
            pass_by = 0 if to_y < 4 else 1
            acc = oret[pass_by, to_y].astype(F32)
            neighbour = left if to_y < 4 else right
            acc = jnp.where(hot_x == neighbour.astype(F32), oret[1 - pass_by, to_y].astype(F32), acc)
            osel[to_y] = jnp.where(here, obuf[0, to_y].astype(F32), acc).astype(BF)
        for d in range(1, NY):
            oyr_copy(d).start()

    def ov_back_z():
        acc = jnp.where(hot_y == y.astype(F32), osel[y].astype(F32), 0.0)
        for d in range(1, NY):
            from_y = lax.rem(y + d, NY)
            remote(osel.at[from_y], oyr.at[from_y], oyr_ss.at[d - 1], oyr_rs.at[from_y], at(from_y, x), z).wait_recv()
            acc = jnp.where(hot_y == from_y.astype(F32), oyr[from_y].astype(F32), acc)
        ozs[...] = dot(p2t[...], acc.astype(BF)).astype(BF).reshape(NZ, OM, 128)
        for d in range(1, NZ):
            ozr_copy(d).start()
        ozr[z] = ozs[z]

    ov_far()
    for k in (2, 1):
        for h in range(H):
            below, above = expert(k, h), expert(k + 3, h)
            q_copy(k, k, h, dn).wait_recv()
            qs[k, rows(h)] = (below + racc[k, rows(h)].astype(F32)).astype(BF)
            q_copy(k, k - 1, h, dn).start()
            q_copy(k + 3, k + 3, h, up).wait_recv()
            qs[k + 3, rows(h)] = (above + racc[k + 3, rows(h)].astype(F32)).astype(BF)
            q_copy(k + 3, k + 2, h, up).start()
        if k == 2:
            ov_near()
        else:
            ov_back_y()

    def a2_copy(r):
        to = near(r)
        return remote(sb2.at[r], rb2.at[chip], a2_ss.at[r], a2_rs.at[chip], to * 2 + p, z)

    for h in range(H):
        value = expert(0, h)
        q_copy(0, 0, h, dn).wait_recv()
        q_copy(0, 3, h, up).wait_recv()
        value = (value + racc[0, rows(h)].astype(F32) + racc[3, rows(h)].astype(F32)).astype(BF)
        for i in range(GH):
            g = h * GH + i
            part = value[GR * i:GR * (i + 1)]
            pieces = [part[:, 128 * c:128 * (c + 1)] for c in range(CH - 1)]
            last = part[:, 128 * (CH - 1):]
            pieces.append(jnp.concatenate([last, jnp.zeros((GR, 128 * CH - HALF), BF)], axis=1))
            out = dot(pt[...], jnp.concatenate(pieces, axis=0)).astype(BF)
            sb2[GS * g:GS * (g + 1)] = out.reshape(GS, MSG, 128)
            for r in range(GS * g, GS * (g + 1)):
                if r:
                    a2_copy(r).start()

    ov_back_z()
    rb2[chip] = sb2[0]
    for d in range(1, NZ):
        from_z = lax.rem(z + d, NZ)
        remote(ozs.at[from_z], ozr.at[from_z], ozr_ss.at[d - 1], ozr_rs.at[from_z], s, from_z).wait_recv()
    third_sum = jnp.sum(ozr[...].astype(F32), axis=0).astype(BF)

    @pl.loop(0, NC)
    def _(src):
        @pl.when(src != chip)
        def _():
            remote(sb2.at[src], rb2.at[src], a2_ss.at[0], a2_rs.at[src], src * 2 + p, z).wait_recv()

    out = dot(cm[...], rb2[...].reshape(NC * MSG, 128)) + dot(co[...], third_sum)
    out = out.astype(BF).reshape(CH, 2 * OWN, 128)
    cm_out = xbuf
    cm_out[...] = out
    theirs = pl.ds(pl.multiple_of((1 - p) * OWN, OWN), OWN)
    fsend[...] = cm_out[:, theirs, :]
    f_copy = remote(fsend, fin.at[p], f_ss, f_rs, other, z)
    f_copy.start()
    fin[p] = cm_out[:, mine, :]
    f_copy.wait_recv()
    esum_ref[...] = jnp.concatenate(
        [fin[h, c][:, :min(128, HALF - 128 * c)] for h in range(2) for c in range(CH)], axis=1
    )

    kv_copy.wait_send()
    info_copy.wait_send()
    st_copy.wait_send()
    f_copy.wait_send()
    for d in range(1, NZ):
        oz_copy(d).wait_send()
        oy_copy(d).wait_send()
        oyr_copy(d).wait_send()
        ozr_copy(d).wait_send()
        for c in range(NP):
            h_copy(d, d, c, up).wait_send()
    for way in range(2):
        of_copy(way).wait_send()
        or_copy(way).wait_send()
    for from_y in range(NY):
        ox_copy(0, x, from_y).wait_send()
        ox_copy(1, x, from_y).wait_send()
        ox_copy(2 if from_y < 4 else 3, x, from_y).wait_send()
    for r in range(1, NC):
        a1_copy(r).wait_send()
        a2_copy(r).wait_send()

    for slot_at in range(OV + NX):
        for h in range(H):
            lo_copy(slot_at, h).wait_send()
            if 0 < slot_at < OV:
                ag_copy(0, slot_at, h, up).wait_send()
                q_copy(slot_at, slot_at, h, up).wait_send()


def deliver(stream_in, esum_in, stream_out, esum_out):
    stream_out[...] = stream_in[...]
    esum_out[...] = esum_in[...]


def per_device(q, kv, wo, res, gain, ids, weights, w_in, w_out):
    vm = pltpu.VMEM
    dma = pltpu.SemaphoreType.DMA
    scratch = [
        vm((TOK, 512), BF), vm((2, TOK, 128), BF), vm((D, 512), BF), vm((OWN, D), BF), vm((D,), F32),
        vm((TOP, TOK), I32), vm((TOP, TOK), BF), vm((2 * TOP, TOK), F32), vm((2, OWN, 128), F32), vm((HALF, 384), BF), vm((192, HALF), BF),
        vm((TOK, 512), BF), vm((NZ, OWN, D), F32), vm((NZ, OWN, D), BF), vm((NZ, OWN, D), BF),
        vm((2, CH, OWN, 128), BF), vm((CH, 2 * OWN, 128), BF),
        vm((NC * MSG, CH * 2 * OWN), BF), vm((CH * 2 * OWN, NC * MSG), BF),
        vm((CH * GR, GS * MSG), BF), vm((GS * MSG, CH * GR), BF),
        vm((NC, MSG, 128), BF), vm((NC, MSG, 128), BF),
        vm((OV + NX, NR, HALF), BF), vm((OV + NX, NR, 384), BF), vm((OV + NX, NR, 384), BF),
        vm((8, NR, HALF), BF), vm((8, NR, HALF), BF),
        vm((NC, MSG, 128), BF), vm((NC, MSG, 128), BF),
        vm((2, CH, OWN, 128), BF), vm((CH, OWN, 128), BF),
        vm((OM, CH * 2 * OWN), BF), vm((CH * 2 * OWN, OM), BF), vm((OB, NZ * OM), BF), vm((NZ * OM, OB), BF),
        vm((OM, 128), BF), vm((NZ, OM, 128), BF), vm((NX, NY, OB, 128), BF), vm((NX, NY, OB, 128), BF),
        vm((NY, OB, 128), BF), vm((2, NY, OB, 128), BF), vm((NY, OB, 128), BF), vm((NY, OB, 128), BF),
        vm((NZ, OM, 128), BF), vm((NZ, OM, 128), BF),
        dma((9,)), dma, dma, dma, dma, dma((NZ, NP)), dma((NZ, NP)), dma, dma,
        dma((NC,)), dma((NC,)), dma((8, H)), dma((8, H)), dma((OV + NX, H)), dma((OV + NX, H)),
        dma((8, H)), dma((8, H)), dma((NC,)), dma((NC,)), dma, dma,
        dma((NZ,)), dma((NZ,)), dma((NY,)), dma((NY,)), dma((NX, NY)), dma((NX, NY)), dma((NX,)), dma((NX,)),
        dma((NY,)), dma((NY,)), dma((NZ,)), dma((NZ,)),
    ]
    made = pl.pallas_call(
        kernel,
        out_shape=(jax.ShapeDtypeStruct((OWN, D), BF), jax.ShapeDtypeStruct((OWN, D), BF)),
        in_specs=[pl.BlockSpec(memory_space=pl.ANY)] * 9,
        out_specs=(pl.BlockSpec(memory_space=vm), pl.BlockSpec(memory_space=vm)),
        scratch_shapes=scratch,
        compiler_params=pltpu.CompilerParams(
            collective_id=0, has_side_effects=True, vmem_limit_bytes=58 * 1024 * 1024
        ),
        cost_estimate=pl.CostEstimate(flops=4_000_000_000, bytes_accessed=8_000_000, transcendentals=300_000),
    )(q, kv.reshape(TOK, 128), wo.T, res, gain, ids.T, weights.T, w_in, w_out)
    return pl.pallas_call(
        deliver,
        out_shape=(jax.ShapeDtypeStruct((OWN, D), BF), jax.ShapeDtypeStruct((OWN, D), BF)),
        in_specs=[pl.BlockSpec(memory_space=vm)] * 2,
        out_specs=(pl.BlockSpec(memory_space=vm), pl.BlockSpec(memory_space=vm)),
    )(*made)


def solution(mesh):
    placed = (
        P("seq", "head"), P("seq", "head", None), P("head", None), P(("seq", "head"), None), P(),
        P("seq", None), P("seq", None), P("seq", None, "head"), P("seq", "head", None),
    )
    return jax.shard_map(
        per_device, mesh=mesh, in_specs=placed,
        out_specs=(P(("seq", "head"), None), P(("seq", "head"), None)), check_vma=False,
    )
```

```python
import jax
import jax.numpy as jnp
from jax import lax
from jax.experimental import pallas as pl
from jax.experimental.pallas import tpu as pltpu
from jax.sharding import PartitionSpec as P

MESH = pl.DeviceIdType.MESH
BF = jnp.bfloat16
F32 = jnp.float32
I32 = jnp.int32

NS, NZ = 64, 8
NC = NS // 2
TOK, OWN, TOP = 128, 16, 4
D, HALF, CH = 2880, 1440, 12
NX, NY = 4, 8
R = 4
CAP = R // 2
MSG = 48
GS, GR = 4, 16
NR = NC * R
H = 2
SB = NR // H
GH = SB // GR
FAR = 7
WHOLE = HALF // 128
TAIL = WHOLE * SB
PACK = TAIL + SB // 4
OV = 8
OM = 32
PIECES = ((0, 1024), (1024, 2048), (2048, D))
NP = len(PIECES)
OB = CH * OWN

NEAR = sorted(
    [(dy, dx) for dy in range(-3, 5) for dx in range(-1, 3)], key=lambda o: (abs(o[0]) + abs(o[1]), o)
)
SEEN = [NEAR.index(((3 - dy) % NY - 3, (1 - dx) % NX - 1)) for dy, dx in NEAR]


def idiv(v, n):
    if n & (n - 1) == 0:
        return lax.shift_right_logical(v, jnp.full_like(v, n.bit_length() - 1))
    return ((v.astype(F32) + 0.5) * (1.0 / n)).astype(I32)


def imod(v, n):
    return v - idiv(v, n) * n


def iota(shape, dim):
    return lax.broadcasted_iota(I32, shape, dim)


def dot(a, b):
    return jnp.dot(a, b, preferred_element_type=F32)


def dot_nt(a, b):
    return lax.dot_general(a, b, (((1,), (1,)), ((), ())), preferred_element_type=F32)


def ones(cond):
    return jnp.where(cond, 1.0, 0.0).astype(BF)


def pack(value):
    part = SB // 4
    last = [value[part * j:part * (j + 1), 128 * WHOLE:] for j in range(4)]
    whole = [value[:, 128 * c:128 * (c + 1)] for c in range(WHOLE)]
    return jnp.concatenate(whole + [jnp.concatenate(last, axis=1)], axis=0)


def unpack(packed):
    last = [packed[TAIL:, 32 * j:32 * (j + 1)] for j in range(4)]
    whole = [packed[SB * c:SB * (c + 1)] for c in range(WHOLE)]
    return jnp.concatenate(whole + [jnp.concatenate(last, axis=0)], axis=1)


def kernel(
    q_hbm, kv_hbm, wo_hbm, res_hbm, gain_hbm, ids_hbm, rw_hbm, win_hbm, wout_hbm,
    stream_ref, esum_ref,
    q_v, kv2, wo_v, res_v, gain_v, ids_v, rw_v, both, info2, win_v, wout_v,
    att_v, own_f, ps, rs, stage, xbuf, dm, cm, pm, pt,
    sb1, rb1, slots, low_own, low_oth, qs, racc, sb2, rb2, fin, fsend,
    om, co, p2, p2t, osend, oz, ox, obuf, ofar, oret, osel, oyr, ozs, ozr,
    load_sem, kv_ss, kv_rs, info_ss, info_rs, rs_ss, rs_rs, st_ss, st_rs,
    a1_ss, a1_rs, ag_ss, ag_rs, lo_ss, lo_rs, q_ss, q_rs, a2_ss, a2_rs, f_ss, f_rs,
    oz_ss, oz_rs, oy_ss, oy_rs, ox_ss, ox_rs, or_ss, or_rs, oyr_ss, oyr_rs, ozr_ss, ozr_rs,
):
    s = lax.axis_index("seq")
    z = lax.axis_index("head")
    p = lax.rem(s, 2)
    chip = lax.div(s, 2)
    x = lax.rem(chip, NX)
    y = lax.div(chip, NX)
    other = s + 1 - 2 * p
    nxt = lax.rem(s + 1, NS)
    prv = lax.rem(s + NS - 1, NS)
    up = lax.rem(z + 1, NZ)
    dn = lax.rem(z + NZ - 1, NZ)

    loads = [
        pltpu.make_async_copy(src, dst, load_sem.at[i])
        for i, (src, dst) in enumerate(
            [
                (kv_hbm, kv2.at[1]),
                (q_hbm, q_v),
                (ids_hbm, ids_v),
                (wo_hbm, wo_v),
                (res_hbm, res_v),
                (gain_hbm, gain_v),
                (win_hbm.at[0], win_v),
                (wout_hbm.at[0], wout_v),
                (rw_hbm, rw_v),
            ]
        )
    ]
    for c in loads:
        c.start()

    barrier = pltpu.get_barrier_semaphore()

    def greet(seq, head):
        pl.semaphore_signal(barrier, inc=1, device_id=(seq, head), device_id_type=MESH)

    greet(other, z)
    greet(prv, z)

    @pl.loop(1, NZ)
    def _(d):
        greet(s, lax.rem(z + d, NZ))

    @pl.loop(1, NC)
    def _(d):
        greet(lax.rem(chip + d, NC) * 2 + p, z)

    pl.semaphore_wait(barrier, 1 + 1 + (NZ - 1) + (NC - 1))

    def remote(src, dst, ss, rs_, seq, head):
        return pltpu.make_async_remote_copy(
            src_ref=src, dst_ref=dst, send_sem=ss, recv_sem=rs_,
            device_id=(seq, head), device_id_type=MESH,
        )

    loads[0].wait()
    kv_copy = remote(kv2.at[1], kv2.at[0], kv_ss, kv_rs, nxt, z)
    kv_copy.start()
    loads[2].wait()
    loads[8].wait()
    both[0:TOP] = ids_v[...].astype(F32)
    both[TOP:] = rw_v[...].astype(F32)
    chosen = ones(iota((OWN, TOK), 1) == iota((OWN, TOK), 0) + z * OWN)
    info2[p, :, 0:2 * TOP] = dot_nt(chosen, both[...].astype(BF))
    info_copy = remote(info2.at[p], info2.at[p], info_ss, info_rs, other, z)
    info_copy.start()
    def perm2(shape, a_dim):
        i, j = iota(shape, a_dim), iota(shape, 1 - a_dim)
        inner = imod(j, OM)
        return ones(
            (idiv(i, OWN) == idiv(inner, 2))
            & (idiv(imod(i, OWN), 2) == idiv(j, OM))
            & (imod(i, 2) == imod(inner, 2))
        )

    p2[...] = perm2((OB, NZ * OM), 0)
    p2t[...] = perm2((NZ * OM, OB), 1)

    def perm(shape, a_dim):
        i, j = iota(shape, a_dim), iota(shape, 1 - a_dim)
        inner = imod(j, MSG)
        return ones(
            (idiv(i, GR) == idiv(inner, R))
            & (idiv(imod(i, GR), R) == idiv(j, MSG))
            & (imod(i, R) == imod(inner, R))
            & (inner < CH * R)
        )

    pm[...] = perm((CH * GR, GS * MSG), 0)
    pt[...] = perm((GS * MSG, CH * GR), 1)
    loads[1].wait()
    kv_copy.wait_recv()

    kvf = kv2[...].reshape(2 * TOK, 128).astype(F32)
    lane = iota((2 * TOK, 128), 1)
    turned = pltpu.roll(kvf, 64, 1)
    k_even = jnp.where(lane < 64, kvf, 0.0).astype(BF)
    k_odd = jnp.where(lane >= 64, turned, 0.0).astype(BF)
    v_even = jnp.where(lane < 64, turned, 0.0).astype(BF)
    v_odd = jnp.where(lane >= 64, kvf, 0.0).astype(BF)
    qpos = iota((TOK, 2 * TOK), 0)
    kpos = iota((TOK, 2 * TOK), 1)
    allowed = (kpos > qpos) & (kpos <= qpos + TOK) & (s * TOK - TOK + kpos >= 0)
    for pair in range(4):
        qp = q_v[:, 128 * pair:128 * (pair + 1)]
        acc = None
        for kk, vv in ((k_even, v_even), (k_odd, v_odd)):
            sc = jnp.where(allowed, dot_nt(qp, kk) * 0.125, -1e30)
            ex = jnp.exp(sc - jnp.max(sc, axis=-1, keepdims=True))
            w = (ex / jnp.sum(ex, axis=-1, keepdims=True)).astype(BF)
            part = dot(w, vv)
            acc = part if acc is None else acc + part
        att_v[:, 128 * pair:128 * (pair + 1)] = acc.astype(BF)

    far_from = 3 + 3 * p
    far_to = lax.rem(z + 1 + (NZ - 2) * p, NZ)
    far_back = lax.rem(z + NZ - 1 + 2 * p, NZ)

    def h_copy(slot_at, dst, c, head):
        lo, hi = PIECES[c]
        return remote(
            ps.at[slot_at, :, lo:hi], rs.at[dst, :, lo:hi], rs_ss.at[slot_at, c], rs_rs.at[dst, c], s, head
        )

    def block(d, c):
        lo, hi = PIECES[c]
        return own_f[lax.rem(z + d + NZ, NZ), :, lo:hi]

    def got_h(dst, c):
        lo, hi = PIECES[c]
        h_copy(FAR, dst, c, up).wait_recv()
        return rs[dst, :, lo:hi].astype(F32)

    def send_h(slot_at, dst, c, head, value):
        lo, hi = PIECES[c]
        ps[slot_at, :, lo:hi] = value.astype(BF)
        h_copy(slot_at, dst, c, head).start()

    loads[3].wait()
    for c, (lo, hi) in enumerate(PIECES):
        for n0 in range(lo, hi, 512):
            n1 = min(hi, n0 + 512)
            own_f[:, :, n0:n1] = dot_nt(att_v[...], wo_v[n0:n1]).reshape(NZ, OWN, n1 - n0)
        send_h(FAR, FAR, c, far_back, block(4, c))

    info_copy.wait_recv()
    inf = info2[...].reshape(2 * OWN, 128)
    lanes = iota((2 * OWN, 128), 1).astype(F32)
    named = jnp.zeros((2 * OWN, 128), F32)
    weight = jnp.zeros((2 * OWN, 128), F32)
    for k in range(TOP):
        hit = inf[:, k:k + 1] == lanes
        named = named + jnp.where(hit, 1.0, 0.0)
        weight = weight + jnp.where(hit, inf[:, TOP + k:TOP + k + 1], 0.0)
    named, weight = named.astype(BF), weight.astype(BF)
    ta, tb = iota((2 * OWN, 2 * OWN), 0), iota((2 * OWN, 2 * OWN), 1)
    before = ones((tb < ta) & (idiv(tb, OWN) == idiv(ta, OWN)))
    slot = dot(before, named).astype(BF)
    ra = iota((NC * R, 128), 0)
    expand = ones(idiv(ra, R) == iota((NC * R, 128), 1))

    for c in range(NP):
        got = got_h(FAR, c)
        send_h(3, 2, c, dn, block(-3, c) + jnp.where(p == 0, got, 0.0))
        send_h(6, 5, c, up, block(3, c) + jnp.where(p == 0, 0.0, got))

    r_i = imod(iota((NC * R, 2 * OWN), 0), R)
    t_i = iota((NC * R, 2 * OWN), 1)
    want = r_i - idiv(r_i, CAP) * CAP
    picked = (
        (dot_nt(expand, named) > 0.5)
        & (dot_nt(expand, slot) == want.astype(F32))
        & (idiv(t_i, OWN) == idiv(r_i, CAP))
    )
    spread = ones(iota((2 * OWN, CH * 2 * OWN), 0) == imod(iota((2 * OWN, CH * 2 * OWN), 1), 2 * OWN))
    wide = dot(ones(picked), spread).astype(BF)
    m_i = iota((NC * MSG, NC * R), 0)
    rest = imod(m_i, MSG)
    rows_of = ones(
        (idiv(m_i, MSG) * R + imod(rest, R) == iota((NC * MSG, NC * R), 1)) & (rest < CH * R)
    )
    mm = iota((MSG, CH * 2 * OWN), 0)
    chunk_ok = jnp.where(idiv(mm, R) == idiv(iota((MSG, CH * 2 * OWN), 1), 2 * OWN), 1.0, 0.0)
    full = dot(rows_of, wide).reshape(NC, MSG, CH * 2 * OWN) * chunk_ok[None]
    dm[...] = full.reshape(NC * MSG, CH * 2 * OWN).astype(BF)


    for c in range(NP):
        send_h(2, 1, c, dn, block(-2, c) + got_h(2, c))
        send_h(5, 4, c, up, block(2, c) + got_h(5, c))

    third = jnp.where((named > 0.5) & (slot > 1.5), 1.0, 0.0)
    third_row = dot_nt(jnp.ones((8, 128), BF), third.astype(BF))[0:1]
    third_wide = dot(jnp.broadcast_to(third_row, (8, 2 * OWN)).astype(BF), spread)[0:1]
    o_m, o_q = iota((OM, CH * 2 * OWN), 0), iota((OM, CH * 2 * OWN), 1)
    o_ok = (idiv(o_m, 2) == idiv(o_q, 2 * OWN)) & (imod(o_m, 2) == imod(idiv(o_q, OWN), 2))
    om[...] = jnp.where(o_ok, third_wide, 0.0).astype(BF)
    hot = jnp.max(third, axis=0, keepdims=True)
    e_row = iota((1, 128), 1)
    hot_x = jnp.sum(hot * imod(e_row, NX).astype(F32), axis=1, keepdims=True)
    hot_y = jnp.sum(hot * idiv(e_row, NX).astype(F32), axis=1, keepdims=True)


    for c in range(NP):
        send_h(1, 0, c, dn, block(-1, c) + got_h(1, c))
        send_h(4, 3, c, up, block(1, c) + got_h(4, c))

    loads[4].wait()
    loads[5].wait()
    total = jnp.concatenate([block(0, c) + (got_h(0, c) + got_h(3, c)) for c in range(NP)], axis=1)
    total = total + res_v[...].astype(F32)
    stream_ref[...] = total.astype(BF)
    mean_square = jnp.mean(total * total, axis=-1, keepdims=True)
    normed = (total * lax.rsqrt(mean_square + 1e-5) * gain_v[...].reshape(1, D)).astype(BF)
    for h in range(2):
        for c in range(CH):
            lo = h * HALF + c * 128
            hi = min(lo + 128, (h + 1) * HALF)
            piece = normed[:, lo:hi]
            if hi - lo < 128:
                piece = jnp.concatenate([piece, jnp.zeros((OWN, 128 - hi + lo), BF)], axis=1)
            stage[h, c] = piece
    mine = pl.ds(pl.multiple_of(p * OWN, OWN), OWN)
    st_copy = remote(stage.at[1 - p], xbuf.at[:, mine, :], st_ss, st_rs, other, z)
    st_copy.start()
    xbuf[:, mine, :] = stage[p]
    st_copy.wait_recv()

    osend[...] = dot(om[...], xbuf[...].reshape(CH * 2 * OWN, 128)).astype(BF)

    def oz_copy(d):
        return remote(osend, oz.at[z], oz_ss.at[d - 1], oz_rs.at[z], s, lax.rem(z + d, NZ))

    for d in range(1, NZ):
        oz_copy(d).start()
    oz[z] = osend[...]

    def at(y_, x_):
        return (y_ * NX + x_) * 2 + p

    msgs = dot(dm[...], xbuf[...].reshape(CH * 2 * OWN, 128)).astype(BF)
    sb1[...] = msgs.reshape(NC, MSG, 128)

    def near(r):
        dy, dx = NEAR[r]
        return lax.rem(y + dy + NY, NY) * NX + lax.rem(x + dx + NX, NX)

    def a1_copy(r):
        to = near(r)
        return remote(sb1.at[to], rb1.at[SEEN[r]], a1_ss.at[r], a1_rs.at[SEEN[r]], to * 2 + p, z)

    for r in range(1, NC):
        a1_copy(r).start()
    rb1[0] = sb1[chip]

    e_l = iota((2 * OWN, NC * R), 1)
    r_l = imod(e_l, R)
    back = ones(iota((128, NC * R), 0) == idiv(iota((128, NC * R), 1), R))
    take = (dot(slot, back) == (r_l - idiv(r_l, CAP) * CAP).astype(F32)) & (
        idiv(iota((2 * OWN, NC * R), 0), OWN) == idiv(r_l, CAP)
    )
    w_t = jnp.where(take, dot(weight, back), 0.0).astype(BF)
    spread_t = ones(iota((CH * 2 * OWN, 2 * OWN), 1) == imod(iota((CH * 2 * OWN, 2 * OWN), 0), 2 * OWN))
    tall = dot(spread_t, w_t).astype(BF)
    m_l = iota((NC * R, NC * MSG), 1)
    rest_l = imod(m_l, MSG)
    cols_of = ones(
        (idiv(m_l, MSG) * R + imod(rest_l, R) == iota((NC * R, NC * MSG), 0)) & (rest_l < CH * R)
    )
    full_t = dot(tall, cols_of)
    c_l = idiv(imod(iota((CH * 2 * OWN, NC * MSG), 1), MSG), R)
    w_third = jnp.sum(third * weight.astype(F32), axis=1, keepdims=True)
    w_tall = dot(spread_t, jnp.broadcast_to(w_third, (2 * OWN, 128)).astype(BF))[:, :OM]
    o_q, o_m = iota((CH * 2 * OWN, OM), 0), iota((CH * 2 * OWN, OM), 1)
    o_ok = (idiv(o_m, 2) == idiv(o_q, 2 * OWN)) & (imod(o_m, 2) == imod(idiv(o_q, OWN), 2))
    co[...] = jnp.where(o_ok, w_tall, 0.0).astype(BF)
    cm[...] = jnp.where(c_l == idiv(iota((CH * 2 * OWN, NC * MSG), 0), 2 * OWN), full_t, 0.0).astype(BF)

    def a1_wait(r):
        if r:
            a1_copy(SEEN[r]).wait_recv()

    def rows(h):
        return pl.ds(h * SB, SB)

    def ag_copy(src, dst, h, head):
        return remote(
            slots.at[src, h], slots.at[dst, h],
            ag_ss.at[dst, h], ag_rs.at[dst, h], s, head,
        )

    def lo_copy(slot_at, h):
        return remote(
            low_own.at[slot_at, rows(h)], low_oth.at[slot_at, rows(h)],
            lo_ss.at[slot_at, h], lo_rs.at[slot_at, h], other, z,
        )

    def low(slot_at, h):
        low_own[slot_at, rows(h)] = dot(unpack(slots[slot_at, h]), win_v[...]).astype(BF)
        lo_copy(slot_at, h).start()

    for h in range(H):
        for g in range(h * GH, (h + 1) * GH):
            for i in range(GS):
                a1_wait(g * GS + i)
            got = dot(pm[...], rb1[GS * g:GS * (g + 1)].reshape(GS * MSG, 128)).astype(BF)
            i = g - h * GH
            for c in range(WHOLE):
                slots[0, h, SB * c + GR * i:SB * c + GR * (i + 1)] = got[GR * c:GR * (c + 1)]
            slots[0, h, TAIL:, 32 * i:32 * (i + 1)] = got[GR * WHOLE:, :32]
        ag_copy(0, 1, h, up).start()
        ag_copy(0, 4, h, dn).start()
    for d in range(1, NZ):
        from_z = lax.rem(z + d, NZ)
        remote(osend, oz.at[from_z], oz_ss.at[d - 1], oz_rs.at[from_z], s, from_z).wait_recv()
    ox[x, y] = dot(p2[...], oz[...].reshape(NZ * OM, 128)).astype(BF)

    def oy_copy(d):
        to = lax.rem(y + d, NY)
        return remote(ox.at[x, y], ox.at[x, y], oy_ss.at[d - 1], oy_rs.at[y], at(to, x), z)

    for d in range(1, NY):
        oy_copy(d).start()

    loads[6].wait()
    for h in range(H):
        low(0, h)

    right, left = lax.rem(x + 1, NX), lax.rem(x + NX - 1, NX)

    def ox_copy(way, from_x, from_y):
        return remote(
            ox.at[from_x, from_y], ox.at[from_x, from_y], ox_ss.at[way, from_y], ox_rs.at[from_x, from_y],
            at(y, right if way in (0, 2) else left), z,
        )

    def ox_send(dy):
        from_y = lax.rem(y + dy, NY)
        if dy:
            remote(
                ox.at[x, from_y], ox.at[x, from_y], ox_ss.at[0, from_y], oy_rs.at[from_y], at(from_y, x), z
            ).wait_recv()
        ox_copy(0, x, from_y).start()
        ox_copy(1, x, from_y).start()

    def ox_take(d):
        from_x = lax.rem(x + d, NX)
        if d:
            for from_y in range(NY):
                ox_copy(0, from_x, from_y).wait_recv()
                if d == 3 and from_y < 4:
                    ox_copy(2, left, from_y).start()
                if d == 1 and from_y >= 4:
                    ox_copy(3, right, from_y).start()
        for h in range(H):
            for c in range(WHOLE):
                piece = ox[from_x, 4 * h:4 * (h + 1), OWN * c:OWN * (c + 1), :]
                slots[OV + d, h, SB * c:SB * (c + 1)] = piece.reshape(SB, 128)
            for j in range(4):
                slots[OV + d, h, TAIL:, 32 * j:32 * (j + 1)] = ox[from_x, 4 * h + j, OWN * WHOLE:, :][:, :32]
            low(OV + d, h)

    ox_send(0)
    aside = {
        (1, 0): (lambda: (ox_send(1), ox_send(7))),
        (1, 1): (lambda: (ox_send(2), ox_send(6))),
        (2, 0): (lambda: (ox_send(3), ox_send(5), ox_send(4))),
        (2, 1): (lambda: ox_take(0)),
        (3, 0): (lambda: ox_take(3)),
        (3, 1): (lambda: ox_take(1)),
    }
    for k in (1, 2, 3):
        for h in range(H):
            ag_copy(0, k, h, up).wait_recv()
            if k < 3:
                ag_copy(k, k + 1, h, up).start()
            ag_copy(0, k + 3, h, dn).wait_recv()
            if k < 3:
                ag_copy(k + 3, k + 4, h, dn).start()
            else:
                ag_copy(far_from, FAR, h, far_to).start()
            low(k, h)
            low(k + 3, h)
            aside[k, h]()
    loads[7].wait()
    for h in range(H):
        ag_copy(far_from, FAR, h, far_to).wait_recv()
        low(FAR, h)

    def expert(slot_at, h):
        lo_copy(slot_at, h).wait_recv()
        inner = low_own[slot_at, rows(h)].astype(F32) + low_oth[slot_at, rows(h)].astype(F32)
        gate, upv = inner[:, :192], inner[:, 192:]
        active = ((upv + 1.0) * gate * jax.nn.sigmoid(1.702 * gate)).astype(BF)
        return pack(dot(active, wout_v[...]))

    def q_copy(slot_at, dst, h, head):
        return remote(
            qs.at[slot_at, h], racc.at[dst, h],
            q_ss.at[slot_at, h], q_rs.at[dst, h], s, head,
        )

    for h in range(H):
        qs[FAR, h] = expert(FAR, h).astype(BF)
        q_copy(FAR, FAR, h, far_back).start()
    ox_take(2)
    for h in range(H):
        below, above = expert(3, h), expert(6, h)
        q_copy(FAR, FAR, h, far_back).wait_recv()
        got = racc[FAR, h].astype(F32)
        qs[3, h] = (below + jnp.where(p == 0, got, 0.0)).astype(BF)
        q_copy(3, 2, h, dn).start()
        qs[6, h] = (above + jnp.where(p == 0, 0.0, got)).astype(BF)
        q_copy(6, 5, h, up).start()

    def of_copy(way):
        part = slice(0, 4) if way == 0 else slice(4, 8)
        return remote(
            obuf.at[2, part], ofar.at[part], or_ss.at[way], or_rs.at[way], at(y, left if way == 0 else right), z
        )

    def or_copy(way):
        return remote(
            obuf.at[3 - 2 * way], oret.at[way], or_ss.at[2 + way], or_rs.at[2 + way],
            at(y, left if way == 0 else right), z,
        )

    def oyr_copy(d):
        to = lax.rem(y + d, NY)
        return remote(osel.at[to], oyr.at[y], oyr_ss.at[d - 1], oyr_rs.at[y], at(to, x), z)

    def ozr_copy(d):
        to = lax.rem(z + d, NZ)
        return remote(ozs.at[to], ozr.at[z], ozr_ss.at[d - 1], ozr_rs.at[z], s, to)

    here = hot_x == x.astype(F32)

    def ov_expert(d):
        for h in range(H):
            value = expert(OV + d, h).astype(BF)
            for c in range(WHOLE):
                piece = value[SB * c:SB * (c + 1)]
                obuf[d, 4 * h:4 * (h + 1), OWN * c:OWN * (c + 1), :] = piece.reshape(4, OWN, 128)
            for j in range(4):
                last = [value[TAIL:, 32 * j:32 * (j + 1)], jnp.zeros((OWN, 96), BF)]
                obuf[d, 4 * h + j, OWN * WHOLE:, :] = jnp.concatenate(last, axis=1)

    def ov_far():
        ov_expert(2)
        for way in range(2):
            of_copy(way).start()

    def ov_near():
        for way in range(2):
            ov_expert(3 - 2 * way)
        for way in range(2):
            of_copy(way).wait_recv()
            for to_y in range(4 * way, 4 * way + 4):
                mixed = jnp.where(here, obuf[3 - 2 * way, to_y].astype(F32), ofar[to_y].astype(F32))
                obuf[3 - 2 * way, to_y] = mixed.astype(BF)
            or_copy(way).start()
        ov_expert(0)

    def ov_back_y():
        for way in range(2):
            or_copy(way).wait_recv()
        for to_y in range(NY):
            pass_by = 0 if to_y < 4 else 1
            acc = oret[pass_by, to_y].astype(F32)
            neighbour = left if to_y < 4 else right
            acc = jnp.where(hot_x == neighbour.astype(F32), oret[1 - pass_by, to_y].astype(F32), acc)
            osel[to_y] = jnp.where(here, obuf[0, to_y].astype(F32), acc).astype(BF)
        for d in range(1, NY):
            oyr_copy(d).start()

    def ov_back_z():
        acc = jnp.where(hot_y == y.astype(F32), osel[y].astype(F32), 0.0)
        for d in range(1, NY):
            from_y = lax.rem(y + d, NY)
            remote(osel.at[from_y], oyr.at[from_y], oyr_ss.at[d - 1], oyr_rs.at[from_y], at(from_y, x), z).wait_recv()
            acc = jnp.where(hot_y == from_y.astype(F32), oyr[from_y].astype(F32), acc)
        ozs[...] = dot(p2t[...], acc.astype(BF)).astype(BF).reshape(NZ, OM, 128)
        for d in range(1, NZ):
            ozr_copy(d).start()
        ozr[z] = ozs[z]

    ov_far()
    for k in (2, 1):
        for h in range(H):
            below, above = expert(k, h), expert(k + 3, h)
            q_copy(k, k, h, dn).wait_recv()
            qs[k, h] = (below + racc[k, h].astype(F32)).astype(BF)
            q_copy(k, k - 1, h, dn).start()
            q_copy(k + 3, k + 3, h, up).wait_recv()
            qs[k + 3, h] = (above + racc[k + 3, h].astype(F32)).astype(BF)
            q_copy(k + 3, k + 2, h, up).start()
        if k == 2:
            ov_near()
        else:
            ov_back_y()

    def a2_copy(r):
        to = near(r)
        return remote(sb2.at[r], rb2.at[chip], a2_ss.at[r], a2_rs.at[chip], to * 2 + p, z)

    for h in range(H):
        value = expert(0, h)
        q_copy(0, 0, h, dn).wait_recv()
        q_copy(0, 3, h, up).wait_recv()
        value = (value + racc[0, h].astype(F32) + racc[3, h].astype(F32)).astype(BF)
        for i in range(GH):
            g = h * GH + i
            pieces = [value[SB * c + GR * i:SB * c + GR * (i + 1)] for c in range(WHOLE)]
            last = value[TAIL:, 32 * i:32 * (i + 1)]
            pieces.append(jnp.concatenate([last, jnp.zeros((GR, 128 * CH - HALF), BF)], axis=1))
            out = dot(pt[...], jnp.concatenate(pieces, axis=0)).astype(BF)
            sb2[GS * g:GS * (g + 1)] = out.reshape(GS, MSG, 128)
            for r in range(GS * g, GS * (g + 1)):
                if r:
                    a2_copy(r).start()

    ov_back_z()
    rb2[chip] = sb2[0]
    for d in range(1, NZ):
        from_z = lax.rem(z + d, NZ)
        remote(ozs.at[from_z], ozr.at[from_z], ozr_ss.at[d - 1], ozr_rs.at[from_z], s, from_z).wait_recv()
    third_sum = jnp.sum(ozr[...].astype(F32), axis=0).astype(BF)

    @pl.loop(0, NC)
    def _(src):
        @pl.when(src != chip)
        def _():
            remote(sb2.at[src], rb2.at[src], a2_ss.at[0], a2_rs.at[src], src * 2 + p, z).wait_recv()

    out = dot(cm[...], rb2[...].reshape(NC * MSG, 128)) + dot(co[...], third_sum)
    out = out.astype(BF).reshape(CH, 2 * OWN, 128)
    cm_out = xbuf
    cm_out[...] = out
    theirs = pl.ds(pl.multiple_of((1 - p) * OWN, OWN), OWN)
    fsend[...] = cm_out[:, theirs, :]
    f_copy = remote(fsend, fin.at[p], f_ss, f_rs, other, z)
    f_copy.start()
    fin[p] = cm_out[:, mine, :]
    f_copy.wait_recv()
    esum_ref[...] = jnp.concatenate(
        [fin[h, c][:, :min(128, HALF - 128 * c)] for h in range(2) for c in range(CH)], axis=1
    )

    kv_copy.wait_send()
    info_copy.wait_send()
    st_copy.wait_send()
    f_copy.wait_send()
    for d in range(1, NZ):
        oz_copy(d).wait_send()
        oy_copy(d).wait_send()
        oyr_copy(d).wait_send()
        ozr_copy(d).wait_send()
        for c in range(NP):
            h_copy(d, d, c, up).wait_send()
    for way in range(2):
        of_copy(way).wait_send()
        or_copy(way).wait_send()
    for from_y in range(NY):
        ox_copy(0, x, from_y).wait_send()
        ox_copy(1, x, from_y).wait_send()
        ox_copy(2 if from_y < 4 else 3, x, from_y).wait_send()
    for r in range(1, NC):
        a1_copy(r).wait_send()
        a2_copy(r).wait_send()

    for slot_at in range(OV + NX):
        for h in range(H):
            lo_copy(slot_at, h).wait_send()
            if 0 < slot_at < OV:
                ag_copy(0, slot_at, h, up).wait_send()
                q_copy(slot_at, slot_at, h, up).wait_send()


def deliver(stream_in, esum_in, stream_out, esum_out):
    stream_out[...] = stream_in[...]
    esum_out[...] = esum_in[...]


def per_device(q, kv, wo, res, gain, ids, weights, w_in, w_out):
    vm = pltpu.VMEM
    dma = pltpu.SemaphoreType.DMA
    scratch = [
        vm((TOK, 512), BF), vm((2, TOK, 128), BF), vm((D, 512), BF), vm((OWN, D), BF), vm((D,), F32),
        vm((TOP, TOK), I32), vm((TOP, TOK), BF), vm((2 * TOP, TOK), F32), vm((2, OWN, 128), F32), vm((HALF, 384), BF), vm((192, HALF), BF),
        vm((TOK, 512), BF), vm((NZ, OWN, D), F32), vm((NZ, OWN, D), BF), vm((NZ, OWN, D), BF),
        vm((2, CH, OWN, 128), BF), vm((CH, 2 * OWN, 128), BF),
        vm((NC * MSG, CH * 2 * OWN), BF), vm((CH * 2 * OWN, NC * MSG), BF),
        vm((CH * GR, GS * MSG), BF), vm((GS * MSG, CH * GR), BF),
        vm((NC, MSG, 128), BF), vm((NC, MSG, 128), BF),
        vm((OV + NX, H, PACK, 128), BF), vm((OV + NX, NR, 384), BF), vm((OV + NX, NR, 384), BF),
        vm((8, H, PACK, 128), BF), vm((8, H, PACK, 128), BF),
        vm((NC, MSG, 128), BF), vm((NC, MSG, 128), BF),
        vm((2, CH, OWN, 128), BF), vm((CH, OWN, 128), BF),
        vm((OM, CH * 2 * OWN), BF), vm((CH * 2 * OWN, OM), BF), vm((OB, NZ * OM), BF), vm((NZ * OM, OB), BF),
        vm((OM, 128), BF), vm((NZ, OM, 128), BF), vm((NX, NY, OB, 128), BF), vm((NX, NY, OB, 128), BF),
        vm((NY, OB, 128), BF), vm((2, NY, OB, 128), BF), vm((NY, OB, 128), BF), vm((NY, OB, 128), BF),
        vm((NZ, OM, 128), BF), vm((NZ, OM, 128), BF),
        dma((9,)), dma, dma, dma, dma, dma((NZ, NP)), dma((NZ, NP)), dma, dma,
        dma((NC,)), dma((NC,)), dma((8, H)), dma((8, H)), dma((OV + NX, H)), dma((OV + NX, H)),
        dma((8, H)), dma((8, H)), dma((NC,)), dma((NC,)), dma, dma,
        dma((NZ,)), dma((NZ,)), dma((NY,)), dma((NY,)), dma((NX, NY)), dma((NX, NY)), dma((NX,)), dma((NX,)),
        dma((NY,)), dma((NY,)), dma((NZ,)), dma((NZ,)),
    ]
    made = pl.pallas_call(
        kernel,
        out_shape=(jax.ShapeDtypeStruct((OWN, D), BF), jax.ShapeDtypeStruct((OWN, D), BF)),
        in_specs=[pl.BlockSpec(memory_space=pl.ANY)] * 9,
        out_specs=(pl.BlockSpec(memory_space=vm), pl.BlockSpec(memory_space=vm)),
        scratch_shapes=scratch,
        compiler_params=pltpu.CompilerParams(
            collective_id=0, has_side_effects=True, vmem_limit_bytes=58 * 1024 * 1024
        ),
        cost_estimate=pl.CostEstimate(flops=4_000_000_000, bytes_accessed=8_000_000, transcendentals=300_000),
    )(q, kv.reshape(TOK, 128), wo.T, res, gain, ids.T, weights.T, w_in, w_out)
    return pl.pallas_call(
        deliver,
        out_shape=(jax.ShapeDtypeStruct((OWN, D), BF), jax.ShapeDtypeStruct((OWN, D), BF)),
        in_specs=[pl.BlockSpec(memory_space=vm)] * 2,
        out_specs=(pl.BlockSpec(memory_space=vm), pl.BlockSpec(memory_space=vm)),
    )(*made)


def solution(mesh):
    placed = (
        P("seq", "head"), P("seq", "head", None), P("head", None), P(("seq", "head"), None), P(),
        P("seq", None), P("seq", None), P("seq", None, "head"), P("seq", "head", None),
    )
    return jax.shard_map(
        per_device, mesh=mesh, in_specs=placed,
        out_specs=(P(("seq", "head"), None), P(("seq", "head"), None)), check_vma=False,
    )
```
